32 devices in a mesh: row: 8 (over y, x, core), col: 4 (over z).
Axes of the slice: x: 2, y: 2, z: 4, core: 2. Of those that a mesh axis runs over, the one named last changes fastest.
Arguments:
- amplitudes: bfloat16 [16384, 2048], P('row', 'col'), may hold values from -6 to 6
- couplings: bfloat16 [2048, 16384], P('row', 'col'), may hold values from -0.125 to 0.125
- ladder: bfloat16 [1024, 1024], replicated, may hold values from -0.1875 to 0.1875
Outputs:
- update: bfloat16 [512, 512, 1024], P('row', 'col')
The draws below stay inside these ranges and needn't reach their ends.
All inputs are finite; a program needn't handle non-finite values.
Results may differ from the reference program's by a relative error of at most 0.0049.
Values may be sent and summed in bfloat16 or wider, within the bound.
No kernel may reach another device: no remote copies, remote signals or barrier semaphores. Data moves between devices by JAX's collectives and lax.ppermute only.
A program may use at most 128 MiB of HBM per device.

```python
import jax
import jax.numpy as jnp

NI = 32
V = 512
K = 2048


def block_levels(own_key, dims, pieces, low, top_value):
    loudness, own = 1.0, jax.random.fold_in(own_key, 6)
    for position, parts in pieces:
        draws = jnp.exp(jax.random.uniform(jax.random.fold_in(own, position), (parts,), jnp.float32, low / len(pieces), top_value / len(pieces)))
        loudness = loudness * jnp.repeat(draws, dims[position] // parts).reshape([-1 if axis == position else 1 for axis in range(len(dims))])
    return loudness


def normal_values(stream_key, dims, width, bound, split=(), dtype=jnp.bfloat16):
    entries = width * jax.random.normal(stream_key, dims, jnp.float32)
    if split:
        entries = entries * block_levels(stream_key, dims, split, -0.22, 0.18)
    return jnp.clip(entries, -bound, bound).astype(dtype)


def setup_inputs(seed: int = 0) -> dict:
    key_list = jax.random.split(jax.random.key(seed), 4)
    amplitudes = normal_values(key_list[0], (NI * V, K), 1.0, 6.0, ((0, 8), (1, 4)))
    couplings = normal_values(key_list[1], (K, NI * V), K ** -0.5, 0.125, ((0, 8), (1, 4)))
    ladder = normal_values(key_list[2], (NI * NI, NI * NI), (NI * NI) ** -0.5, 0.1875)
    return dict(amplitudes=amplitudes, couplings=couplings, ladder=ladder)


def reference(amplitudes, couplings, ladder):
    cycle = jnp.dot(amplitudes, couplings, preferred_element_type=jnp.float32).astype(jnp.bfloat16)
    pairs = jnp.transpose(cycle.reshape(NI, V, NI, V), (1, 3, 0, 2)).reshape(V * V, NI * NI)
    mixed = jax.lax.dot_general(pairs, ladder, (((1,), (1,)), ((), ())), preferred_element_type=jnp.float32)
    total = mixed + pairs.astype(jnp.float32)
    return total.astype(jnp.bfloat16).reshape(V, V, NI * NI)
```

```python
import functools

import jax
import jax.numpy as jnp
from jax import lax
from jax.experimental import pallas as pl
from jax.experimental.pallas import tpu as pltpu
from jax.sharding import PartitionSpec as P

V = 512
GROUP = 16
STEP_J = 8
STEP_A = 4


def chunk_kernel(own, *refs, parts, occupied, b_local, steps_w):
    t_refs = refs[:parts]
    w_ref, ladder_ref, out_ref, t_all, pairs, lhs = (
        refs[parts], refs[parts + 1], *refs[-4:])
    step = pl.program_id(0)
    depth = t_refs[0].shape[1]
    count = occupied * occupied

    @pl.when(step == 0)
    def _():
        for s in range(parts):
            block = lax.rem(own[0] - s + parts, parts)
            t_all[:, pl.ds(pl.multiple_of(block * depth, depth), depth)] = t_refs[s][...]

    @pl.when(step < steps_w)
    def _():
        per_part = occupied // parts
        first = step * STEP_J
        shift = first // per_part
        j0 = lax.rem(own[0] - shift + parts, parts) * per_part + lax.rem(first, per_part)
        wide = 256 // b_local

        @pl.loop(0, STEP_J // wide)
        def _(tile):
            cols = pl.ds(pl.multiple_of(tile * 256, 256), 256)
            acc = jnp.dot(t_all[...], w_ref[:, cols], preferred_element_type=jnp.float32)
            for k in range(wide):
                j = j0 + tile * wide + k
                for i in range(occupied):
                    for h in range(GROUP // 8):
                        row = i * GROUP + h * 8
                        pairs[pl.ds(h * 8 * count + i * occupied + j, 8, stride=count), :] = (
                            acc[row:row + 8, k * b_local:(k + 1) * b_local])

    @pl.when(step >= steps_w)
    def _():
        a0 = (step - steps_w) * STEP_A
        for k in range(STEP_A):
            rows = pl.ds(pl.multiple_of((a0 + k) * count, count), count)
            lhs[k * b_local:(k + 1) * b_local, :] = pairs[rows, :].astype(jnp.bfloat16).T
        for m in range(count // 256):
            cols = slice(m * 256, (m + 1) * 256)
            mixed = jnp.dot(lhs[...], ladder_ref[:, cols], preferred_element_type=jnp.float32)
            total = (mixed + lhs[:, cols].astype(jnp.float32)).astype(jnp.bfloat16)
            out_ref[:, :, cols] = total.reshape(STEP_A, b_local, 256)


def chunk_update(own, pieces, panel_w, ladder_t, out, q, a_local, b_local, occupied):
    parts = len(pieces)
    rows, depth = pieces[0].shape
    count = occupied * occupied
    steps_w = occupied // STEP_J
    steps_a = GROUP // STEP_A
    k_all = panel_w.shape[0]
    whole = lambda s, own: (0, 0)
    in_specs = [pl.BlockSpec((rows, depth), whole, pipeline_mode=pl.Buffered(1))] * parts
    in_specs.append(pl.BlockSpec((k_all, STEP_J * b_local), lambda s, own: (0, jnp.minimum(s, steps_w - 1))))
    in_specs.append(pl.BlockSpec((count, count), whole, pipeline_mode=pl.Buffered(1)))
    args = [own, *pieces, panel_w, ladder_t]
    aliases = {}
    if out is not None:
        in_specs.append(pl.BlockSpec(memory_space=pl.ANY))
        aliases = {len(args): 0}
        args.append(out)
    flops = 2 * rows * k_all * occupied * b_local + 2 * GROUP * b_local * count * count
    return pl.pallas_call(
        functools.partial(chunk_kernel, parts=parts, occupied=occupied, b_local=b_local, steps_w=steps_w),
        out_shape=jax.ShapeDtypeStruct((a_local, b_local, count), jnp.bfloat16),
        grid_spec=pltpu.PrefetchScalarGridSpec(
            num_scalar_prefetch=1,
            grid=(steps_w + steps_a,),
            in_specs=in_specs,
            out_specs=pl.BlockSpec(
                (STEP_A, b_local, count),
                lambda s, own: (q * steps_a + jnp.maximum(s - steps_w, 0), 0, 0)),
            scratch_shapes=[
                pltpu.VMEM((rows, k_all), jnp.bfloat16),
                pltpu.VMEM((GROUP * count, b_local), jnp.float32),
                pltpu.VMEM((STEP_A * b_local, count), jnp.bfloat16),
            ],
        ),
        input_output_aliases=aliases,
        compiler_params=pltpu.CompilerParams(vmem_limit_bytes=48 * 1024 * 1024),
        cost_estimate=pl.CostEstimate(
            flops=flops, bytes_accessed=2 * (panel_w.size + count * count + rows * k_all + GROUP * b_local * count),
            transcendentals=0),
    )(*args)


def plain_update(own, pieces, panel_w, ladder, b_local, occupied):
    parts = len(pieces)
    order = lax.rem(own - jnp.arange(parts) + parts, parts)
    panel_t = jnp.stack(pieces, 1)[:, jnp.argsort(order)].reshape(pieces[0].shape[0], -1)
    cycle = jnp.dot(panel_t, panel_w, preferred_element_type=jnp.float32).astype(jnp.bfloat16)
    cycle = cycle.reshape(occupied, -1, parts, occupied // parts, b_local)[:, :, jnp.argsort(order)]
    cycle = cycle.reshape(occupied, -1, occupied, b_local)
    a_count = cycle.shape[1]
    pairs = jnp.transpose(cycle, (1, 3, 0, 2)).reshape(a_count * b_local, occupied * occupied)
    mixed = lax.dot_general(pairs, ladder, (((1,), (1,)), ((), ())), preferred_element_type=jnp.float32)
    total = (mixed + pairs.astype(jnp.float32)).astype(jnp.bfloat16)
    return total.reshape(a_count, b_local, occupied * occupied)


def local(rows, cols, amplitudes, couplings, ladder):
    depth = amplitudes.shape[1]
    i_local = amplitudes.shape[0] // V
    j_local = couplings.shape[1] // V
    occupied = i_local * rows
    a_local, b_local = V // rows, V // cols
    own = lax.axis_index("col")

    split = couplings.reshape(couplings.shape[0], j_local, cols, b_local)
    arrived = []
    for s in range(cols):
        to = lax.rem(own + s, cols)
        part = lax.dynamic_slice_in_dim(split, to, 1, axis=2)
        part = part.reshape(couplings.shape[0], j_local * b_local)
        if s:
            part = lax.ppermute(part, "col", [(c, (c + s) % cols) for c in range(cols)])
        arrived.append(part)
    panel_w = lax.all_gather(jnp.concatenate(arrived, axis=1), "row", axis=0, tiled=True)

    chunks = a_local // GROUP
    blocks = amplitudes.reshape(i_local, rows, chunks, GROUP, depth).transpose(1, 2, 0, 3, 4)
    blocks = lax.all_to_all(blocks, "row", split_axis=0, concat_axis=0, tiled=True)
    ring = [(c, (c + 1) % cols) for c in range(cols)]
    pieces = []
    for q in range(chunks):
        held = blocks[:, q].reshape(occupied * GROUP, depth)
        got = [held]
        for _ in range(cols - 1):
            held = lax.ppermute(held, "col", ring)
            got.append(held)
        pieces.append(got)

    if b_local % 128 or 256 % b_local or depth % 128 or (occupied // cols) % STEP_J:
        return jnp.concatenate(
            [plain_update(own, got, panel_w, ladder, b_local, occupied) for got in pieces], axis=0)
    ladder_t = ladder.T
    out = None
    for q in range(chunks):
        out = chunk_update(own.reshape(1), pieces[q], panel_w, ladder_t, out, q, a_local, b_local, occupied)
    return out


def solution(mesh):
    in_specs = (P("row", "col"), P("row", "col"), P())
    out_specs = P("row", "col", None)
    body = functools.partial(local, mesh.shape["row"], mesh.shape["col"])
    return jax.shard_map(body, mesh=mesh, in_specs=in_specs, out_specs=out_specs, check_vma=False)
```

```python
import functools

import jax
import jax.numpy as jnp
from jax import lax
from jax.experimental import pallas as pl
from jax.experimental.pallas import tpu as pltpu
from jax.sharding import PartitionSpec as P

V = 512
GROUP = 16
STEP_J = 8
STEP_A = 4
PAD = 8


def partner(own, k, count):
    if count & (count - 1) == 0:
        return own ^ k, own ^ k
    return (own + k) % count, (own - k + count) % count


def split_kernel(own, w_ref, *out_refs, j_local, b_local):
    cols = len(out_refs)
    for s in range(cols):
        to = lax.rem(own[0] + s, cols)
        for j in range(j_local):
            start = pl.multiple_of((j * cols + to) * b_local, b_local)
            out_refs[s][:, j * b_local:(j + 1) * b_local] = w_ref[:, pl.ds(start, b_local)]


def split_columns(own, couplings, cols, j_local, b_local):
    depth = couplings.shape[0]
    if b_local % 128:
        split = couplings.reshape(depth, j_local, cols, b_local)
        return [
            lax.dynamic_index_in_dim(split, lax.rem(own + s, cols), 2, keepdims=False).reshape(depth, -1)
            for s in range(cols)
        ]
    return pl.pallas_call(
        functools.partial(split_kernel, j_local=j_local, b_local=b_local),
        out_shape=[jax.ShapeDtypeStruct((depth, j_local * b_local), couplings.dtype)] * cols,
        in_specs=[pl.BlockSpec(memory_space=pltpu.SMEM), pl.BlockSpec(memory_space=pltpu.VMEM)],
        out_specs=[pl.BlockSpec(memory_space=pltpu.VMEM)] * cols,
        compiler_params=pltpu.CompilerParams(vmem_limit_bytes=24 * 1024 * 1024),
        cost_estimate=pl.CostEstimate(flops=0, bytes_accessed=4 * couplings.size, transcendentals=0),
    )(own.reshape(1), couplings)


def chunk_kernel(own, *refs, parts, occupied, b_local, steps_w):
    t_refs = refs[:parts]
    w_ref, ladder_ref, out_ref, t_all, pairs = refs[parts], refs[parts + 1], *refs[-3:]
    step = pl.program_id(0)
    depth = t_refs[0].shape[1]
    count = occupied * occupied
    pitch = count + PAD
    sources = own.shape[0] - 1
    i_local = occupied // sources

    @pl.when(step == 0)
    def _():
        for s in range(parts):
            block = lax.rem(own[0] - s + parts, parts)
            t_all[:, pl.ds(pl.multiple_of(block * depth, depth), depth)] = t_refs[s][...]

    @pl.when(step < steps_w)
    def _():
        per_part = occupied // parts
        first = step * STEP_J
        shift = first // per_part
        j0 = lax.rem(own[0] - shift + parts, parts) * per_part + lax.rem(first, per_part)
        wide = 256 // b_local
        for tile in range(STEP_J // wide):
            acc = jnp.dot(
                t_all[...], w_ref[:, tile * 256:(tile + 1) * 256], preferred_element_type=jnp.float32)
            for source in range(sources):
                start = own[1 + source] * (i_local * occupied) + j0
                for i in range(i_local):
                    for k in range(wide):
                        n = start + (i * occupied + tile * wide + k)
                        for h in range(GROUP // 8):
                            row = (source * i_local + i) * GROUP + h * 8
                            pairs[pl.ds(h * 8 * pitch + n, 8, stride=pitch), :] = (
                                acc[row:row + 8, k * b_local:(k + 1) * b_local])

    @pl.when(step >= steps_w)
    def _():
        a0 = (step - steps_w) * STEP_A
        wide = 256 // b_local
        for g in range(STEP_A // wide):
            blocks = []
            for k in range(wide):
                row = pl.multiple_of((a0 + g * wide + k) * pitch, 8)
                blocks.append(pairs[pl.ds(row, count), :].astype(jnp.bfloat16))
            both = jnp.concatenate(blocks, axis=1)
            for m in range(count // 256):
                rows = slice(m * 256, (m + 1) * 256)
                mixed = jnp.dot(ladder_ref[rows, :], both, preferred_element_type=jnp.float32)
                total = (mixed + both[rows, :].astype(jnp.float32)).astype(jnp.bfloat16)
                out_ref[g * wide:(g + 1) * wide, :, rows] = total.T.reshape(wide, b_local, 256)


def chunk_update(own, pieces, panel_w, ladder, out, q, a_local, b_local, occupied):
    parts = len(pieces)
    rows, depth = pieces[0].shape
    count = occupied * occupied
    steps_w = occupied // STEP_J
    steps_a = GROUP // STEP_A
    k_all = panel_w.shape[0]
    whole = lambda s, own: (0, 0)
    in_specs = [pl.BlockSpec((rows, depth), whole, pipeline_mode=pl.Buffered(1))] * parts
    in_specs.append(pl.BlockSpec((k_all, STEP_J * b_local), lambda s, own: (0, jnp.minimum(s, steps_w - 1))))
    in_specs.append(pl.BlockSpec((count, count), whole, pipeline_mode=pl.Buffered(1)))
    args = [own, *pieces, panel_w, ladder]
    aliases = {}
    if out is not None:
        in_specs.append(pl.BlockSpec(memory_space=pl.ANY))
        aliases = {len(args): 0}
        args.append(out)
    flops = 2 * rows * k_all * occupied * b_local + 2 * GROUP * b_local * count * count
    return pl.pallas_call(
        functools.partial(chunk_kernel, parts=parts, occupied=occupied, b_local=b_local, steps_w=steps_w),
        out_shape=jax.ShapeDtypeStruct((a_local, b_local, count), jnp.bfloat16),
        grid_spec=pltpu.PrefetchScalarGridSpec(
            num_scalar_prefetch=1,
            grid=(steps_w + steps_a,),
            in_specs=in_specs,
            out_specs=pl.BlockSpec(
                (STEP_A, b_local, count),
                lambda s, own: (q * steps_a + jnp.maximum(s - steps_w, 0), 0, 0)),
            scratch_shapes=[
                pltpu.VMEM((rows, k_all), jnp.bfloat16),
                pltpu.VMEM((GROUP * (count + PAD), b_local), jnp.float32),
            ],
        ),
        input_output_aliases=aliases,
        compiler_params=pltpu.CompilerParams(vmem_limit_bytes=48 * 1024 * 1024),
        cost_estimate=pl.CostEstimate(
            flops=flops, bytes_accessed=2 * (panel_w.size + count * count + rows * k_all + GROUP * b_local * count),
            transcendentals=0),
    )(*args)


def plain_update(own, sources, pieces, panel_w, ladder, b_local, occupied):
    parts = len(pieces)
    back = jnp.argsort(lax.rem(own - jnp.arange(parts) + parts, parts))
    rows, depth = pieces[0].shape
    panel_t = jnp.stack(pieces, 0)[back].reshape(parts, sources.shape[0], -1, depth)
    panel_t = panel_t[:, jnp.argsort(sources)].reshape(parts, rows, depth)
    panel_t = jnp.transpose(panel_t, (1, 0, 2)).reshape(rows, -1)
    cycle = jnp.dot(panel_t, panel_w, preferred_element_type=jnp.float32).astype(jnp.bfloat16)
    cycle = cycle.reshape(occupied, -1, parts, occupied // parts, b_local)[:, :, back]
    cycle = cycle.reshape(occupied, -1, occupied, b_local)
    a_count = cycle.shape[1]
    pairs = jnp.transpose(cycle, (1, 3, 0, 2)).reshape(a_count * b_local, occupied * occupied)
    mixed = lax.dot_general(pairs, ladder, (((1,), (1,)), ((), ())), preferred_element_type=jnp.float32)
    total = (mixed + pairs.astype(jnp.float32)).astype(jnp.bfloat16)
    return total.reshape(a_count, b_local, occupied * occupied)


def local(rows, cols, amplitudes, couplings, ladder):
    depth = amplitudes.shape[1]
    i_local = amplitudes.shape[0] // V
    j_local = couplings.shape[1] // V
    occupied = i_local * rows
    a_local, b_local = V // rows, V // cols
    own, own_row = lax.axis_index("col"), lax.axis_index("row")

    arrived = list(split_columns(own, couplings, cols, j_local, b_local))
    for s in range(1, cols):
        arrived[s] = lax.ppermute(arrived[s], "col", [(c, (c + s) % cols) for c in range(cols)])

    by_row = amplitudes.reshape(i_local, V, depth)
    blocks, sources = [], []
    for k in range(rows):
        to, source = partner(own_row, k, rows)
        blocks.append(lax.dynamic_slice_in_dim(by_row, to * a_local, a_local, axis=1))
        sources.append(source)
    sources = jnp.stack(sources)
    half = rows // 2
    order = [k for pair in zip(range(half, rows), [*range(2, half), 1]) for k in pair]
    order += [k for k in range(1, rows) if k not in order]
    for n, k in enumerate(order):
        if n >= 2:
            blocks[k], blocks[order[n - 2]] = lax.optimization_barrier((blocks[k], blocks[order[n - 2]]))
        blocks[k] = lax.ppermute(blocks[k], "row", [(r, partner(r, k, rows)[0]) for r in range(rows)])

    arrived, blocks = lax.optimization_barrier((arrived, blocks))
    panel_w = lax.all_gather(jnp.concatenate(arrived, axis=1), "row", axis=0, tiled=True)

    ring = [(c, (c + 1) % cols) for c in range(cols)]
    pieces = []
    for q in range(a_local // GROUP):
        held = jnp.concatenate([block[:, q * GROUP:(q + 1) * GROUP] for block in blocks], axis=0)
        held = held.reshape(occupied * GROUP, depth)
        got = [held]
        for _ in range(cols - 1):
            held = lax.ppermute(held, "col", ring)
            got.append(held)
        pieces.append(got)

    if b_local % 128 or 256 % b_local or depth % 128 or (occupied // cols) % STEP_J:
        return jnp.concatenate(
            [plain_update(own, sources, got, panel_w, ladder, b_local, occupied) for got in pieces], axis=0)
    place = jnp.concatenate([own.reshape(1), sources])
    out = None
    for q in range(a_local // GROUP):
        out = chunk_update(place, pieces[q], panel_w, ladder, out, q, a_local, b_local, occupied)
    return out


def solution(mesh):
    in_specs = (P("row", "col"), P("row", "col"), P())
    out_specs = P("row", "col", None)
    body = functools.partial(local, mesh.shape["row"], mesh.shape["col"])
    return jax.shard_map(body, mesh=mesh, in_specs=in_specs, out_specs=out_specs, check_vma=False)
```

```python
import functools

import jax
import jax.numpy as jnp
from jax import lax
from jax.experimental import pallas as pl
from jax.experimental.pallas import tpu as pltpu
from jax.sharding import PartitionSpec as P

V = 512
GROUP = 16
STEP_A = 4
PAD = 8
WIDE = 512
ANY = pl.BlockSpec(memory_space=pl.ANY)


def split_kernel(own, w_ref, *out_refs, j_local, b_local):
    cols = len(out_refs)
    for s in range(cols):
        to = lax.rem(own[0] + s, cols)
        for j in range(j_local):
            start = pl.multiple_of((j * cols + to) * b_local, b_local)
            out_refs[s][:, j * b_local:(j + 1) * b_local] = w_ref[:, pl.ds(start, b_local)]


def split_columns(own, couplings, cols, j_local, b_local):
    depth = couplings.shape[0]
    if b_local % 128:
        split = couplings.reshape(depth, j_local, cols, b_local)
        return [
            lax.dynamic_index_in_dim(split, lax.rem(own + s, cols), 2, keepdims=False).reshape(depth, -1)
            for s in range(cols)
        ]
    return pl.pallas_call(
        functools.partial(split_kernel, j_local=j_local, b_local=b_local),
        out_shape=[jax.ShapeDtypeStruct((depth, j_local * b_local), couplings.dtype)] * cols,
        in_specs=[pl.BlockSpec(memory_space=pltpu.SMEM), pl.BlockSpec(memory_space=pltpu.VMEM)],
        out_specs=[pl.BlockSpec(memory_space=pltpu.VMEM)] * cols,
        compiler_params=pltpu.CompilerParams(vmem_limit_bytes=24 * 1024 * 1024),
        cost_estimate=pl.CostEstimate(flops=0, bytes_accessed=4 * couplings.size, transcendentals=0),
    )(own.reshape(1), couplings)


def chunk_kernel(own, *refs, parts, occupied, b_local, q):
    t_own, t_right, t_left = refs[0], refs[1:parts], refs[parts:2 * parts - 1]
    w_refs = refs[2 * parts - 1:3 * parts - 1]
    ladder_hbm = refs[3 * parts - 1]
    out_ref, t_all, w_buf, ladder, pairs, out_buf, t_sem, w_sem, l_sem, out_sem = refs[-10:]
    depth = t_own.shape[1]
    count = occupied * occupied
    pitch = count + PAD
    per_part = occupied // parts
    wide = WIDE // b_local

    def t_copy(src, block, s):
        cols = pl.ds(pl.multiple_of(block * depth, depth), depth)
        return pltpu.make_async_copy(src, t_all.at[:, cols], t_sem.at[s])

    def w_copy(s, slot):
        return pltpu.make_async_copy(w_refs[s], w_buf.at[slot], w_sem.at[slot])

    blocks = [lax.rem(own[0] - s + parts, parts) for s in range(parts)]
    t_copy(t_own, blocks[0], 0).start()
    for s in range(1, parts):
        @pl.when(own[0] >= s)
        def _():
            t_copy(t_right[s - 1], blocks[s], s).start()

        @pl.when(own[0] < s)
        def _():
            t_copy(t_left[parts - s - 1], blocks[s], s).start()
    w_copy(0, 0).start()
    w_copy(1 % parts, 1).start()
    ladder_copy = pltpu.make_async_copy(ladder_hbm, ladder, l_sem)
    ladder_copy.start()
    for s in range(parts):
        t_copy(t_own, blocks[s], s).wait()

    @pl.loop(0, parts)
    def _(step):
        slot = lax.rem(step, 2)
        w_copy(0, slot).wait()
        j0 = lax.rem(own[0] - step + parts, parts) * per_part
        for tile in range(per_part // wide):
            acc = jnp.dot(
                t_all[...], w_buf[slot, :, tile * WIDE:(tile + 1) * WIDE], preferred_element_type=jnp.float32)
            for i in range(occupied):
                for k in range(wide):
                    n = j0 + (i * occupied + tile * wide + k)
                    for h in range(GROUP // 8):
                        row = i * GROUP + h * 8
                        pairs[pl.ds(h * 8 * pitch + n, 8, stride=pitch), :] = (
                            acc[row:row + 8, k * b_local:(k + 1) * b_local])
        for s in range(2, parts):
            @pl.when(step + 2 == s)
            def _():
                w_copy(s, slot).start()

    ladder_copy.wait()
    steps = GROUP // STEP_A

    def out_copy(step, slot):
        rows = pl.ds(q * GROUP + step * STEP_A, STEP_A)
        return pltpu.make_async_copy(out_buf.at[slot], out_ref.at[rows], out_sem.at[slot])

    @pl.loop(0, steps)
    def _(step):
        slot = lax.rem(step, 2)

        @pl.when(step >= 2)
        def _():
            out_copy(step - 2, slot).wait()

        for g in range(STEP_A // wide):
            blocks = []
            for k in range(wide):
                row = pl.multiple_of((step * STEP_A + g * wide + k) * pitch, 8)
                blocks.append(pairs[pl.ds(row, count), :].astype(jnp.bfloat16))
            both = jnp.concatenate(blocks, axis=1)
            for m in range(count // 256):
                rows = slice(m * 256, (m + 1) * 256)
                mixed = jnp.dot(ladder[rows, :], both, preferred_element_type=jnp.float32)
                total = (mixed + both[rows, :].astype(jnp.float32)).astype(jnp.bfloat16)
                out_buf[slot, g * wide:(g + 1) * wide, :, rows] = total.T.reshape(wide, b_local, 256)
        out_copy(step, slot).start()

    for step in range(max(steps - 2, 0), steps):
        out_copy(step, step % 2).wait()


def chunk_update(own, pieces, panel_w, ladder, out, after, q, a_local, b_local, occupied):
    parts = len(panel_w)
    rows, depth = pieces[0].shape
    count = occupied * occupied
    k_all, width = panel_w[0].shape
    args = [*pieces, *panel_w, ladder, *after]
    aliases = {}
    if out is not None:
        aliases = {len(args) + 1: 0}
        args.append(out)
    flops = 2 * rows * k_all * occupied * b_local + 2 * GROUP * b_local * count * count
    size = parts * k_all * width + count * count + rows * k_all + GROUP * b_local * count
    return pl.pallas_call(
        functools.partial(chunk_kernel, parts=parts, occupied=occupied, b_local=b_local, q=q),
        out_shape=jax.ShapeDtypeStruct((a_local, b_local, count), jnp.bfloat16),
        in_specs=[pl.BlockSpec(memory_space=pltpu.SMEM)] + [ANY] * len(args),
        out_specs=ANY,
        scratch_shapes=[
            pltpu.VMEM((rows, k_all), jnp.bfloat16),
            pltpu.VMEM((2, k_all, width), jnp.bfloat16),
            pltpu.VMEM((count, count), jnp.bfloat16),
            pltpu.VMEM((GROUP * (count + PAD), b_local), jnp.float32),
            pltpu.VMEM((2, STEP_A, b_local, count), jnp.bfloat16),
            pltpu.SemaphoreType.DMA((parts,)),
            pltpu.SemaphoreType.DMA((2,)),
            pltpu.SemaphoreType.DMA,
            pltpu.SemaphoreType.DMA((2,)),
        ],
        input_output_aliases=aliases,
        compiler_params=pltpu.CompilerParams(vmem_limit_bytes=60 * 1024 * 1024),
        cost_estimate=pl.CostEstimate(flops=flops, bytes_accessed=2 * size, transcendentals=0),
    )(own.reshape(1), *args)


def plain_update(own, pieces, panel_w, ladder, b_local, occupied):
    parts = len(panel_w)
    back = jnp.argsort(lax.rem(own - jnp.arange(parts) + parts, parts))
    rows, depth = pieces[0].shape
    right, left = pieces[1:parts], pieces[parts:]
    by_shift = [pieces[0]] + [jnp.where(own >= s, right[s - 1], left[parts - s - 1]) for s in range(1, parts)]
    panel_t = jnp.transpose(jnp.stack(by_shift, 0)[back], (1, 0, 2)).reshape(rows, -1)
    cycle = jnp.dot(panel_t, jnp.concatenate(panel_w, axis=1), preferred_element_type=jnp.float32)
    cycle = cycle.astype(jnp.bfloat16).reshape(occupied, -1, parts, occupied // parts, b_local)[:, :, back]
    cycle = cycle.reshape(occupied, -1, occupied, b_local)
    a_count = cycle.shape[1]
    pairs = jnp.transpose(cycle, (1, 3, 0, 2)).reshape(a_count * b_local, occupied * occupied)
    mixed = lax.dot_general(pairs, ladder, (((1,), (1,)), ((), ())), preferred_element_type=jnp.float32)
    total = (mixed + pairs.astype(jnp.float32)).astype(jnp.bfloat16)
    return total.reshape(a_count, b_local, occupied * occupied)


def local(rows, cols, amplitudes, couplings, ladder):
    depth = amplitudes.shape[1]
    i_local = amplitudes.shape[0] // V
    j_local = couplings.shape[1] // V
    occupied = i_local * rows
    a_local, b_local = V // rows, V // cols
    own = lax.axis_index("col")

    arrived = list(split_columns(own, couplings, cols, j_local, b_local))
    arrived[0], amplitudes = lax.optimization_barrier((arrived[0], amplitudes))
    for s in range(1, cols):
        arrived[s] = lax.ppermute(arrived[s], "col", [(c, (c + s) % cols) for c in range(cols)])

    chunks = a_local // GROUP
    blocks = amplitudes.reshape(i_local, rows, chunks, GROUP, depth).transpose(1, 2, 0, 3, 4)
    blocks = lax.all_to_all(blocks, "row", split_axis=0, concat_axis=0, tiled=True)

    arrived[1:], blocks = lax.optimization_barrier((arrived[1:], blocks))
    panel_w = [lax.all_gather(part, "row", axis=0, tiled=True) for part in arrived]

    pieces = []
    for q in range(0, chunks, 2):
        both = [blocks[:, p].reshape(occupied * GROUP, depth) for p in range(q, min(q + 2, chunks))]
        if q:
            middle = (cols - 1) // 2
            for n, (right, left) in enumerate(pieces[-2:][:len(both)]):
                both[n], right[middle + 1], left[middle + 1] = lax.optimization_barrier(
                    (both[n], right[middle + 1], left[middle + 1]))
        pair = [([held], [held]) for held in both]
        for s in range(1, cols):
            for right, left in pair:
                right.append(lax.ppermute(right[-1], "col", [(c, c + 1) for c in range(s - 1, cols - 1)]))
                left.append(lax.ppermute(left[-1], "col", [(c + 1, c) for c in range(cols - s)]))
            if s == 1:
                started = [got[-1] for sides in pair for got in sides]
        pieces += pair
    pieces = [[right[0], *right[1:], *left[1:]] for right, left in pieces]

    per_part = occupied // cols
    if b_local % 128 or WIDE % b_local or depth % 128 or cols < 2 or per_part * b_local % WIDE:
        return jnp.concatenate(
            [plain_update(own, got, panel_w, ladder, b_local, occupied) for got in pieces], axis=0)
    out = None
    for q in range(chunks):
        after = () if q else started
        out = chunk_update(own, pieces[q], panel_w, ladder, out, after, q, a_local, b_local, occupied)
    return out


def solution(mesh):
    in_specs = (P("row", "col"), P("row", "col"), P())
    out_specs = P("row", "col", None)
    body = functools.partial(local, mesh.shape["row"], mesh.shape["col"])
    return jax.shard_map(body, mesh=mesh, in_specs=in_specs, out_specs=out_specs, check_vma=False)
```

```python
import functools

import jax
import jax.numpy as jnp
from jax import lax
from jax.experimental import pallas as pl
from jax.experimental.pallas import tpu as pltpu
from jax.sharding import PartitionSpec as P

V = 512
GROUP = 16
STEP_A = 4
ANY = pl.BlockSpec(memory_space=pl.ANY)


def split_kernel(own, w_ref, *out_refs, j_local, b_local):
    cols = len(out_refs)
    for s in range(cols):
        to = lax.rem(own[0] + s, cols)
        for j in range(j_local):
            start = pl.multiple_of((j * cols + to) * b_local, b_local)
            out_refs[s][:, j * b_local:(j + 1) * b_local] = w_ref[:, pl.ds(start, b_local)]


def split_columns(own, couplings, cols, j_local, b_local):
    depth = couplings.shape[0]
    if b_local % 128:
        split = couplings.reshape(depth, j_local, cols, b_local)
        return [
            lax.dynamic_index_in_dim(split, lax.rem(own + s, cols), 2, keepdims=False).reshape(depth, -1)
            for s in range(cols)
        ]
    return pl.pallas_call(
        functools.partial(split_kernel, j_local=j_local, b_local=b_local),
        out_shape=[jax.ShapeDtypeStruct((depth, j_local * b_local), couplings.dtype)] * cols,
        in_specs=[pl.BlockSpec(memory_space=pltpu.SMEM), pl.BlockSpec(memory_space=pltpu.VMEM)],
        out_specs=[pl.BlockSpec(memory_space=pltpu.VMEM)] * cols,
        compiler_params=pltpu.CompilerParams(vmem_limit_bytes=24 * 1024 * 1024),
        cost_estimate=pl.CostEstimate(flops=0, bytes_accessed=4 * couplings.size, transcendentals=0),
    )(own.reshape(1), couplings)


def swap_tiles(tiles):
    row = lax.broadcasted_iota(jnp.int32, tiles[0].shape, 0)
    for k in (4, 2, 1):
        keep = (row & k) == 0
        moved = list(tiles)
        for c in range(8):
            if c & k == 0:
                low, high = tiles[c], tiles[c | k]
                moved[c] = jnp.where(keep, low, pltpu.roll(high, k, 0))
                moved[c | k] = jnp.where(keep, pltpu.roll(low, 8 - k, 0), high)
        tiles = moved
    return tiles


def chunk_kernel(own, *refs, parts, occupied, b_local, q):
    t_own, t_right, t_left = refs[0], refs[1:parts], refs[parts:2 * parts - 1]
    w_own, w_rest, ladder_hbm = refs[2 * parts - 1:2 * parts + 2]
    (out_ref, t_all, w_all, ladder, cycle_a, cycle_b, pairs, mixed_a, mixed_b, out_buf,
     t_sem, w_sem, l_sem, out_sem) = refs[-14:]
    depth = t_own.shape[1]
    width = w_own.shape[1]
    count = occupied * occupied
    per_part = occupied // parts

    def t_copy(src, block, s):
        cols = pl.ds(pl.multiple_of(block * depth, depth), depth)
        return pltpu.make_async_copy(src, t_all.at[:, cols], t_sem.at[s])

    def w_copy(s):
        src = w_rest.at[:, (s - 1) * width:s * width] if s else w_own
        return pltpu.make_async_copy(src, w_all.at[s], w_sem.at[s])

    blocks = [lax.rem(own[0] - s + parts, parts) for s in range(parts)]
    t_copy(t_own, blocks[0], 0).start()
    for s in range(1, parts):
        @pl.when(own[0] >= s)
        def _():
            t_copy(t_right[s - 1], blocks[s], s).start()

        @pl.when(own[0] < s)
        def _():
            t_copy(t_left[parts - s - 1], blocks[s], s).start()
    for s in range(parts):
        w_copy(s).start()
    ladder_copy = pltpu.make_async_copy(ladder_hbm, ladder, l_sem)
    ladder_copy.start()
    for s in range(parts):
        t_copy(t_own, blocks[s], s).wait()

    cycles = (cycle_a, cycle_b)

    def regroup(s):
        src = cycles[s % 2]
        j0 = blocks[s] * per_part
        for j in range(0, per_part, 8):
            for i in range(occupied):
                for h in range(0, GROUP, 8):
                    rows = slice(i * GROUP + h, i * GROUP + h + 8)
                    tiles = [src[rows, (j + k) * b_local:(j + k + 1) * b_local] for k in range(8)]
                    for a, tile in enumerate(swap_tiles(tiles)):
                        row = pl.multiple_of((h + a) * count + i * occupied + j + j0, 8)
                        pairs[pl.ds(row, 8), :] = tile

    for s in range(parts):
        w_copy(s).wait()
        cycles[s % 2][...] = jnp.dot(t_all[...], w_all[s], preferred_element_type=jnp.float32)
        if s:
            regroup(s - 1)
    regroup(parts - 1)

    ladder_copy.wait()
    steps = GROUP // STEP_A
    mixes = (mixed_a, mixed_b)

    def block(step, k):
        a = step * STEP_A + k
        return pairs[a * count:(a + 1) * count, :].astype(jnp.bfloat16)

    def out_copy(step):
        rows = pl.ds(q * GROUP + step * STEP_A, STEP_A)
        return pltpu.make_async_copy(out_buf.at[step], out_ref.at[rows], out_sem.at[step])

    def finish(step):
        src = mixes[step % 2]
        for k in range(STEP_A):
            total = src[:, k * b_local:(k + 1) * b_local] + block(step, k).astype(jnp.float32)
            out_buf[step, k] = total.astype(jnp.bfloat16).T
        out_copy(step).start()

    for step in range(steps):
        both = jnp.concatenate([block(step, k) for k in range(STEP_A)], axis=1)
        mixes[step % 2][...] = jnp.dot(ladder[...], both, preferred_element_type=jnp.float32)
        if step:
            finish(step - 1)
    finish(steps - 1)
    for step in range(steps):
        out_copy(step).wait()


def chunk_update(own, pieces, panel_w, ladder, out, after, q, a_local, b_local, occupied):
    rows, depth = pieces[0].shape
    count = occupied * occupied
    k_all, width = panel_w[0].shape
    parts = 1 + panel_w[1].shape[1] // width
    args = [*pieces, *panel_w, ladder, *after]
    aliases = {}
    if out is not None:
        aliases = {len(args) + 1: 0}
        args.append(out)
    flops = 2 * rows * k_all * occupied * b_local + 2 * GROUP * b_local * count * count
    size = parts * k_all * width + count * count + rows * k_all + GROUP * b_local * count
    return pl.pallas_call(
        functools.partial(chunk_kernel, parts=parts, occupied=occupied, b_local=b_local, q=q),
        out_shape=jax.ShapeDtypeStruct((a_local, b_local, count), jnp.bfloat16),
        in_specs=[pl.BlockSpec(memory_space=pltpu.SMEM)] + [ANY] * len(args),
        out_specs=ANY,
        scratch_shapes=[
            pltpu.VMEM((rows, k_all), jnp.bfloat16),
            pltpu.VMEM((parts, k_all, width), jnp.bfloat16),
            pltpu.VMEM((count, count), jnp.bfloat16),
            pltpu.VMEM((rows, width), jnp.float32),
            pltpu.VMEM((rows, width), jnp.float32),
            pltpu.VMEM((GROUP * count, b_local), jnp.float32),
            pltpu.VMEM((count, STEP_A * b_local), jnp.float32),
            pltpu.VMEM((count, STEP_A * b_local), jnp.float32),
            pltpu.VMEM((GROUP // STEP_A, STEP_A, b_local, count), jnp.bfloat16),
            pltpu.SemaphoreType.DMA((parts,)),
            pltpu.SemaphoreType.DMA((parts,)),
            pltpu.SemaphoreType.DMA,
            pltpu.SemaphoreType.DMA((GROUP // STEP_A,)),
        ],
        input_output_aliases=aliases,
        compiler_params=pltpu.CompilerParams(vmem_limit_bytes=60 * 1024 * 1024),
        cost_estimate=pl.CostEstimate(flops=flops, bytes_accessed=2 * size, transcendentals=0),
    )(own.reshape(1), *args)


def plain_update(own, pieces, panel_w, ladder, b_local, occupied):
    parts = (len(pieces) + 1) // 2
    back = jnp.argsort(lax.rem(own - jnp.arange(parts) + parts, parts))
    rows, depth = pieces[0].shape
    right, left = pieces[1:parts], pieces[parts:]
    by_shift = [pieces[0]] + [jnp.where(own >= s, right[s - 1], left[parts - s - 1]) for s in range(1, parts)]
    panel_t = jnp.transpose(jnp.stack(by_shift, 0)[back], (1, 0, 2)).reshape(rows, -1)
    cycle = jnp.dot(panel_t, jnp.concatenate(panel_w, axis=1), preferred_element_type=jnp.float32)
    cycle = cycle.astype(jnp.bfloat16).reshape(occupied, -1, parts, occupied // parts, b_local)[:, :, back]
    cycle = cycle.reshape(occupied, -1, occupied, b_local)
    a_count = cycle.shape[1]
    pairs = jnp.transpose(cycle, (1, 3, 0, 2)).reshape(a_count * b_local, occupied * occupied)
    mixed = lax.dot_general(pairs, ladder, (((1,), (1,)), ((), ())), preferred_element_type=jnp.float32)
    total = (mixed + pairs.astype(jnp.float32)).astype(jnp.bfloat16)
    return total.reshape(a_count, b_local, occupied * occupied)


def local(rows, cols, amplitudes, couplings, ladder):
    depth = amplitudes.shape[1]
    i_local = amplitudes.shape[0] // V
    j_local = couplings.shape[1] // V
    occupied = i_local * rows
    a_local, b_local = V // rows, V // cols
    own = lax.axis_index("col")

    arrived = list(split_columns(own, couplings, cols, j_local, b_local))
    arrived[0], amplitudes = lax.optimization_barrier((arrived[0], amplitudes))
    for s in range(1, cols):
        arrived[s] = lax.ppermute(arrived[s], "col", [(c, (c + s) % cols) for c in range(cols)])

    chunks = a_local // GROUP
    blocks = amplitudes.reshape(i_local, rows, chunks, GROUP, depth).transpose(1, 2, 0, 3, 4)
    blocks = lax.all_to_all(blocks, "row", split_axis=0, concat_axis=0, tiled=True)

    rest, _ = lax.optimization_barrier((arrived[1:], blocks))
    panel_w = [
        lax.all_gather(part, "row", axis=0, tiled=True) for part in (arrived[0], jnp.concatenate(rest, axis=1))
    ]

    pieces = []
    for q in range(0, chunks, 2):
        both = [blocks[:, p].reshape(occupied * GROUP, depth) for p in range(q, min(q + 2, chunks))]
        if q:
            middle = (cols - 1) // 2
            for n, (right, left) in enumerate(pieces[-2:][:len(both)]):
                both[n], right[middle + 1], left[middle + 1] = lax.optimization_barrier(
                    (both[n], right[middle + 1], left[middle + 1]))
        pair = [([held], [held]) for held in both]
        for s in range(1, cols):
            for right, left in pair:
                right.append(lax.ppermute(right[-1], "col", [(c, c + 1) for c in range(s - 1, cols - 1)]))
                left.append(lax.ppermute(left[-1], "col", [(c + 1, c) for c in range(cols - s)]))
            if s == 1:
                started = [got[-1] for sides in pair for got in sides]
        pieces += pair
    pieces = [[right[0], *right[1:], *left[1:]] for right, left in pieces]

    per_part = occupied // cols
    if b_local % 128 or depth % 128 or cols < 2 or per_part % 8:
        return jnp.concatenate(
            [plain_update(own, got, panel_w, ladder, b_local, occupied) for got in pieces], axis=0)
    out = None
    for q in range(chunks):
        after = () if q else started
        out = chunk_update(own, pieces[q], panel_w, ladder, out, after, q, a_local, b_local, occupied)
    return out


def solution(mesh):
    in_specs = (P("row", "col"), P("row", "col"), P())
    out_specs = P("row", "col", None)
    body = functools.partial(local, mesh.shape["row"], mesh.shape["col"])
    return jax.shard_map(body, mesh=mesh, in_specs=in_specs, out_specs=out_specs, check_vma=False)
```

```python
import functools

import jax
import jax.numpy as jnp
from jax import lax
from jax.experimental import pallas as pl
from jax.experimental.pallas import tpu as pltpu
from jax.sharding import PartitionSpec as P

V = 512
GROUP = 16
STEP_A = 4
PAD = 8
WIDE = 512
ANY = pl.BlockSpec(memory_space=pl.ANY)


def split_kernel(own, w_ref, *out_refs, j_local, b_local):
    cols = len(out_refs)
    for s in range(cols):
        to = lax.rem(own[0] + s, cols)
        for j in range(j_local):
            start = pl.multiple_of((j * cols + to) * b_local, b_local)
            out_refs[s][:, j * b_local:(j + 1) * b_local] = w_ref[:, pl.ds(start, b_local)]


def split_columns(own, couplings, cols, j_local, b_local):
    depth = couplings.shape[0]
    if b_local % 128:
        split = couplings.reshape(depth, j_local, cols, b_local)
        return [
            lax.dynamic_index_in_dim(split, lax.rem(own + s, cols), 2, keepdims=False).reshape(depth, -1)
            for s in range(cols)
        ]
    return pl.pallas_call(
        functools.partial(split_kernel, j_local=j_local, b_local=b_local),
        out_shape=[jax.ShapeDtypeStruct((depth, j_local * b_local), couplings.dtype)] * cols,
        in_specs=[pl.BlockSpec(memory_space=pltpu.SMEM), pl.BlockSpec(memory_space=pltpu.VMEM)],
        out_specs=[pl.BlockSpec(memory_space=pltpu.VMEM)] * cols,
        compiler_params=pltpu.CompilerParams(vmem_limit_bytes=24 * 1024 * 1024),
        cost_estimate=pl.CostEstimate(flops=0, bytes_accessed=4 * couplings.size, transcendentals=0),
    )(own.reshape(1), couplings)


def chunk_kernel(own, *refs, parts, occupied, b_local, q):
    t_own, t_right, t_left = refs[0], refs[1:parts], refs[parts:2 * parts - 1]
    w_own, w_rest, ladder_hbm = refs[2 * parts - 1:2 * parts + 2]
    out_ref, t_all, w_buf, ladder, pairs, out_buf, t_sem, w_sem, l_sem, out_sem = refs[-10:]
    depth = t_own.shape[1]
    width = w_own.shape[1]
    count = occupied * occupied
    pitch = count + PAD
    per_part = occupied // parts
    wide = WIDE // b_local

    def t_copy(src, block, s):
        cols = pl.ds(pl.multiple_of(block * depth, depth), depth)
        return pltpu.make_async_copy(src, t_all.at[:, cols], t_sem.at[s])

    def w_copy(s, slot):
        src = w_rest.at[:, (s - 1) * width:s * width] if s else w_own
        return pltpu.make_async_copy(src, w_buf.at[slot], w_sem.at[slot])

    blocks = [lax.rem(own[0] - s + parts, parts) for s in range(parts)]
    t_copy(t_own, blocks[0], 0).start()
    for s in range(1, parts):
        @pl.when(own[0] >= s)
        def _():
            t_copy(t_right[s - 1], blocks[s], s).start()

        @pl.when(own[0] < s)
        def _():
            t_copy(t_left[parts - s - 1], blocks[s], s).start()
    w_copy(0, 0).start()
    ladder_copy = pltpu.make_async_copy(ladder_hbm, ladder, l_sem)
    for s in range(parts):
        t_copy(t_own, blocks[s], s).wait()

    @pl.loop(0, parts)
    def _(step):
        slot = lax.rem(step, 2)
        w_copy(0, slot).wait()
        for s in range(1, parts):
            @pl.when(step + 1 == s)
            def _():
                w_copy(s, s % 2).start()

        @pl.when(step == parts - 1)
        def _():
            ladder_copy.start()

        j0 = lax.rem(own[0] - step + parts, parts) * per_part
        for tile in range(per_part // wide):
            acc = jnp.dot(
                t_all[...], w_buf[slot, :, tile * WIDE:(tile + 1) * WIDE], preferred_element_type=jnp.float32)
            for i in range(occupied):
                for k in range(wide):
                    n = j0 + (i * occupied + tile * wide + k)
                    for h in range(GROUP // 8):
                        row = i * GROUP + h * 8
                        pairs[pl.ds(h * 8 * pitch + n, 8, stride=pitch), :] = (
                            acc[row:row + 8, k * b_local:(k + 1) * b_local])

    ladder_copy.wait()
    steps = GROUP // STEP_A

    def out_copy(step, slot):
        rows = pl.ds(q * GROUP + step * STEP_A, STEP_A)
        return pltpu.make_async_copy(out_buf.at[slot], out_ref.at[rows], out_sem.at[slot])

    @pl.loop(0, steps)
    def _(step):
        slot = lax.rem(step, 2)

        @pl.when(step >= 2)
        def _():
            out_copy(step - 2, slot).wait()

        for g in range(STEP_A // wide):
            blocks = []
            for k in range(wide):
                row = pl.multiple_of((step * STEP_A + g * wide + k) * pitch, 8)
                blocks.append(pairs[pl.ds(row, count), :].astype(jnp.bfloat16))
            both = jnp.concatenate(blocks, axis=1)
            for m in range(count // 256):
                rows = slice(m * 256, (m + 1) * 256)
                mixed = jnp.dot(ladder[rows, :], both, preferred_element_type=jnp.float32)
                total = (mixed + both[rows, :].astype(jnp.float32)).astype(jnp.bfloat16)
                out_buf[slot, g * wide:(g + 1) * wide, :, rows] = total.T.reshape(wide, b_local, 256)
        out_copy(step, slot).start()

    for step in range(max(steps - 2, 0), steps):
        out_copy(step, step % 2).wait()


def chunk_update(own, pieces, panel_w, ladder, out, after, q, a_local, b_local, occupied):
    rows, depth = pieces[0].shape
    count = occupied * occupied
    k_all, width = panel_w[0].shape
    parts = 1 + panel_w[1].shape[1] // width
    args = [*pieces, *panel_w, ladder, *after]
    aliases = {}
    if out is not None:
        aliases = {len(args) + 1: 0}
        args.append(out)
    flops = 2 * rows * k_all * occupied * b_local + 2 * GROUP * b_local * count * count
    size = parts * k_all * width + count * count + rows * k_all + GROUP * b_local * count
    return pl.pallas_call(
        functools.partial(chunk_kernel, parts=parts, occupied=occupied, b_local=b_local, q=q),
        out_shape=jax.ShapeDtypeStruct((a_local, b_local, count), jnp.bfloat16),
        in_specs=[pl.BlockSpec(memory_space=pltpu.SMEM)] + [ANY] * len(args),
        out_specs=ANY,
        scratch_shapes=[
            pltpu.VMEM((rows, k_all), jnp.bfloat16),
            pltpu.VMEM((2, k_all, width), jnp.bfloat16),
            pltpu.VMEM((count, count), jnp.bfloat16),
            pltpu.VMEM((GROUP * (count + PAD), b_local), jnp.float32),
            pltpu.VMEM((2, STEP_A, b_local, count), jnp.bfloat16),
            pltpu.SemaphoreType.DMA((parts,)),
            pltpu.SemaphoreType.DMA((2,)),
            pltpu.SemaphoreType.DMA,
            pltpu.SemaphoreType.DMA((2,)),
        ],
        input_output_aliases=aliases,
        compiler_params=pltpu.CompilerParams(vmem_limit_bytes=60 * 1024 * 1024),
        cost_estimate=pl.CostEstimate(flops=flops, bytes_accessed=2 * size, transcendentals=0),
    )(own.reshape(1), *args)


def plain_update(own, pieces, panel_w, ladder, b_local, occupied):
    parts = (len(pieces) + 1) // 2
    back = jnp.argsort(lax.rem(own - jnp.arange(parts) + parts, parts))
    rows, depth = pieces[0].shape
    right, left = pieces[1:parts], pieces[parts:]
    by_shift = [pieces[0]] + [jnp.where(own >= s, right[s - 1], left[parts - s - 1]) for s in range(1, parts)]
    panel_t = jnp.transpose(jnp.stack(by_shift, 0)[back], (1, 0, 2)).reshape(rows, -1)
    cycle = jnp.dot(panel_t, jnp.concatenate(panel_w, axis=1), preferred_element_type=jnp.float32)
    cycle = cycle.astype(jnp.bfloat16).reshape(occupied, -1, parts, occupied // parts, b_local)[:, :, back]
    cycle = cycle.reshape(occupied, -1, occupied, b_local)
    a_count = cycle.shape[1]
    pairs = jnp.transpose(cycle, (1, 3, 0, 2)).reshape(a_count * b_local, occupied * occupied)
    mixed = lax.dot_general(pairs, ladder, (((1,), (1,)), ((), ())), preferred_element_type=jnp.float32)
    total = (mixed + pairs.astype(jnp.float32)).astype(jnp.bfloat16)
    return total.reshape(a_count, b_local, occupied * occupied)


def local(rows, cols, amplitudes, couplings, ladder):
    depth = amplitudes.shape[1]
    i_local = amplitudes.shape[0] // V
    j_local = couplings.shape[1] // V
    occupied = i_local * rows
    a_local, b_local = V // rows, V // cols
    own = lax.axis_index("col")

    arrived = list(split_columns(own, couplings, cols, j_local, b_local))
    arrived[0], amplitudes = lax.optimization_barrier((arrived[0], amplitudes))
    for s in range(1, cols):
        arrived[s] = lax.ppermute(arrived[s], "col", [(c, (c + s) % cols) for c in range(cols)])

    chunks = a_local // GROUP
    blocks = amplitudes.reshape(i_local, rows, chunks, GROUP, depth).transpose(1, 2, 0, 3, 4)
    blocks = lax.all_to_all(blocks, "row", split_axis=0, concat_axis=0, tiled=True)

    per_part = occupied // cols
    plain = b_local % 128 or WIDE % b_local or depth % 128 or cols < 3 or per_part * b_local % WIDE or chunks < 3

    def update(q, out, after):
        return chunk_update(own, flat(pieces[q]), panel_w, ladder, out, after, q, a_local, b_local, occupied)

    def flat(sides):
        right, left = sides
        return [right[0], *right[1:], *left[1:]]

    rest, _ = lax.optimization_barrier((arrived[1:], blocks))
    panel_w = [
        lax.all_gather(part, "row", axis=0, tiled=True) for part in (arrived[0], jnp.concatenate(rest, axis=1))
    ]

    pieces, out = [], None
    for q in range(0, chunks, 2):
        both = [blocks[:, p].reshape(occupied * GROUP, depth) for p in range(q, min(q + 2, chunks))]
        if q:
            middle = (cols - 1) // 2
            for n, (right, left) in enumerate(pieces[-2:][:len(both)]):
                both[n], right[middle + 1], left[middle + 1] = lax.optimization_barrier(
                    (both[n], right[middle + 1], left[middle + 1]))
        pair = [([held], [held]) for held in both]
        final = q + 2 >= chunks and not plain
        for s in range(1, cols):
            if final and s == cols - 1:
                out = update(0, None, (pair[0][0][-1], pair[0][1][-1]))
            for n, (right, left) in enumerate(pair):
                if final and s == cols - 1 and n:
                    out, right[-1], left[-1] = lax.optimization_barrier((out, right[-1], left[-1]))
                right.append(lax.ppermute(right[-1], "col", [(c, c + 1) for c in range(s - 1, cols - 1)]))
                left.append(lax.ppermute(left[-1], "col", [(c + 1, c) for c in range(cols - s)]))
        pieces += pair

    if plain:
        return jnp.concatenate(
            [plain_update(own, flat(got), panel_w, ladder, b_local, occupied) for got in pieces], axis=0)
    for q in range(1, chunks):
        out = update(q, out, ())
    return out


def solution(mesh):
    in_specs = (P("row", "col"), P("row", "col"), P())
    out_specs = P("row", "col", None)
    body = functools.partial(local, mesh.shape["row"], mesh.shape["col"])
    return jax.shard_map(body, mesh=mesh, in_specs=in_specs, out_specs=out_specs, check_vma=False)
```

```python
import functools

import jax
import jax.numpy as jnp
from jax import lax
from jax.experimental import pallas as pl
from jax.experimental.pallas import tpu as pltpu
from jax.sharding import PartitionSpec as P

V = 512
GROUP = 16
STEP_A = 4
PAD = 8
WIDE = 512
ANY = pl.BlockSpec(memory_space=pl.ANY)


def cut_kernel(own, t_ref, w_ref, t_out, *refs, j_local, b_local):
    w_outs, t_sem, w_sem = refs[:-2], refs[-2], refs[-1]
    cols = len(w_outs)
    for s in range(cols):
        to = lax.rem(own[0] + s, cols)
        for j in range(j_local):
            start = pl.multiple_of((j * cols + to) * b_local, b_local)
            pltpu.make_async_copy(
                w_ref.at[:, pl.ds(start, b_local)], w_outs[s].at[:, j * b_local:(j + 1) * b_local], w_sem.at[s]
            ).start()
    for i in range(t_ref.shape[0]):
        for r in range(t_ref.shape[1]):
            pltpu.make_async_copy(t_ref.at[i, r], t_out.at[r, :, i], t_sem).start()
    for s in range(cols):
        pltpu.make_async_copy(w_outs[s], w_outs[s], w_sem.at[s]).wait()
    pltpu.make_async_copy(t_out, t_out, t_sem).wait()


def cut(own, blocks, couplings, cols, j_local, b_local):
    i_local, rows, chunks, group, t_depth = blocks.shape
    depth = couplings.shape[0]
    if b_local % 128 or t_depth % 128:
        split = couplings.reshape(depth, j_local, cols, b_local)
        parts = [
            lax.dynamic_index_in_dim(split, lax.rem(own + s, cols), 2, keepdims=False).reshape(depth, -1)
            for s in range(cols)
        ]
        return [blocks.transpose(1, 2, 0, 3, 4), *parts]
    return pl.pallas_call(
        functools.partial(cut_kernel, j_local=j_local, b_local=b_local),
        out_shape=[jax.ShapeDtypeStruct((rows, chunks, i_local, group, t_depth), blocks.dtype)]
        + [jax.ShapeDtypeStruct((depth, j_local * b_local), couplings.dtype)] * cols,
        in_specs=[pl.BlockSpec(memory_space=pltpu.SMEM), ANY, ANY],
        out_specs=[ANY] * (1 + cols),
        scratch_shapes=[pltpu.SemaphoreType.DMA, pltpu.SemaphoreType.DMA((cols,))],
        compiler_params=pltpu.CompilerParams(vmem_limit_bytes=60 * 1024 * 1024),
        cost_estimate=pl.CostEstimate(flops=0, bytes_accessed=4 * (blocks.size + couplings.size), transcendentals=0),
    )(own.reshape(1), blocks, couplings)


def chunk_kernel(own, *refs, parts, occupied, b_local, q):
    t_own, t_right, t_left = refs[0], refs[1:parts], refs[parts:2 * parts - 1]
    w_own, w_rest, ladder_hbm = refs[2 * parts - 1:2 * parts + 2]
    out_ref, t_all, w_buf, ladder, pairs, out_buf, t_sem, w_sem, l_sem, out_sem = refs[-10:]
    depth = t_own.shape[1]
    width = w_own.shape[1]
    count = occupied * occupied
    pitch = count + PAD
    per_part = occupied // parts
    wide = WIDE // b_local

    def t_copy(src, block, s):
        cols = pl.ds(pl.multiple_of(block * depth, depth), depth)
        return pltpu.make_async_copy(src, t_all.at[:, cols], t_sem.at[s])

    def w_copy(s, slot):
        src = w_rest.at[:, (s - 1) * width:s * width] if s else w_own
        return pltpu.make_async_copy(src, w_buf.at[slot], w_sem.at[slot])

    blocks = [lax.rem(own[0] - s + parts, parts) for s in range(parts)]
    t_copy(t_own, blocks[0], 0).start()
    for s in range(1, parts):
        @pl.when(own[0] >= s)
        def _():
            t_copy(t_right[s - 1], blocks[s], s).start()

        @pl.when(own[0] < s)
        def _():
            t_copy(t_left[parts - s - 1], blocks[s], s).start()
    w_copy(0, 0).start()
    ladder_copy = pltpu.make_async_copy(ladder_hbm, ladder, l_sem)
    for s in range(parts):
        t_copy(t_own, blocks[s], s).wait()

    @pl.loop(0, parts)
    def _(step):
        slot = lax.rem(step, 2)
        w_copy(0, slot).wait()
        for s in range(1, parts):
            @pl.when(step + 1 == s)
            def _():
                w_copy(s, s % 2).start()

        @pl.when(step == parts - 1)
        def _():
            ladder_copy.start()

        j0 = lax.rem(own[0] - step + parts, parts) * per_part
        for tile in range(per_part // wide):
            acc = jnp.dot(
                t_all[...], w_buf[slot, :, tile * WIDE:(tile + 1) * WIDE], preferred_element_type=jnp.float32)
            for i in range(occupied):
                for k in range(wide):
                    n = j0 + (i * occupied + tile * wide + k)
                    for h in range(GROUP // 8):
                        row = i * GROUP + h * 8
                        pairs[pl.ds(h * 8 * pitch + n, 8, stride=pitch), :] = (
                            acc[row:row + 8, k * b_local:(k + 1) * b_local])

    ladder_copy.wait()
    steps = GROUP // STEP_A

    def out_copy(step, slot):
        rows = pl.ds(q * GROUP + step * STEP_A, STEP_A)
        return pltpu.make_async_copy(out_buf.at[slot], out_ref.at[rows], out_sem.at[slot])

    @pl.loop(0, steps)
    def _(step):
        slot = lax.rem(step, 2)

        @pl.when(step >= 2)
        def _():
            out_copy(step - 2, slot).wait()

        for g in range(STEP_A // wide):
            blocks = []
            for k in range(wide):
                row = pl.multiple_of((step * STEP_A + g * wide + k) * pitch, 8)
                blocks.append(pairs[pl.ds(row, count), :].astype(jnp.bfloat16))
            both = jnp.concatenate(blocks, axis=1)
            for m in range(count // 256):
                rows = slice(m * 256, (m + 1) * 256)
                mixed = jnp.dot(ladder[rows, :], both, preferred_element_type=jnp.float32)
                total = (mixed + both[rows, :].astype(jnp.float32)).astype(jnp.bfloat16)
                out_buf[slot, g * wide:(g + 1) * wide, :, rows] = total.T.reshape(wide, b_local, 256)
        out_copy(step, slot).start()

    for step in range(max(steps - 2, 0), steps):
        out_copy(step, step % 2).wait()


def chunk_update(own, pieces, panel_w, ladder, out, after, q, a_local, b_local, occupied):
    rows, depth = pieces[0].shape
    count = occupied * occupied
    k_all, width = panel_w[0].shape
    parts = 1 + panel_w[1].shape[1] // width
    args = [*pieces, *panel_w, ladder, *after]
    aliases = {}
    if out is not None:
        aliases = {len(args) + 1: 0}
        args.append(out)
    flops = 2 * rows * k_all * occupied * b_local + 2 * GROUP * b_local * count * count
    size = parts * k_all * width + count * count + rows * k_all + GROUP * b_local * count
    return pl.pallas_call(
        functools.partial(chunk_kernel, parts=parts, occupied=occupied, b_local=b_local, q=q),
        out_shape=jax.ShapeDtypeStruct((a_local, b_local, count), jnp.bfloat16),
        in_specs=[pl.BlockSpec(memory_space=pltpu.SMEM)] + [ANY] * len(args),
        out_specs=ANY,
        scratch_shapes=[
            pltpu.VMEM((rows, k_all), jnp.bfloat16),
            pltpu.VMEM((2, k_all, width), jnp.bfloat16),
            pltpu.VMEM((count, count), jnp.bfloat16),
            pltpu.VMEM((GROUP * (count + PAD), b_local), jnp.float32),
            pltpu.VMEM((2, STEP_A, b_local, count), jnp.bfloat16),
            pltpu.SemaphoreType.DMA((parts,)),
            pltpu.SemaphoreType.DMA((2,)),
            pltpu.SemaphoreType.DMA,
            pltpu.SemaphoreType.DMA((2,)),
        ],
        input_output_aliases=aliases,
        compiler_params=pltpu.CompilerParams(vmem_limit_bytes=60 * 1024 * 1024),
        cost_estimate=pl.CostEstimate(flops=flops, bytes_accessed=2 * size, transcendentals=0),
    )(own.reshape(1), *args)


def plain_update(own, pieces, panel_w, ladder, b_local, occupied):
    parts = (len(pieces) + 1) // 2
    back = jnp.argsort(lax.rem(own - jnp.arange(parts) + parts, parts))
    rows, depth = pieces[0].shape
    right, left = pieces[1:parts], pieces[parts:]
    by_shift = [pieces[0]] + [jnp.where(own >= s, right[s - 1], left[parts - s - 1]) for s in range(1, parts)]
    panel_t = jnp.transpose(jnp.stack(by_shift, 0)[back], (1, 0, 2)).reshape(rows, -1)
    cycle = jnp.dot(panel_t, jnp.concatenate(panel_w, axis=1), preferred_element_type=jnp.float32)
    cycle = cycle.astype(jnp.bfloat16).reshape(occupied, -1, parts, occupied // parts, b_local)[:, :, back]
    cycle = cycle.reshape(occupied, -1, occupied, b_local)
    a_count = cycle.shape[1]
    pairs = jnp.transpose(cycle, (1, 3, 0, 2)).reshape(a_count * b_local, occupied * occupied)
    mixed = lax.dot_general(pairs, ladder, (((1,), (1,)), ((), ())), preferred_element_type=jnp.float32)
    total = (mixed + pairs.astype(jnp.float32)).astype(jnp.bfloat16)
    return total.reshape(a_count, b_local, occupied * occupied)


def local(rows, cols, amplitudes, couplings, ladder):
    depth = amplitudes.shape[1]
    i_local = amplitudes.shape[0] // V
    j_local = couplings.shape[1] // V
    occupied = i_local * rows
    a_local, b_local = V // rows, V // cols
    own = lax.axis_index("col")

    chunks = a_local // GROUP
    blocks = amplitudes.reshape(i_local, rows, chunks, GROUP, depth)
    blocks, *arrived = cut(own, blocks, couplings, cols, j_local, b_local)
    for s in range(1, cols):
        arrived[s] = lax.ppermute(arrived[s], "col", [(c, (c + s) % cols) for c in range(cols)])
    blocks = lax.all_to_all(blocks, "row", split_axis=0, concat_axis=0, tiled=True)

    rest, _ = lax.optimization_barrier((arrived[1:], blocks))
    panel_w = [
        lax.all_gather(part, "row", axis=0, tiled=True) for part in (arrived[0], jnp.concatenate(rest, axis=1))
    ]

    per_part = occupied // cols
    plain = (b_local % 128 or WIDE % b_local or depth % 128 or cols < 4
             or per_part * b_local % WIDE or chunks < 4 or chunks % 2)

    def flat(sides):
        right, left = sides
        return [right[0], *right[1:], *left[1:]]

    def update(q, out, after):
        return chunk_update(own, flat(pieces[q]), panel_w, ladder, out, after, q, a_local, b_local, occupied)

    def hop(sides, s):
        right, left = sides
        right.append(lax.ppermute(right[-1], "col", [(c, c + 1) for c in range(s - 1, cols - 1)]))
        left.append(lax.ppermute(left[-1], "col", [(c + 1, c) for c in range(cols - s)]))

    pieces, out = [], None
    for q in range(0, chunks, 2):
        both = [blocks[:, p].reshape(occupied * GROUP, depth) for p in range(q, min(q + 2, chunks))]
        if q:
            middle = (cols - 1) // 2
            for n, (right, left) in enumerate(pieces[-2:][:len(both)]):
                both[n], right[middle + 1], left[middle + 1] = lax.optimization_barrier(
                    (both[n], right[middle + 1], left[middle + 1]))
        pair = [([held], [held]) for held in both]
        pieces += pair
        if plain or q + 2 < chunks:
            for s in range(1, cols):
                for sides in pair:
                    hop(sides, s)
            continue
        x, y = pair
        hop(x, 1)
        for s in range(1, cols):
            if s == cols - 2:
                out = update(0, None, (x[0][s - 1], x[1][s - 1]))
                out, x[0][-1], x[1][-1], y[0][-1], y[1][-1] = lax.optimization_barrier(
                    (out, x[0][-1], x[1][-1], y[0][-1], y[1][-1]))
            if s == cols - 1:
                out = update(1, out, ())
                out, y[0][-1], y[1][-1] = lax.optimization_barrier((out, y[0][-1], y[1][-1]))
            hop(y, s)
            if s < cols - 1:
                hop(x, s + 1)

    if plain:
        return jnp.concatenate(
            [plain_update(own, flat(got), panel_w, ladder, b_local, occupied) for got in pieces], axis=0)
    for q in range(2, chunks):
        out = update(q, out, ())
    return out


def solution(mesh):
    in_specs = (P("row", "col"), P("row", "col"), P())
    out_specs = P("row", "col", None)
    body = functools.partial(local, mesh.shape["row"], mesh.shape["col"])
    return jax.shard_map(body, mesh=mesh, in_specs=in_specs, out_specs=out_specs, check_vma=False)
```

```python
import functools

import jax
import jax.numpy as jnp
from jax import lax
from jax.experimental import pallas as pl
from jax.experimental.pallas import tpu as pltpu
from jax.sharding import PartitionSpec as P

V = 512
GROUP = 16
STEP_A = 4
PAD = 8
WIDE = 512
ANY = pl.BlockSpec(memory_space=pl.ANY)


def cut_kernel(own, t_ref, w_ref, t_out, *refs, j_local, b_local):
    w_outs, t_sem, w_sem = refs[:-2], refs[-2], refs[-1]
    cols = len(w_outs)
    for s in range(cols):
        to = lax.rem(own[0] + s, cols)
        for j in range(j_local):
            start = pl.multiple_of((j * cols + to) * b_local, b_local)
            pltpu.make_async_copy(
                w_ref.at[:, pl.ds(start, b_local)], w_outs[s].at[:, j * b_local:(j + 1) * b_local], w_sem.at[s]
            ).start()
    for i in range(t_ref.shape[0]):
        for r in range(t_ref.shape[1]):
            pltpu.make_async_copy(t_ref.at[i, r], t_out.at[r, :, i], t_sem).start()
    for s in range(cols):
        pltpu.make_async_copy(w_outs[s], w_outs[s], w_sem.at[s]).wait()
    pltpu.make_async_copy(t_out, t_out, t_sem).wait()


def cut(own, blocks, couplings, cols, j_local, b_local):
    i_local, rows, chunks, group, t_depth = blocks.shape
    depth = couplings.shape[0]
    if b_local % 128 or t_depth % 128:
        split = couplings.reshape(depth, j_local, cols, b_local)
        parts = [
            lax.dynamic_index_in_dim(split, lax.rem(own + s, cols), 2, keepdims=False).reshape(depth, -1)
            for s in range(cols)
        ]
        return [blocks.transpose(1, 2, 0, 3, 4), *parts]
    return pl.pallas_call(
        functools.partial(cut_kernel, j_local=j_local, b_local=b_local),
        out_shape=[jax.ShapeDtypeStruct((rows, chunks, i_local, group, t_depth), blocks.dtype)]
        + [jax.ShapeDtypeStruct((depth, j_local * b_local), couplings.dtype)] * cols,
        in_specs=[pl.BlockSpec(memory_space=pltpu.SMEM), ANY, ANY],
        out_specs=[pl.BlockSpec(memory_space=pltpu.VMEM)] * (1 + cols),
        scratch_shapes=[pltpu.SemaphoreType.DMA, pltpu.SemaphoreType.DMA((cols,))],
        compiler_params=pltpu.CompilerParams(vmem_limit_bytes=60 * 1024 * 1024),
        cost_estimate=pl.CostEstimate(flops=0, bytes_accessed=4 * (blocks.size + couplings.size), transcendentals=0),
    )(own.reshape(1), blocks, couplings)


def chunk_kernel(own, *refs, starts, parts, occupied, b_local, q):
    t_refs = [ref.at[pl.ds(start, GROUP * occupied)] for ref, start in zip(refs, starts)]
    t_own, t_right, t_left = t_refs[0], t_refs[1:parts], t_refs[parts:]
    w_own, w_rest, ladder_hbm = refs[2 * parts - 1:2 * parts + 2]
    out_ref, t_all, w_buf, ladder, pairs, out_buf, t_sem, w_sem, l_sem, out_sem = refs[-10:]
    depth = t_own.shape[1]
    width = w_own.shape[1]
    count = occupied * occupied
    pitch = count + PAD
    per_part = occupied // parts
    wide = WIDE // b_local

    def t_copy(src, block, s):
        cols = pl.ds(pl.multiple_of(block * depth, depth), depth)
        return pltpu.make_async_copy(src, t_all.at[:, cols], t_sem.at[s])

    def w_copy(s, slot):
        src = w_rest.at[:, (s - 1) * width:s * width] if s else w_own
        return pltpu.make_async_copy(src, w_buf.at[slot], w_sem.at[slot])

    blocks = [lax.rem(own[0] - s + parts, parts) for s in range(parts)]
    t_copy(t_own, blocks[0], 0).start()
    for s in range(1, parts):
        @pl.when(own[0] >= s)
        def _():
            t_copy(t_right[s - 1], blocks[s], s).start()

        @pl.when(own[0] < s)
        def _():
            t_copy(t_left[parts - s - 1], blocks[s], s).start()
    w_copy(0, 0).start()
    ladder_copy = pltpu.make_async_copy(ladder_hbm, ladder, l_sem)
    for s in range(parts):
        t_copy(t_own, blocks[s], s).wait()

    @pl.loop(0, parts)
    def _(step):
        slot = lax.rem(step, 2)
        w_copy(0, slot).wait()
        for s in range(1, parts):
            @pl.when(step + 1 == s)
            def _():
                w_copy(s, s % 2).start()

        @pl.when(step == parts - 1)
        def _():
            ladder_copy.start()

        j0 = lax.rem(own[0] - step + parts, parts) * per_part
        for tile in range(per_part // wide):
            acc = jnp.dot(
                t_all[...], w_buf[slot, :, tile * WIDE:(tile + 1) * WIDE], preferred_element_type=jnp.float32)
            for i in range(occupied):
                for k in range(wide):
                    n = j0 + (i * occupied + tile * wide + k)
                    for h in range(GROUP // 8):
                        row = i * GROUP + h * 8
                        pairs[pl.ds(h * 8 * pitch + n, 8, stride=pitch), :] = (
                            acc[row:row + 8, k * b_local:(k + 1) * b_local])

    ladder_copy.wait()
    steps = GROUP // STEP_A

    def out_copy(step, slot):
        rows = pl.ds(q * GROUP + step * STEP_A, STEP_A)
        return pltpu.make_async_copy(out_buf.at[slot], out_ref.at[rows], out_sem.at[slot])

    @pl.loop(0, steps)
    def _(step):
        slot = lax.rem(step, 2)

        @pl.when(step >= 2)
        def _():
            out_copy(step - 2, slot).wait()

        for g in range(STEP_A // wide):
            blocks = []
            for k in range(wide):
                row = pl.multiple_of((step * STEP_A + g * wide + k) * pitch, 8)
                blocks.append(pairs[pl.ds(row, count), :].astype(jnp.bfloat16))
            both = jnp.concatenate(blocks, axis=1)
            for m in range(count // 256):
                rows = slice(m * 256, (m + 1) * 256)
                mixed = jnp.dot(ladder[rows, :], both, preferred_element_type=jnp.float32)
                total = (mixed + both[rows, :].astype(jnp.float32)).astype(jnp.bfloat16)
                out_buf[slot, g * wide:(g + 1) * wide, :, rows] = total.T.reshape(wide, b_local, 256)
        out_copy(step, slot).start()

    for step in range(max(steps - 2, 0), steps):
        out_copy(step, step % 2).wait()


def chunk_update(own, pieces, panel_w, ladder, out, after, q, a_local, b_local, occupied):
    arrays, starts = zip(*pieces)
    rows = GROUP * occupied
    count = occupied * occupied
    k_all, width = panel_w[0].shape
    parts = 1 + panel_w[1].shape[1] // width
    args = [*arrays, *panel_w, ladder, *after]
    aliases = {}
    if out is not None:
        aliases = {len(args) + 1: 0}
        args.append(out)
    flops = 2 * rows * k_all * occupied * b_local + 2 * GROUP * b_local * count * count
    size = parts * k_all * width + count * count + rows * k_all + GROUP * b_local * count
    return pl.pallas_call(
        functools.partial(chunk_kernel, starts=starts, parts=parts, occupied=occupied, b_local=b_local, q=q),
        out_shape=jax.ShapeDtypeStruct((a_local, b_local, count), jnp.bfloat16),
        in_specs=[pl.BlockSpec(memory_space=pltpu.SMEM)] + [ANY] * len(args),
        out_specs=ANY,
        scratch_shapes=[
            pltpu.VMEM((rows, k_all), jnp.bfloat16),
            pltpu.VMEM((2, k_all, width), jnp.bfloat16),
            pltpu.VMEM((count, count), jnp.bfloat16),
            pltpu.VMEM((GROUP * (count + PAD), b_local), jnp.float32),
            pltpu.VMEM((2, STEP_A, b_local, count), jnp.bfloat16),
            pltpu.SemaphoreType.DMA((parts,)),
            pltpu.SemaphoreType.DMA((2,)),
            pltpu.SemaphoreType.DMA,
            pltpu.SemaphoreType.DMA((2,)),
        ],
        input_output_aliases=aliases,
        compiler_params=pltpu.CompilerParams(vmem_limit_bytes=60 * 1024 * 1024),
        cost_estimate=pl.CostEstimate(flops=flops, bytes_accessed=2 * size, transcendentals=0),
    )(own.reshape(1), *args)


def plain_update(own, pieces, panel_w, ladder, b_local, occupied):
    parts = (len(pieces) + 1) // 2
    back = jnp.argsort(lax.rem(own - jnp.arange(parts) + parts, parts))
    rows, depth = pieces[0].shape
    right, left = pieces[1:parts], pieces[parts:]
    by_shift = [pieces[0]] + [jnp.where(own >= s, right[s - 1], left[parts - s - 1]) for s in range(1, parts)]
    panel_t = jnp.transpose(jnp.stack(by_shift, 0)[back], (1, 0, 2)).reshape(rows, -1)
    cycle = jnp.dot(panel_t, jnp.concatenate(panel_w, axis=1), preferred_element_type=jnp.float32)
    cycle = cycle.astype(jnp.bfloat16).reshape(occupied, -1, parts, occupied // parts, b_local)[:, :, back]
    cycle = cycle.reshape(occupied, -1, occupied, b_local)
    a_count = cycle.shape[1]
    pairs = jnp.transpose(cycle, (1, 3, 0, 2)).reshape(a_count * b_local, occupied * occupied)
    mixed = lax.dot_general(pairs, ladder, (((1,), (1,)), ((), ())), preferred_element_type=jnp.float32)
    total = (mixed + pairs.astype(jnp.float32)).astype(jnp.bfloat16)
    return total.reshape(a_count, b_local, occupied * occupied)


def local(rows, cols, amplitudes, couplings, ladder):
    depth = amplitudes.shape[1]
    i_local = amplitudes.shape[0] // V
    j_local = couplings.shape[1] // V
    occupied = i_local * rows
    a_local, b_local = V // rows, V // cols
    own = lax.axis_index("col")

    chunks = a_local // GROUP
    blocks = amplitudes.reshape(i_local, rows, chunks, GROUP, depth)
    blocks, *arrived = cut(own, blocks, couplings, cols, j_local, b_local)
    for s in range(1, cols):
        arrived[s] = lax.ppermute(arrived[s], "col", [(c, (c + s) % cols) for c in range(cols)])
    blocks = lax.all_to_all(blocks, "row", split_axis=0, concat_axis=0, tiled=True)

    rest, _ = lax.optimization_barrier((arrived[1:], blocks))
    panel_w = [
        lax.all_gather(part, "row", axis=0, tiled=True) for part in (arrived[0], jnp.concatenate(rest, axis=1))
    ]

    per_part = occupied // cols
    plain = (b_local % 128 or WIDE % b_local or depth % 128 or cols < 4
             or per_part * b_local % WIDE or chunks < 4 or chunks % 2)

    def flat(sides):
        right, left = sides
        return [right[0], *right[1:], *left[1:]]

    def update(q, out, after):
        blocks = [piece if isinstance(piece, tuple) else (piece, 0) for piece in flat(pieces[q])]
        return chunk_update(own, blocks, panel_w, ladder, out, after, q, a_local, b_local, occupied)

    def hop(sides, s, direct=False):
        right, left = sides
        first = 0 if direct else s - 1
        step = s if direct else 1
        source = 0 if direct else -1
        right.append(lax.ppermute(right[source], "col", [(c, c + step) for c in range(first, cols - step)]))
        left.append(lax.ppermute(left[source], "col", [(c + step, c) for c in range(cols - step - first)]))

    pieces = []
    for q in range(chunks):
        held = blocks[:, q].reshape(occupied * GROUP, depth)
        pieces.append(([held], [held]))

    if plain:
        for sides in pieces:
            for s in range(1, cols):
                hop(sides, s)
        return jnp.concatenate(
            [plain_update(own, flat(sides), panel_w, ladder, b_local, occupied) for sides in pieces], axis=0)

    def after(done, sides):
        right, left = sides
        done, right[0], left[0] = lax.optimization_barrier((done, right[0], left[0]))
        return done

    *early, x, y = pieces
    for q in range(0, len(early), 2):
        if q:
            for before, sides in zip(early[q - 2:q], early[q:q + 2]):
                before[0][-2], before[1][-2] = after((before[0][-2], before[1][-2]), sides)
        for s in range(1, cols):
            for sides in early[q:q + 2]:
                hop(sides, s)
    before = early[-2]
    before[0][-2], before[1][-2] = after((before[0][-2], before[1][-2]), x)
    for s in range(1, cols - 1):
        hop(x, s)
    far = (jnp.concatenate([x[0][0], y[0][0]]),) * 2
    far = ([far[0]], [far[1]])
    size = x[0][0].shape[0]
    out = update(0, None, (x[0][1], x[1][1]))
    moving = (early[-1][0], early[-1][1], x[0], x[1])
    out, *ends = after((out, *[side[-1] for side in moving]), far)
    for side, end in zip(moving, ends):
        side[-1] = end
    hop(far, cols - 1, direct=True)
    for n in (0, 1):
        x[n].append((far[n][1], 0))
    out = update(1, out, ())
    out = after(out, y)
    for s in range(1, cols - 1):
        hop(y, s, direct=True)
    for n in (0, 1):
        y[n].append((far[n][1], size))
    for q in range(2, chunks):
        out = update(q, out, ())
    return out


def solution(mesh):
    in_specs = (P("row", "col"), P("row", "col"), P())
    out_specs = P("row", "col", None)
    body = functools.partial(local, mesh.shape["row"], mesh.shape["col"])
    return jax.shard_map(body, mesh=mesh, in_specs=in_specs, out_specs=out_specs, check_vma=False)
```

```python
import functools

import jax
import jax.numpy as jnp
from jax import lax
from jax.experimental import pallas as pl
from jax.experimental.pallas import tpu as pltpu
from jax.sharding import PartitionSpec as P

V = 512
GROUP = 16
STEP_A = 4
PAD = 8
WIDE = 512
ANY = pl.BlockSpec(memory_space=pl.ANY)


def cut_kernel(own, t_ref, w_ref, t_out, *refs, j_local, b_local):
    w_outs, t_sem, w_sem = refs[:-2], refs[-2], refs[-1]
    cols = len(w_outs)
    for s in range(cols):
        to = lax.rem(own[0] + s, cols)
        for j in range(j_local):
            start = pl.multiple_of((j * cols + to) * b_local, b_local)
            pltpu.make_async_copy(
                w_ref.at[:, pl.ds(start, b_local)], w_outs[s].at[:, j * b_local:(j + 1) * b_local], w_sem.at[s]
            ).start()
    for i in range(t_ref.shape[0]):
        for r in range(t_ref.shape[1]):
            pltpu.make_async_copy(t_ref.at[i, r], t_out.at[r, :, i], t_sem).start()
    for s in range(cols):
        pltpu.make_async_copy(w_outs[s], w_outs[s], w_sem.at[s]).wait()
    pltpu.make_async_copy(t_out, t_out, t_sem).wait()


def cut(own, blocks, couplings, cols, j_local, b_local):
    i_local, rows, chunks, group, t_depth = blocks.shape
    depth = couplings.shape[0]
    if b_local % 128 or t_depth % 128:
        split = couplings.reshape(depth, j_local, cols, b_local)
        parts = [
            lax.dynamic_index_in_dim(split, lax.rem(own + s, cols), 2, keepdims=False).reshape(depth, -1)
            for s in range(cols)
        ]
        return [blocks.transpose(1, 2, 0, 3, 4), *parts]
    return pl.pallas_call(
        functools.partial(cut_kernel, j_local=j_local, b_local=b_local),
        out_shape=[jax.ShapeDtypeStruct((rows, chunks, i_local, group, t_depth), blocks.dtype)]
        + [jax.ShapeDtypeStruct((depth, j_local * b_local), couplings.dtype)] * cols,
        in_specs=[pl.BlockSpec(memory_space=pltpu.SMEM), ANY, ANY],
        out_specs=[pl.BlockSpec(memory_space=pltpu.VMEM)] * (1 + cols),
        scratch_shapes=[pltpu.SemaphoreType.DMA, pltpu.SemaphoreType.DMA((cols,))],
        compiler_params=pltpu.CompilerParams(vmem_limit_bytes=60 * 1024 * 1024),
        cost_estimate=pl.CostEstimate(flops=0, bytes_accessed=4 * (blocks.size + couplings.size), transcendentals=0),
    )(own.reshape(1), blocks, couplings)


def chunk_kernel(own, *refs, pieces, parts, occupied, b_local, q):
    t_own, t_right, t_left = refs[0], refs[1:parts], refs[parts:pieces]
    w_own, w_rest, ladder_hbm = refs[pieces:pieces + 3]
    out_ref, t_all, w_buf, ladder, pairs, out_buf, t_sem, w_sem, l_sem, out_sem = refs[-10:]
    depth = t_all.shape[1] // parts
    width = w_own.shape[1]
    count = occupied * occupied
    pitch = count + PAD
    per_part = occupied // parts
    wide = WIDE // b_local

    def t_copy(src, block, s):
        cols = pl.ds(pl.multiple_of(block * depth, depth), depth)
        return pltpu.make_async_copy(src, t_all.at[:, cols], t_sem.at[s])

    def w_copy(s, slot):
        src = w_rest.at[:, (s - 1) * width:s * width] if s else w_own
        return pltpu.make_async_copy(src, w_buf.at[slot], w_sem.at[slot])

    blocks = [lax.rem(own[0] - s + parts, parts) for s in range(parts)]
    if pieces == 1:
        pltpu.make_async_copy(t_own, t_all, t_sem.at[0]).start()
    else:
        t_copy(t_own, blocks[0], 0).start()
        for s in range(1, parts):
            @pl.when(own[0] >= s)
            def _():
                t_copy(t_right[s - 1], blocks[s], s).start()

            @pl.when(own[0] < s)
            def _():
                t_copy(t_left[parts - s - 1], blocks[s], s).start()
    w_copy(0, 0).start()
    ladder_copy = pltpu.make_async_copy(ladder_hbm, ladder, l_sem)
    if pieces == 1:
        pltpu.make_async_copy(t_own, t_all, t_sem.at[0]).wait()
    else:
        for s in range(parts):
            t_copy(t_own, blocks[s], s).wait()

    @pl.loop(0, parts)
    def _(step):
        slot = lax.rem(step, 2)
        w_copy(0, slot).wait()
        for s in range(1, parts):
            @pl.when(step + 1 == s)
            def _():
                w_copy(s, s % 2).start()

        @pl.when(step == parts - 1)
        def _():
            ladder_copy.start()

        j0 = lax.rem(own[0] - step + parts, parts) * per_part
        for tile in range(per_part // wide):
            acc = jnp.dot(
                t_all[...], w_buf[slot, :, tile * WIDE:(tile + 1) * WIDE], preferred_element_type=jnp.float32)
            for i in range(occupied):
                for k in range(wide):
                    n = j0 + (i * occupied + tile * wide + k)
                    for h in range(GROUP // 8):
                        row = i * GROUP + h * 8
                        pairs[pl.ds(h * 8 * pitch + n, 8, stride=pitch), :] = (
                            acc[row:row + 8, k * b_local:(k + 1) * b_local])

    ladder_copy.wait()
    steps = GROUP // STEP_A

    def out_copy(step, slot):
        rows = pl.ds(q * GROUP + step * STEP_A, STEP_A)
        return pltpu.make_async_copy(out_buf.at[slot], out_ref.at[rows], out_sem.at[slot])

    @pl.loop(0, steps)
    def _(step):
        slot = lax.rem(step, 2)

        @pl.when(step >= 2)
        def _():
            out_copy(step - 2, slot).wait()

        for g in range(STEP_A // wide):
            blocks = []
            for k in range(wide):
                row = pl.multiple_of((step * STEP_A + g * wide + k) * pitch, 8)
                blocks.append(pairs[pl.ds(row, count), :].astype(jnp.bfloat16))
            both = jnp.concatenate(blocks, axis=1)
            for m in range(count // 256):
                rows = slice(m * 256, (m + 1) * 256)
                mixed = jnp.dot(ladder[rows, :], both, preferred_element_type=jnp.float32)
                total = (mixed + both[rows, :].astype(jnp.float32)).astype(jnp.bfloat16)
                out_buf[slot, g * wide:(g + 1) * wide, :, rows] = total.T.reshape(wide, b_local, 256)
        out_copy(step, slot).start()

    for step in range(max(steps - 2, 0), steps):
        out_copy(step, step % 2).wait()


def chunk_update(own, pieces, panel_w, ladder, out, after, q, a_local, b_local, occupied):
    rows = GROUP * occupied
    count = occupied * occupied
    k_all, width = panel_w[0].shape
    parts = 1 + panel_w[1].shape[1] // width
    args = [*pieces, *panel_w, ladder, *after]
    aliases = {}
    if out is not None:
        aliases = {len(args) + 1: 0}
        args.append(out)
    flops = 2 * rows * k_all * occupied * b_local + 2 * GROUP * b_local * count * count
    size = parts * k_all * width + count * count + rows * k_all + GROUP * b_local * count
    return pl.pallas_call(
        functools.partial(chunk_kernel, pieces=len(pieces), parts=parts, occupied=occupied, b_local=b_local, q=q),
        out_shape=jax.ShapeDtypeStruct((a_local, b_local, count), jnp.bfloat16),
        in_specs=[pl.BlockSpec(memory_space=pltpu.SMEM)] + [ANY] * len(args),
        out_specs=ANY,
        scratch_shapes=[
            pltpu.VMEM((rows, k_all), jnp.bfloat16),
            pltpu.VMEM((2, k_all, width), jnp.bfloat16),
            pltpu.VMEM((count, count), jnp.bfloat16),
            pltpu.VMEM((GROUP * (count + PAD), b_local), jnp.float32),
            pltpu.VMEM((2, STEP_A, b_local, count), jnp.bfloat16),
            pltpu.SemaphoreType.DMA((parts,)),
            pltpu.SemaphoreType.DMA((2,)),
            pltpu.SemaphoreType.DMA,
            pltpu.SemaphoreType.DMA((2,)),
        ],
        input_output_aliases=aliases,
        compiler_params=pltpu.CompilerParams(vmem_limit_bytes=60 * 1024 * 1024),
        cost_estimate=pl.CostEstimate(flops=flops, bytes_accessed=2 * size, transcendentals=0),
    )(own.reshape(1), *args)


def plain_update(own, pieces, panel_w, ladder, b_local, occupied):
    parts = (len(pieces) + 1) // 2
    back = jnp.argsort(lax.rem(own - jnp.arange(parts) + parts, parts))
    rows, depth = pieces[0].shape
    right, left = pieces[1:parts], pieces[parts:]
    by_shift = [pieces[0]] + [jnp.where(own >= s, right[s - 1], left[parts - s - 1]) for s in range(1, parts)]
    panel_t = jnp.transpose(jnp.stack(by_shift, 0)[back], (1, 0, 2)).reshape(rows, -1)
    cycle = jnp.dot(panel_t, jnp.concatenate(panel_w, axis=1), preferred_element_type=jnp.float32)
    cycle = cycle.astype(jnp.bfloat16).reshape(occupied, -1, parts, occupied // parts, b_local)[:, :, back]
    cycle = cycle.reshape(occupied, -1, occupied, b_local)
    a_count = cycle.shape[1]
    pairs = jnp.transpose(cycle, (1, 3, 0, 2)).reshape(a_count * b_local, occupied * occupied)
    mixed = lax.dot_general(pairs, ladder, (((1,), (1,)), ((), ())), preferred_element_type=jnp.float32)
    total = (mixed + pairs.astype(jnp.float32)).astype(jnp.bfloat16)
    return total.reshape(a_count, b_local, occupied * occupied)


def local(rows, cols, amplitudes, couplings, ladder):
    depth = amplitudes.shape[1]
    i_local = amplitudes.shape[0] // V
    j_local = couplings.shape[1] // V
    occupied = i_local * rows
    a_local, b_local = V // rows, V // cols
    own = lax.axis_index("col")

    chunks = a_local // GROUP
    blocks = amplitudes.reshape(i_local, rows, chunks, GROUP, depth)
    blocks, *arrived = cut(own, blocks, couplings, cols, j_local, b_local)
    for s in range(1, cols):
        arrived[s] = lax.ppermute(arrived[s], "col", [(c, (c + s) % cols) for c in range(cols)])
    blocks = lax.all_to_all(blocks, "row", split_axis=0, concat_axis=0, tiled=True)

    rest, _ = lax.optimization_barrier((arrived[1:], blocks))
    panel_w = [
        lax.all_gather(part, "row", axis=0, tiled=True) for part in (arrived[0], jnp.concatenate(rest, axis=1))
    ]

    per_part = occupied // cols
    plain = (b_local % 128 or WIDE % b_local or depth % 128 or cols < 4
             or per_part * b_local % WIDE or chunks < 4 or chunks % 2)

    def flat(sides):
        right, left = sides
        return [right[0], *right[1:], *left[1:]]

    def update(q, out, after):
        blocks = [last] if q == chunks - 1 else flat(pieces[q])
        return chunk_update(own, blocks, panel_w, ladder, out, after, q, a_local, b_local, occupied)

    def hop(sides, s, direct=False):
        right, left = sides
        first = 0 if direct else s - 1
        step = s if direct else 1
        source = 0 if direct else -1
        right.append(lax.ppermute(right[source], "col", [(c, c + step) for c in range(first, cols - step)]))
        left.append(lax.ppermute(left[source], "col", [(c + step, c) for c in range(cols - step - first)]))

    pieces = []
    for q in range(chunks):
        held = blocks[:, q].reshape(occupied * GROUP, depth)
        pieces.append(([held], [held]))

    if plain:
        for sides in pieces:
            for s in range(1, cols):
                hop(sides, s)
        return jnp.concatenate(
            [plain_update(own, flat(sides), panel_w, ladder, b_local, occupied) for sides in pieces], axis=0)

    def after(done, sides):
        right, left = sides
        done, right[0], left[0] = lax.optimization_barrier((done, right[0], left[0]))
        return done

    *early, x, y = pieces
    for q in range(0, len(early), 2):
        if q:
            for before, sides in zip(early[q - 2:q], early[q:q + 2]):
                before[0][-2], before[1][-2] = after((before[0][-2], before[1][-2]), sides)
        for s in range(1, cols):
            for sides in early[q:q + 2]:
                hop(sides, s)
    first = early[0]
    first[0][1], first[1][1] = after((first[0][1], first[1][1]), y)
    last = lax.all_gather(y[0][0], "col", axis=1, tiled=True)

    before = early[-2]
    before[0][-2], before[1][-2] = after((before[0][-2], before[1][-2]), x)
    for s in range(1, cols - 1):
        hop(x, s)
    for sides, n in ((early[-1], -2), (x, 1)):
        sides[0][n], sides[1][n] = after((sides[0][n], sides[1][n]), x)
    hop(x, cols - 1, direct=True)
    out = None
    for q in range(chunks):
        out = update(q, out, () if q else (x[0][1], x[1][1]))
    return out


def solution(mesh):
    in_specs = (P("row", "col"), P("row", "col"), P())
    out_specs = P("row", "col", None)
    body = functools.partial(local, mesh.shape["row"], mesh.shape["col"])
    return jax.shard_map(body, mesh=mesh, in_specs=in_specs, out_specs=out_specs, check_vma=False)
```

```python
import functools

import jax
import jax.numpy as jnp
from jax import lax
from jax.experimental import pallas as pl
from jax.experimental.pallas import tpu as pltpu
from jax.sharding import PartitionSpec as P

V = 512
GROUP = 16
STEP_A = 4
PAD = 8
WIDE = 512
ANY = pl.BlockSpec(memory_space=pl.ANY)


def cut_kernel(own, t_ref, w_ref, t_out, *refs, j_local, b_local):
    w_outs, t_sem, w_sem = refs[:-2], refs[-2], refs[-1]
    cols = len(w_outs)
    for s in range(cols):
        to = lax.rem(own[0] + s, cols)
        for j in range(j_local):
            start = pl.multiple_of((j * cols + to) * b_local, b_local)
            pltpu.make_async_copy(
                w_ref.at[:, pl.ds(start, b_local)], w_outs[s].at[:, j * b_local:(j + 1) * b_local], w_sem.at[s]
            ).start()
    for i in range(t_ref.shape[0]):
        for r in range(t_ref.shape[1]):
            pltpu.make_async_copy(t_ref.at[i, r], t_out.at[r, :, i], t_sem).start()
    for s in range(cols):
        pltpu.make_async_copy(w_outs[s], w_outs[s], w_sem.at[s]).wait()
    pltpu.make_async_copy(t_out, t_out, t_sem).wait()


def cut(own, blocks, couplings, cols, j_local, b_local):
    i_local, rows, chunks, group, t_depth = blocks.shape
    depth = couplings.shape[0]
    if b_local % 128 or t_depth % 128:
        split = couplings.reshape(depth, j_local, cols, b_local)
        parts = [
            lax.dynamic_index_in_dim(split, lax.rem(own + s, cols), 2, keepdims=False).reshape(depth, -1)
            for s in range(cols)
        ]
        return [blocks.transpose(1, 2, 0, 3, 4), *parts]
    return pl.pallas_call(
        functools.partial(cut_kernel, j_local=j_local, b_local=b_local),
        out_shape=[jax.ShapeDtypeStruct((rows, chunks, i_local, group, t_depth), blocks.dtype)]
        + [jax.ShapeDtypeStruct((depth, j_local * b_local), couplings.dtype)] * cols,
        in_specs=[pl.BlockSpec(memory_space=pltpu.SMEM), ANY, ANY],
        out_specs=[pl.BlockSpec(memory_space=pltpu.VMEM)] * (1 + cols),
        scratch_shapes=[pltpu.SemaphoreType.DMA, pltpu.SemaphoreType.DMA((cols,))],
        compiler_params=pltpu.CompilerParams(vmem_limit_bytes=60 * 1024 * 1024),
        cost_estimate=pl.CostEstimate(flops=0, bytes_accessed=4 * (blocks.size + couplings.size), transcendentals=0),
    )(own.reshape(1), blocks, couplings)


def chunk_kernel(own, *refs, groups, pieces, parts, occupied, b_local, q):
    t_refs = [refs[g * pieces:(g + 1) * pieces] for g in range(groups)]
    w_own, w_rest, ladder_hbm = refs[groups * pieces:groups * pieces + 3]
    out_ref, t_all, w_buf, ladder, pairs, out_buf, t_sem, w_sem, l_sem, out_sem = refs[-10:]
    depth = t_all.shape[1] // parts
    width = w_own.shape[1]
    count = occupied * occupied
    pitch = count + PAD
    per_part = occupied // parts
    wide = WIDE // b_local

    size = GROUP * occupied

    def t_copy(src, g, block, s):
        cols = pl.ds(pl.multiple_of(block * depth, depth), depth)
        return pltpu.make_async_copy(src, t_all.at[g * size:(g + 1) * size, cols], t_sem.at[g, s])

    def w_copy(s, slot):
        src = w_rest.at[:, (s - 1) * width:s * width] if s else w_own
        return pltpu.make_async_copy(src, w_buf.at[slot], w_sem.at[slot])

    blocks = [lax.rem(own[0] - s + parts, parts) for s in range(parts)]
    for g in range(groups):
        t_own, t_right, t_left = t_refs[g][0], t_refs[g][1:parts], t_refs[g][parts:]
        if pieces == 1:
            pltpu.make_async_copy(t_own, t_all.at[g * size:(g + 1) * size], t_sem.at[g, 0]).start()
            continue
        t_copy(t_own, g, blocks[0], 0).start()
        for s in range(1, parts):
            @pl.when(own[0] >= s)
            def _():
                t_copy(t_right[s - 1], g, blocks[s], s).start()

            @pl.when(own[0] < s)
            def _():
                t_copy(t_left[parts - s - 1], g, blocks[s], s).start()
    w_copy(0, 0).start()
    ladder_copy = pltpu.make_async_copy(ladder_hbm, ladder, l_sem)
    for g in range(groups):
        if pieces == 1:
            pltpu.make_async_copy(t_refs[g][0], t_all.at[g * size:(g + 1) * size], t_sem.at[g, 0]).wait()
            continue
        for s in range(parts):
            t_copy(t_refs[g][0], g, blocks[s], s).wait()

    @pl.loop(0, parts)
    def _(step):
        slot = lax.rem(step, 2)
        w_copy(0, slot).wait()
        for s in range(1, parts):
            @pl.when(step + 1 == s)
            def _():
                w_copy(s, s % 2).start()

        @pl.when(step == parts - 1)
        def _():
            ladder_copy.start()

        j0 = lax.rem(own[0] - step + parts, parts) * per_part
        for tile in range(per_part // wide):
            acc = jnp.dot(
                t_all[...], w_buf[slot, :, tile * WIDE:(tile + 1) * WIDE], preferred_element_type=jnp.float32)
            for i in range(occupied):
                for k in range(wide):
                    n = j0 + (i * occupied + tile * wide + k)
                    for g in range(groups):
                        for h in range(0, GROUP, 8):
                            row = g * size + i * GROUP + h
                            pairs[pl.ds((g * GROUP + h) * pitch + n, 8, stride=pitch), :] = (
                                acc[row:row + 8, k * b_local:(k + 1) * b_local])

    ladder_copy.wait()
    steps = groups * GROUP // STEP_A

    def out_copy(step, slot):
        rows = pl.ds(q * GROUP + step * STEP_A, STEP_A)
        return pltpu.make_async_copy(out_buf.at[slot], out_ref.at[rows], out_sem.at[slot])

    @pl.loop(0, steps)
    def _(step):
        slot = lax.rem(step, 2)

        @pl.when(step >= 2)
        def _():
            out_copy(step - 2, slot).wait()

        for g in range(STEP_A // wide):
            blocks = []
            for k in range(wide):
                row = pl.multiple_of((step * STEP_A + g * wide + k) * pitch, 8)
                blocks.append(pairs[pl.ds(row, count), :].astype(jnp.bfloat16))
            both = jnp.concatenate(blocks, axis=1)
            for m in range(count // 256):
                rows = slice(m * 256, (m + 1) * 256)
                mixed = jnp.dot(ladder[rows, :], both, preferred_element_type=jnp.float32)
                total = (mixed + both[rows, :].astype(jnp.float32)).astype(jnp.bfloat16)
                out_buf[slot, g * wide:(g + 1) * wide, :, rows] = total.T.reshape(wide, b_local, 256)
        out_copy(step, slot).start()

    for step in range(max(steps - 2, 0), steps):
        out_copy(step, step % 2).wait()


def chunk_update(own, chunks, panel_w, ladder, out, q, a_local, b_local, occupied):
    groups = len(chunks)
    rows = groups * GROUP * occupied
    count = occupied * occupied
    k_all, width = panel_w[0].shape
    parts = 1 + panel_w[1].shape[1] // width
    args = [*[piece for pieces in chunks for piece in pieces], *panel_w, ladder]
    aliases = {}
    if out is not None:
        aliases = {len(args) + 1: 0}
        args.append(out)
    flops = 2 * rows * k_all * occupied * b_local + 2 * groups * GROUP * b_local * count * count
    size = parts * k_all * width + count * count + rows * k_all + groups * GROUP * b_local * count
    return pl.pallas_call(
        functools.partial(
            chunk_kernel, groups=groups, pieces=len(chunks[0]), parts=parts, occupied=occupied, b_local=b_local, q=q),
        out_shape=jax.ShapeDtypeStruct((a_local, b_local, count), jnp.bfloat16),
        in_specs=[pl.BlockSpec(memory_space=pltpu.SMEM)] + [ANY] * len(args),
        out_specs=ANY,
        scratch_shapes=[
            pltpu.VMEM((rows, k_all), jnp.bfloat16),
            pltpu.VMEM((2, k_all, width), jnp.bfloat16),
            pltpu.VMEM((count, count), jnp.bfloat16),
            pltpu.VMEM((groups * GROUP * (count + PAD), b_local), jnp.float32),
            pltpu.VMEM((2, STEP_A, b_local, count), jnp.bfloat16),
            pltpu.SemaphoreType.DMA((groups, parts)),
            pltpu.SemaphoreType.DMA((2,)),
            pltpu.SemaphoreType.DMA,
            pltpu.SemaphoreType.DMA((2,)),
        ],
        input_output_aliases=aliases,
        compiler_params=pltpu.CompilerParams(vmem_limit_bytes=60 * 1024 * 1024),
        cost_estimate=pl.CostEstimate(flops=flops, bytes_accessed=2 * size, transcendentals=0),
    )(own.reshape(1), *args)


def plain_update(own, pieces, panel_w, ladder, b_local, occupied):
    parts = (len(pieces) + 1) // 2
    back = jnp.argsort(lax.rem(own - jnp.arange(parts) + parts, parts))
    rows, depth = pieces[0].shape
    right, left = pieces[1:parts], pieces[parts:]
    by_shift = [pieces[0]] + [jnp.where(own >= s, right[s - 1], left[parts - s - 1]) for s in range(1, parts)]
    panel_t = jnp.transpose(jnp.stack(by_shift, 0)[back], (1, 0, 2)).reshape(rows, -1)
    cycle = jnp.dot(panel_t, jnp.concatenate(panel_w, axis=1), preferred_element_type=jnp.float32)
    cycle = cycle.astype(jnp.bfloat16).reshape(occupied, -1, parts, occupied // parts, b_local)[:, :, back]
    cycle = cycle.reshape(occupied, -1, occupied, b_local)
    a_count = cycle.shape[1]
    pairs = jnp.transpose(cycle, (1, 3, 0, 2)).reshape(a_count * b_local, occupied * occupied)
    mixed = lax.dot_general(pairs, ladder, (((1,), (1,)), ((), ())), preferred_element_type=jnp.float32)
    total = (mixed + pairs.astype(jnp.float32)).astype(jnp.bfloat16)
    return total.reshape(a_count, b_local, occupied * occupied)


def local(rows, cols, amplitudes, couplings, ladder):
    depth = amplitudes.shape[1]
    i_local = amplitudes.shape[0] // V
    j_local = couplings.shape[1] // V
    occupied = i_local * rows
    a_local, b_local = V // rows, V // cols
    own = lax.axis_index("col")

    chunks = a_local // GROUP
    blocks = amplitudes.reshape(i_local, rows, chunks, GROUP, depth)
    blocks, *arrived = cut(own, blocks, couplings, cols, j_local, b_local)
    for s in range(1, cols):
        arrived[s] = lax.ppermute(arrived[s], "col", [(c, (c + s) % cols) for c in range(cols)])
    blocks = lax.all_to_all(blocks, "row", split_axis=0, concat_axis=0, tiled=True)

    rest, _ = lax.optimization_barrier((arrived[1:], blocks))
    panel_w = [
        lax.all_gather(part, "row", axis=0, tiled=True) for part in (arrived[0], jnp.concatenate(rest, axis=1))
    ]

    per_part = occupied // cols
    plain = (b_local % 128 or WIDE % b_local or depth % 128 or cols < 4
             or per_part * b_local % WIDE or chunks < 4 or chunks % 2)

    def flat(sides):
        right, left = sides
        return [right[0], *right[1:], *left[1:]]

    def hop(sides, s, direct=False):
        right, left = sides
        first = 0 if direct else s - 1
        step = s if direct else 1
        source = 0 if direct else -1
        right.append(lax.ppermute(right[source], "col", [(c, c + step) for c in range(first, cols - step)]))
        left.append(lax.ppermute(left[source], "col", [(c + step, c) for c in range(cols - step - first)]))

    pieces = []
    for q in range(chunks):
        held = blocks[:, q].reshape(occupied * GROUP, depth)
        pieces.append(([held], [held]))

    if plain:
        for sides in pieces:
            for s in range(1, cols):
                hop(sides, s)
        return jnp.concatenate(
            [plain_update(own, flat(sides), panel_w, ladder, b_local, occupied) for sides in pieces], axis=0)

    def after(done, sides):
        right, left = sides
        done, right[0], left[0] = lax.optimization_barrier((done, right[0], left[0]))
        return done

    *early, x, y = pieces
    for q in range(0, len(early), 2):
        if q:
            for before, sides in zip(early[q - 2:q], early[q:q + 2]):
                before[0][-2], before[1][-2] = after((before[0][-2], before[1][-2]), sides)
        for s in range(1, cols):
            for sides in early[q:q + 2]:
                hop(sides, s)
    first = early[0]
    first[0][1], first[1][1] = after((first[0][1], first[1][1]), y)
    last = lax.all_gather(y[0][0], "col", axis=1, tiled=True)

    before = early[-2]
    before[0][-2], before[1][-2] = after((before[0][-2], before[1][-2]), x)
    for s in range(1, cols - 1):
        hop(x, s)
    for sides, n in ((early[0], -1), (early[-1], -2), (x, 1)):
        sides[0][n], sides[1][n] = after((sides[0][n], sides[1][n]), x)
    hop(x, cols - 1, direct=True)
    update = functools.partial(chunk_update, own, a_local=a_local, b_local=b_local, occupied=occupied)
    out = None
    for q in range(0, len(early), 2):
        out = update([flat(sides) for sides in early[q:q + 2]], panel_w, ladder, out, q)
    out = update([flat(x)], panel_w, ladder, out, len(early))
    return update([[last]], panel_w, ladder, out, chunks - 1)


def solution(mesh):
    in_specs = (P("row", "col"), P("row", "col"), P())
    out_specs = P("row", "col", None)
    body = functools.partial(local, mesh.shape["row"], mesh.shape["col"])
    return jax.shard_map(body, mesh=mesh, in_specs=in_specs, out_specs=out_specs, check_vma=False)
```

```python
import functools

import jax
import jax.numpy as jnp
from jax import lax
from jax.experimental import pallas as pl
from jax.experimental.pallas import tpu as pltpu
from jax.sharding import PartitionSpec as P

V = 512
GROUP = 16
STEP_A = 4
PAD = 8
WIDE = 512
ANY = pl.BlockSpec(memory_space=pl.ANY)


def cut_kernel(own, t_ref, w_ref, t_out, *refs, j_local, b_local):
    w_outs, t_sem, w_sem = refs[:-2], refs[-2], refs[-1]
    cols = len(w_outs)
    for s in range(cols):
        to = lax.rem(own[0] + s, cols)
        for j in range(j_local):
            start = pl.multiple_of((j * cols + to) * b_local, b_local)
            pltpu.make_async_copy(
                w_ref.at[:, pl.ds(start, b_local)], w_outs[s].at[:, j * b_local:(j + 1) * b_local], w_sem.at[s]
            ).start()
    for i in range(t_ref.shape[0]):
        for r in range(t_ref.shape[1]):
            pltpu.make_async_copy(t_ref.at[i, r], t_out.at[r, :, i], t_sem).start()
    for s in range(cols):
        pltpu.make_async_copy(w_outs[s], w_outs[s], w_sem.at[s]).wait()
    pltpu.make_async_copy(t_out, t_out, t_sem).wait()


def cut(own, blocks, couplings, cols, j_local, b_local):
    i_local, rows, chunks, group, t_depth = blocks.shape
    depth = couplings.shape[0]
    if b_local % 128 or t_depth % 128:
        split = couplings.reshape(depth, j_local, cols, b_local)
        parts = [
            lax.dynamic_index_in_dim(split, lax.rem(own + s, cols), 2, keepdims=False).reshape(depth, -1)
            for s in range(cols)
        ]
        return [blocks.transpose(1, 2, 0, 3, 4), *parts]
    return pl.pallas_call(
        functools.partial(cut_kernel, j_local=j_local, b_local=b_local),
        out_shape=[jax.ShapeDtypeStruct((rows, chunks, i_local, group, t_depth), blocks.dtype)]
        + [jax.ShapeDtypeStruct((depth, j_local * b_local), couplings.dtype)] * cols,
        in_specs=[pl.BlockSpec(memory_space=pltpu.SMEM), ANY, ANY],
        out_specs=[pl.BlockSpec(memory_space=pltpu.VMEM)] * (1 + cols),
        scratch_shapes=[pltpu.SemaphoreType.DMA, pltpu.SemaphoreType.DMA((cols,))],
        compiler_params=pltpu.CompilerParams(vmem_limit_bytes=60 * 1024 * 1024),
        cost_estimate=pl.CostEstimate(flops=0, bytes_accessed=4 * (blocks.size + couplings.size), transcendentals=0),
    )(own.reshape(1), blocks, couplings)


def chunk_kernel(own, *refs, groups, pieces, parts, occupied, b_local, q):
    t_refs = [refs[g * pieces:(g + 1) * pieces] for g in range(groups)]
    w_own, w_rest, ladder_hbm = refs[groups * pieces:groups * pieces + 3]
    out_ref, t_all, w_buf, ladder, pairs, out_buf, t_sem, w_sem, l_sem, out_sem = refs[-10:]
    depth = t_all.shape[1] // parts
    width = w_own.shape[1]
    count = occupied * occupied
    pitch = count + PAD
    per_part = occupied // parts
    wide = WIDE // b_local

    size = GROUP * occupied

    def t_copy(src, g, block, s):
        cols = pl.ds(pl.multiple_of(block * depth, depth), depth)
        return pltpu.make_async_copy(src, t_all.at[g * size:(g + 1) * size, cols], t_sem.at[g, s])

    def w_copy(s, slot):
        src = w_rest.at[:, (s - 1) * width:s * width] if s else w_own
        return pltpu.make_async_copy(src, w_buf.at[slot], w_sem.at[slot])

    blocks = [lax.rem(own[0] - s + parts, parts) for s in range(parts)]
    for g in range(groups):
        t_own, t_right, t_left = t_refs[g][0], t_refs[g][1:parts], t_refs[g][parts:]
        if pieces == 1:
            pltpu.make_async_copy(t_own, t_all.at[g * size:(g + 1) * size], t_sem.at[g, 0]).start()
            continue
        t_copy(t_own, g, blocks[0], 0).start()
        for s in range(1, parts):
            @pl.when(own[0] >= s)
            def _():
                t_copy(t_right[s - 1], g, blocks[s], s).start()

            @pl.when(own[0] < s)
            def _():
                t_copy(t_left[parts - s - 1], g, blocks[s], s).start()
    w_copy(0, 0).start()
    ladder_copy = pltpu.make_async_copy(ladder_hbm, ladder, l_sem)
    for g in range(groups):
        if pieces == 1:
            pltpu.make_async_copy(t_refs[g][0], t_all.at[g * size:(g + 1) * size], t_sem.at[g, 0]).wait()
            continue
        for s in range(parts):
            t_copy(t_refs[g][0], g, blocks[s], s).wait()

    @pl.loop(0, parts)
    def _(step):
        slot = lax.rem(step, 2)
        w_copy(0, slot).wait()
        for s in range(1, parts):
            @pl.when(step + 1 == s)
            def _():
                w_copy(s, s % 2).start()

        @pl.when(step == parts - 1)
        def _():
            ladder_copy.start()

        j0 = lax.rem(own[0] - step + parts, parts) * per_part
        for tile in range(per_part // wide):
            acc = jnp.dot(
                t_all[...], w_buf[slot, :, tile * WIDE:(tile + 1) * WIDE], preferred_element_type=jnp.float32)
            for i in range(occupied):
                for k in range(wide):
                    n = j0 + (i * occupied + tile * wide + k)
                    for g in range(groups):
                        for h in range(0, GROUP, 8):
                            row = g * size + i * GROUP + h
                            pairs[pl.ds((g * GROUP + h) * pitch + n, 8, stride=pitch), :] = (
                                acc[row:row + 8, k * b_local:(k + 1) * b_local])

    ladder_copy.wait()
    steps = groups * GROUP // STEP_A

    def out_copy(step, slot):
        rows = pl.ds(q * GROUP + step * STEP_A, STEP_A)
        return pltpu.make_async_copy(out_buf.at[slot], out_ref.at[rows], out_sem.at[slot])

    @pl.loop(0, steps)
    def _(step):
        slot = lax.rem(step, 2)

        @pl.when(step >= 2)
        def _():
            out_copy(step - 2, slot).wait()

        for g in range(STEP_A // wide):
            blocks = []
            for k in range(wide):
                row = pl.multiple_of((step * STEP_A + g * wide + k) * pitch, 8)
                blocks.append(pairs[pl.ds(row, count), :].astype(jnp.bfloat16))
            both = jnp.concatenate(blocks, axis=1)
            for m in range(count // 256):
                rows = slice(m * 256, (m + 1) * 256)
                mixed = jnp.dot(ladder[rows, :], both, preferred_element_type=jnp.float32)
                total = (mixed + both[rows, :].astype(jnp.float32)).astype(jnp.bfloat16)
                out_buf[slot, g * wide:(g + 1) * wide, :, rows] = total.T.reshape(wide, b_local, 256)
        out_copy(step, slot).start()

    for step in range(max(steps - 2, 0), steps):
        out_copy(step, step % 2).wait()


def chunk_update(own, chunks, panel_w, ladder, out, q, a_local, b_local, occupied):
    groups = len(chunks)
    rows = groups * GROUP * occupied
    count = occupied * occupied
    k_all, width = panel_w[0].shape
    parts = 1 + panel_w[1].shape[1] // width
    args = [*[piece for pieces in chunks for piece in pieces], *panel_w, ladder]
    aliases = {}
    if out is not None:
        aliases = {len(args) + 1: 0}
        args.append(out)
    flops = 2 * rows * k_all * occupied * b_local + 2 * groups * GROUP * b_local * count * count
    size = parts * k_all * width + count * count + rows * k_all + groups * GROUP * b_local * count
    return pl.pallas_call(
        functools.partial(
            chunk_kernel, groups=groups, pieces=len(chunks[0]), parts=parts, occupied=occupied, b_local=b_local, q=q),
        out_shape=jax.ShapeDtypeStruct((a_local, b_local, count), jnp.bfloat16),
        in_specs=[pl.BlockSpec(memory_space=pltpu.SMEM)] + [ANY] * len(args),
        out_specs=ANY,
        scratch_shapes=[
            pltpu.VMEM((rows, k_all), jnp.bfloat16),
            pltpu.VMEM((2, k_all, width), jnp.bfloat16),
            pltpu.VMEM((count, count), jnp.bfloat16),
            pltpu.VMEM((groups * GROUP * (count + PAD), b_local), jnp.float32),
            pltpu.VMEM((2, STEP_A, b_local, count), jnp.bfloat16),
            pltpu.SemaphoreType.DMA((groups, parts)),
            pltpu.SemaphoreType.DMA((2,)),
            pltpu.SemaphoreType.DMA,
            pltpu.SemaphoreType.DMA((2,)),
        ],
        input_output_aliases=aliases,
        compiler_params=pltpu.CompilerParams(vmem_limit_bytes=60 * 1024 * 1024),
        cost_estimate=pl.CostEstimate(flops=flops, bytes_accessed=2 * size, transcendentals=0),
    )(own.reshape(1), *args)


def plain_update(own, pieces, panel_w, ladder, b_local, occupied):
    parts = (len(pieces) + 1) // 2
    back = jnp.argsort(lax.rem(own - jnp.arange(parts) + parts, parts))
    rows, depth = pieces[0].shape
    right, left = pieces[1:parts], pieces[parts:]
    by_shift = [pieces[0]] + [jnp.where(own >= s, right[s - 1], left[parts - s - 1]) for s in range(1, parts)]
    panel_t = jnp.transpose(jnp.stack(by_shift, 0)[back], (1, 0, 2)).reshape(rows, -1)
    cycle = jnp.dot(panel_t, jnp.concatenate(panel_w, axis=1), preferred_element_type=jnp.float32)
    cycle = cycle.astype(jnp.bfloat16).reshape(occupied, -1, parts, occupied // parts, b_local)[:, :, back]
    cycle = cycle.reshape(occupied, -1, occupied, b_local)
    a_count = cycle.shape[1]
    pairs = jnp.transpose(cycle, (1, 3, 0, 2)).reshape(a_count * b_local, occupied * occupied)
    mixed = lax.dot_general(pairs, ladder, (((1,), (1,)), ((), ())), preferred_element_type=jnp.float32)
    total = (mixed + pairs.astype(jnp.float32)).astype(jnp.bfloat16)
    return total.reshape(a_count, b_local, occupied * occupied)


def local(rows, cols, amplitudes, couplings, ladder):
    depth = amplitudes.shape[1]
    i_local = amplitudes.shape[0] // V
    j_local = couplings.shape[1] // V
    occupied = i_local * rows
    a_local, b_local = V // rows, V // cols
    own = lax.axis_index("col")

    chunks = a_local // GROUP
    blocks = amplitudes.reshape(i_local, rows, chunks, GROUP, depth)
    blocks, *arrived = cut(own, blocks, couplings, cols, j_local, b_local)
    for s in range(1, cols):
        arrived[s] = lax.ppermute(arrived[s], "col", [(c, (c + s) % cols) for c in range(cols)])
    blocks = lax.all_to_all(blocks, "row", split_axis=0, concat_axis=0, tiled=True)

    rest, _ = lax.optimization_barrier((arrived[1:], blocks))
    panel_w = [
        lax.all_gather(part, "row", axis=0, tiled=True) for part in (arrived[0], jnp.concatenate(rest, axis=1))
    ]

    per_part = occupied // cols
    plain = (b_local % 128 or WIDE % b_local or depth % 128 or cols < 4
             or per_part * b_local % WIDE or chunks < 4 or chunks % 2)

    def flat(sides):
        right, left = sides
        return [right[0], *right[1:], *left[1:]]

    def hop(sides, s, direct=False):
        right, left = sides
        first = 0 if direct else s - 1
        step = s if direct else 1
        source = 0 if direct else -1
        right.append(lax.ppermute(right[source], "col", [(c, c + step) for c in range(first, cols - step)]))
        left.append(lax.ppermute(left[source], "col", [(c + step, c) for c in range(cols - step - first)]))

    pieces = []
    for q in range(chunks):
        held = blocks[:, q].reshape(occupied * GROUP, depth)
        pieces.append(([held], [held]))

    if plain:
        for sides in pieces:
            for s in range(1, cols):
                hop(sides, s)
        return jnp.concatenate(
            [plain_update(own, flat(sides), panel_w, ladder, b_local, occupied) for sides in pieces], axis=0)

    def after(done, sides):
        right, left = sides
        done, right[0], left[0] = lax.optimization_barrier((done, right[0], left[0]))
        return done

    *early, x, y = pieces
    for q in range(0, len(early), 2):
        if q:
            for before, sides in zip(early[q - 2:q], early[q:q + 2]):
                before[0][-2], before[1][-2] = after((before[0][-2], before[1][-2]), sides)
        for s in range(1, cols):
            for sides in early[q:q + 2]:
                hop(sides, s)
    ends = early[0]
    ends[0][-1], ends[1][-1] = after((ends[0][-1], ends[1][-1]), x)
    for s in range(1, cols - 1):
        hop(x, s)
    x[0][1], x[1][1] = after((x[0][1], x[1][1]), x)
    hop(x, cols - 1, direct=True)
    x[0][1], x[1][1] = after((x[0][1], x[1][1]), y)
    last = lax.all_gather(y[0][0], "col", axis=1, tiled=True)

    update = functools.partial(chunk_update, own, a_local=a_local, b_local=b_local, occupied=occupied)
    out = None
    for q in range(0, len(early), 2):
        out = update([flat(sides) for sides in early[q:q + 2]], panel_w, ladder, out, q)
    out = update([flat(x)], panel_w, ladder, out, len(early))
    return update([[last]], panel_w, ladder, out, chunks - 1)


def solution(mesh):
    in_specs = (P("row", "col"), P("row", "col"), P())
    out_specs = P("row", "col", None)
    body = functools.partial(local, mesh.shape["row"], mesh.shape["col"])
    return jax.shard_map(body, mesh=mesh, in_specs=in_specs, out_specs=out_specs, check_vma=False)
```

```python
import functools

import jax
import jax.numpy as jnp
from jax import lax
from jax.experimental import pallas as pl
from jax.experimental.pallas import tpu as pltpu
from jax.sharding import PartitionSpec as P

V = 512
GROUP = 16
STEP_A = 4
PAD = 8
WIDE = 512
ANY = pl.BlockSpec(memory_space=pl.ANY)


def cut_kernel(own, t_ref, w_ref, t_out, *refs, j_local, b_local):
    w_outs, t_sem, w_sem = refs[:-2], refs[-2], refs[-1]
    cols = len(w_outs)
    for s in range(cols):
        to = lax.rem(own[0] + s, cols)
        for j in range(j_local):
            start = pl.multiple_of((j * cols + to) * b_local, b_local)
            pltpu.make_async_copy(
                w_ref.at[:, pl.ds(start, b_local)], w_outs[s].at[:, j * b_local:(j + 1) * b_local], w_sem.at[s]
            ).start()
    for i in range(t_ref.shape[0]):
        for r in range(t_ref.shape[1]):
            pltpu.make_async_copy(t_ref.at[i, r], t_out.at[r, :, i], t_sem).start()
    for s in range(cols):
        pltpu.make_async_copy(w_outs[s], w_outs[s], w_sem.at[s]).wait()
    pltpu.make_async_copy(t_out, t_out, t_sem).wait()


def cut(own, blocks, couplings, cols, j_local, b_local):
    i_local, rows, chunks, group, t_depth = blocks.shape
    depth = couplings.shape[0]
    if b_local % 128 or t_depth % 128:
        split = couplings.reshape(depth, j_local, cols, b_local)
        parts = [
            lax.dynamic_index_in_dim(split, lax.rem(own + s, cols), 2, keepdims=False).reshape(depth, -1)
            for s in range(cols)
        ]
        return [blocks.transpose(1, 2, 0, 3, 4), *parts]
    return pl.pallas_call(
        functools.partial(cut_kernel, j_local=j_local, b_local=b_local),
        out_shape=[jax.ShapeDtypeStruct((rows, chunks, i_local, group, t_depth), blocks.dtype)]
        + [jax.ShapeDtypeStruct((depth, j_local * b_local), couplings.dtype)] * cols,
        in_specs=[pl.BlockSpec(memory_space=pltpu.SMEM), ANY, ANY],
        out_specs=[pl.BlockSpec(memory_space=pltpu.VMEM)] * (1 + cols),
        scratch_shapes=[pltpu.SemaphoreType.DMA, pltpu.SemaphoreType.DMA((cols,))],
        compiler_params=pltpu.CompilerParams(vmem_limit_bytes=60 * 1024 * 1024),
        cost_estimate=pl.CostEstimate(flops=0, bytes_accessed=4 * (blocks.size + couplings.size), transcendentals=0),
    )(own.reshape(1), blocks, couplings)


def chunk_kernel(own, *refs, groups, pieces, parts, occupied, b_local, q):
    t_refs = [refs[g * pieces:(g + 1) * pieces] for g in range(groups)]
    w_own, w_rest, ladder_hbm = refs[groups * pieces:groups * pieces + 3]
    out_ref, t_all, w_buf, ladder, pairs, out_buf, t_sem, w_sem, l_sem, out_sem = refs[-10:]
    depth = t_all.shape[1] // parts
    width = w_own.shape[1]
    count = occupied * occupied
    pitch = count + PAD
    per_part = occupied // parts
    wide = WIDE // b_local

    size = GROUP * occupied

    def t_copy(src, g, block, s):
        cols = pl.ds(pl.multiple_of(block * depth, depth), depth)
        return pltpu.make_async_copy(src, t_all.at[g * size:(g + 1) * size, cols], t_sem.at[g, s])

    def w_copy(s, slot):
        src = w_rest.at[:, (s - 1) * width:s * width] if s else w_own
        return pltpu.make_async_copy(src, w_buf.at[slot], w_sem.at[slot])

    blocks = [lax.rem(own[0] - s + parts, parts) for s in range(parts)]
    for g in range(groups):
        t_own, t_right, t_left = t_refs[g][0], t_refs[g][1:parts], t_refs[g][parts:]
        if pieces == 1:
            pltpu.make_async_copy(t_own, t_all.at[g * size:(g + 1) * size], t_sem.at[g, 0]).start()
            continue
        t_copy(t_own, g, blocks[0], 0).start()
        for s in range(1, parts):
            @pl.when(own[0] >= s)
            def _():
                t_copy(t_right[s - 1], g, blocks[s], s).start()

            @pl.when(own[0] < s)
            def _():
                t_copy(t_left[parts - s - 1], g, blocks[s], s).start()
    w_copy(0, 0).start()
    ladder_copy = pltpu.make_async_copy(ladder_hbm, ladder, l_sem)
    for g in range(groups):
        if pieces == 1:
            pltpu.make_async_copy(t_refs[g][0], t_all.at[g * size:(g + 1) * size], t_sem.at[g, 0]).wait()
            continue
        for s in range(parts):
            t_copy(t_refs[g][0], g, blocks[s], s).wait()

    @pl.loop(0, parts)
    def _(step):
        slot = lax.rem(step, 2)
        w_copy(0, slot).wait()
        for s in range(1, parts):
            @pl.when(step + 1 == s)
            def _():
                w_copy(s, s % 2).start()

        @pl.when(step == parts - 1)
        def _():
            ladder_copy.start()

        j0 = lax.rem(own[0] - step + parts, parts) * per_part
        for tile in range(per_part // wide):
            acc = jnp.dot(
                t_all[...], w_buf[slot, :, tile * WIDE:(tile + 1) * WIDE], preferred_element_type=jnp.float32)
            for i in range(occupied):
                for k in range(wide):
                    n = j0 + (i * occupied + tile * wide + k)
                    for g in range(groups):
                        for h in range(0, GROUP, 8):
                            row = g * size + i * GROUP + h
                            pairs[pl.ds((g * GROUP + h) * pitch + n, 8, stride=pitch), :] = (
                                acc[row:row + 8, k * b_local:(k + 1) * b_local])

    ladder_copy.wait()
    steps = groups * GROUP // STEP_A

    def out_copy(step, slot):
        rows = pl.ds(q * GROUP + step * STEP_A, STEP_A)
        return pltpu.make_async_copy(out_buf.at[slot], out_ref.at[rows], out_sem.at[slot])

    @pl.loop(0, steps)
    def _(step):
        slot = lax.rem(step, 2)

        @pl.when(step >= 2)
        def _():
            out_copy(step - 2, slot).wait()

        for g in range(STEP_A // wide):
            blocks = []
            for k in range(wide):
                row = pl.multiple_of((step * STEP_A + g * wide + k) * pitch, 8)
                blocks.append(pairs[pl.ds(row, count), :].astype(jnp.bfloat16))
            both = jnp.concatenate(blocks, axis=1)
            for m in range(count // 256):
                rows = slice(m * 256, (m + 1) * 256)
                mixed = jnp.dot(ladder[rows, :], both, preferred_element_type=jnp.float32)
                total = (mixed + both[rows, :].astype(jnp.float32)).astype(jnp.bfloat16)
                out_buf[slot, g * wide:(g + 1) * wide, :, rows] = total.T.reshape(wide, b_local, 256)
        out_copy(step, slot).start()

    for step in range(max(steps - 2, 0), steps):
        out_copy(step, step % 2).wait()


def chunk_update(own, chunks, panel_w, ladder, out, q, a_local, b_local, occupied):
    groups = len(chunks)
    rows = groups * GROUP * occupied
    count = occupied * occupied
    k_all, width = panel_w[0].shape
    parts = 1 + panel_w[1].shape[1] // width
    args = [*[piece for pieces in chunks for piece in pieces], *panel_w, ladder]
    aliases = {}
    if out is not None:
        aliases = {len(args) + 1: 0}
        args.append(out)
    flops = 2 * rows * k_all * occupied * b_local + 2 * groups * GROUP * b_local * count * count
    size = parts * k_all * width + count * count + rows * k_all + groups * GROUP * b_local * count
    return pl.pallas_call(
        functools.partial(
            chunk_kernel, groups=groups, pieces=len(chunks[0]), parts=parts, occupied=occupied, b_local=b_local, q=q),
        out_shape=jax.ShapeDtypeStruct((a_local, b_local, count), jnp.bfloat16),
        in_specs=[pl.BlockSpec(memory_space=pltpu.SMEM)] + [ANY] * len(args),
        out_specs=ANY,
        scratch_shapes=[
            pltpu.VMEM((rows, k_all), jnp.bfloat16),
            pltpu.VMEM((2, k_all, width), jnp.bfloat16),
            pltpu.VMEM((count, count), jnp.bfloat16),
            pltpu.VMEM((groups * GROUP * (count + PAD), b_local), jnp.float32),
            pltpu.VMEM((2, STEP_A, b_local, count), jnp.bfloat16),
            pltpu.SemaphoreType.DMA((groups, parts)),
            pltpu.SemaphoreType.DMA((2,)),
            pltpu.SemaphoreType.DMA,
            pltpu.SemaphoreType.DMA((2,)),
        ],
        input_output_aliases=aliases,
        compiler_params=pltpu.CompilerParams(vmem_limit_bytes=60 * 1024 * 1024),
        cost_estimate=pl.CostEstimate(flops=flops, bytes_accessed=2 * size, transcendentals=0),
    )(own.reshape(1), *args)


def plain_update(own, pieces, panel_w, ladder, b_local, occupied):
    parts = (len(pieces) + 1) // 2
    back = jnp.argsort(lax.rem(own - jnp.arange(parts) + parts, parts))
    rows, depth = pieces[0].shape
    right, left = pieces[1:parts], pieces[parts:]
    by_shift = [pieces[0]] + [jnp.where(own >= s, right[s - 1], left[parts - s - 1]) for s in range(1, parts)]
    panel_t = jnp.transpose(jnp.stack(by_shift, 0)[back], (1, 0, 2)).reshape(rows, -1)
    cycle = jnp.dot(panel_t, jnp.concatenate(panel_w, axis=1), preferred_element_type=jnp.float32)
    cycle = cycle.astype(jnp.bfloat16).reshape(occupied, -1, parts, occupied // parts, b_local)[:, :, back]
    cycle = cycle.reshape(occupied, -1, occupied, b_local)
    a_count = cycle.shape[1]
    pairs = jnp.transpose(cycle, (1, 3, 0, 2)).reshape(a_count * b_local, occupied * occupied)
    mixed = lax.dot_general(pairs, ladder, (((1,), (1,)), ((), ())), preferred_element_type=jnp.float32)
    total = (mixed + pairs.astype(jnp.float32)).astype(jnp.bfloat16)
    return total.reshape(a_count, b_local, occupied * occupied)


def local(rows, cols, amplitudes, couplings, ladder):
    depth = amplitudes.shape[1]
    i_local = amplitudes.shape[0] // V
    j_local = couplings.shape[1] // V
    occupied = i_local * rows
    a_local, b_local = V // rows, V // cols
    own = lax.axis_index("col")

    chunks = a_local // GROUP
    blocks = amplitudes.reshape(i_local, rows, chunks, GROUP, depth)
    blocks, *arrived = cut(own, blocks, couplings, cols, j_local, b_local)
    shifts = sorted(range(1, cols), key=lambda s: min(s, cols - s))
    for s in shifts:
        arrived[s] = lax.ppermute(arrived[s], "col", [(c, (c + s) % cols) for c in range(cols)])
    blocks = lax.all_to_all(blocks, "row", split_axis=0, concat_axis=0, tiled=True)

    *near, blocks = lax.optimization_barrier((*[arrived[s] for s in shifts[:-1]], blocks))
    for s, part in zip(shifts, near):
        arrived[s] = part

    def gather_w(rest):
        return [lax.all_gather(part, "row", axis=0, tiled=True) for part in (arrived[0], jnp.concatenate(rest, axis=1))]

    per_part = occupied // cols
    plain = (b_local % 128 or WIDE % b_local or depth % 128 or cols < 4
             or per_part * b_local % WIDE or chunks < 4 or chunks % 2)

    def flat(sides):
        right, left = sides
        return [right[0], *right[1:], *left[1:]]

    def hop(sides, s, direct=False):
        right, left = sides
        first = 0 if direct else s - 1
        step = s if direct else 1
        source = 0 if direct else -1
        right.append(lax.ppermute(right[source], "col", [(c, c + step) for c in range(first, cols - step)]))
        left.append(lax.ppermute(left[source], "col", [(c + step, c) for c in range(cols - step - first)]))

    pieces = []
    for q in range(chunks):
        held = blocks[:, q].reshape(occupied * GROUP, depth)
        pieces.append(([held], [held]))

    if plain:
        for sides in pieces:
            for s in range(1, cols):
                hop(sides, s)
        return jnp.concatenate(
            [plain_update(own, flat(sides), gather_w(arrived[1:]), ladder, b_local, occupied) for sides in pieces], axis=0)

    def after(done, sides):
        right, left = sides
        done, right[0], left[0] = lax.optimization_barrier((done, right[0], left[0]))
        return done

    *early, x, y = pieces
    for q in range(0, len(early), 2):
        if q:
            for before, sides in zip(early[q - 2:q], early[q:q + 2]):
                before[0][-2], before[1][-2] = after((before[0][-2], before[1][-2]), sides)
        for s in range(1, cols):
            for sides in early[q:q + 2]:
                hop(sides, s)
            if q == 0 and s == 1:
                right, left = early[0]
                rest, right[1], left[1] = lax.optimization_barrier((arrived[1:], right[1], left[1]))
                panel_w = gather_w(rest)
    right, left = early[-1]
    right[-2], left[-2] = after((right[-2], left[-2]), x)
    for s in range(1, cols):
        hop(x, s)
    x[0][1], x[1][1] = after((x[0][1], x[1][1]), y)
    last = lax.all_gather(y[0][0], "col", axis=1, tiled=True)

    update = functools.partial(chunk_update, own, a_local=a_local, b_local=b_local, occupied=occupied)
    out = None
    for q in range(0, len(early), 2):
        out = update([flat(sides) for sides in early[q:q + 2]], panel_w, ladder, out, q)
    out = update([flat(x)], panel_w, ladder, out, len(early))
    return update([[last]], panel_w, ladder, out, chunks - 1)


def solution(mesh):
    in_specs = (P("row", "col"), P("row", "col"), P())
    out_specs = P("row", "col", None)
    body = functools.partial(local, mesh.shape["row"], mesh.shape["col"])
    return jax.shard_map(body, mesh=mesh, in_specs=in_specs, out_specs=out_specs, check_vma=False)
```

```python
import functools

import jax
import jax.numpy as jnp
from jax import lax
from jax.experimental import pallas as pl
from jax.experimental.pallas import tpu as pltpu
from jax.sharding import PartitionSpec as P

V = 512
GROUP = 16
STEP_A = 4
PAD = 8
WIDE = 512
ANY = pl.BlockSpec(memory_space=pl.ANY)


def cut_kernel(own, t_ref, w_ref, t_out, *refs, j_local, b_local):
    w_outs, t_sem, w_sem = refs[:-2], refs[-2], refs[-1]
    cols = len(w_outs)
    for s in range(cols):
        to = lax.rem(own[0] + s, cols)
        for j in range(j_local):
            start = pl.multiple_of((j * cols + to) * b_local, b_local)
            pltpu.make_async_copy(
                w_ref.at[:, pl.ds(start, b_local)], w_outs[s].at[:, j * b_local:(j + 1) * b_local], w_sem.at[s]
            ).start()
    for i in range(t_ref.shape[0]):
        for r in range(t_ref.shape[1]):
            pltpu.make_async_copy(t_ref.at[i, r], t_out.at[r, :, i], t_sem).start()
    for s in range(cols):
        pltpu.make_async_copy(w_outs[s], w_outs[s], w_sem.at[s]).wait()
    pltpu.make_async_copy(t_out, t_out, t_sem).wait()


def cut(own, blocks, couplings, cols, j_local, b_local):
    i_local, rows, chunks, group, t_depth = blocks.shape
    depth = couplings.shape[0]
    if b_local % 128 or t_depth % 128:
        split = couplings.reshape(depth, j_local, cols, b_local)
        parts = [
            lax.dynamic_index_in_dim(split, lax.rem(own + s, cols), 2, keepdims=False).reshape(depth, -1)
            for s in range(cols)
        ]
        return [blocks.transpose(1, 2, 0, 3, 4), *parts]
    return pl.pallas_call(
        functools.partial(cut_kernel, j_local=j_local, b_local=b_local),
        out_shape=[jax.ShapeDtypeStruct((rows, chunks, i_local, group, t_depth), blocks.dtype)]
        + [jax.ShapeDtypeStruct((depth, j_local * b_local), couplings.dtype)] * cols,
        in_specs=[pl.BlockSpec(memory_space=pltpu.SMEM), ANY, ANY],
        out_specs=[pl.BlockSpec(memory_space=pltpu.VMEM)] * (1 + cols),
        scratch_shapes=[pltpu.SemaphoreType.DMA, pltpu.SemaphoreType.DMA((cols,))],
        compiler_params=pltpu.CompilerParams(vmem_limit_bytes=60 * 1024 * 1024),
        cost_estimate=pl.CostEstimate(flops=0, bytes_accessed=4 * (blocks.size + couplings.size), transcendentals=0),
    )(own.reshape(1), blocks, couplings)


def chunk_kernel(own, *refs, starts, parts, occupied, b_local, q):
    t_refs = [ref.at[pl.ds(start, GROUP * occupied)] for ref, start in zip(refs, starts)]
    t_own, t_right, t_left = t_refs[0], t_refs[1:parts], t_refs[parts:]
    w_own, w_rest, ladder_hbm = refs[2 * parts - 1:2 * parts + 2]
    out_ref, t_all, w_buf, ladder, pairs, out_buf, t_sem, w_sem, l_sem, out_sem = refs[-10:]
    depth = t_own.shape[1]
    width = w_own.shape[1]
    count = occupied * occupied
    pitch = count + PAD
    per_part = occupied // parts
    wide = WIDE // b_local

    def t_copy(src, block, s):
        cols = pl.ds(pl.multiple_of(block * depth, depth), depth)
        return pltpu.make_async_copy(src, t_all.at[:, cols], t_sem.at[s])

    def w_copy(s, slot):
        src = w_rest.at[:, (s - 1) * width:s * width] if s else w_own
        return pltpu.make_async_copy(src, w_buf.at[slot], w_sem.at[slot])

    blocks = [lax.rem(own[0] - s + parts, parts) for s in range(parts)]
    t_copy(t_own, blocks[0], 0).start()
    for s in range(1, parts):
        @pl.when(own[0] >= s)
        def _():
            t_copy(t_right[s - 1], blocks[s], s).start()

        @pl.when(own[0] < s)
        def _():
            t_copy(t_left[parts - s - 1], blocks[s], s).start()
    w_copy(0, 0).start()
    ladder_copy = pltpu.make_async_copy(ladder_hbm, ladder, l_sem)
    for s in range(parts):
        t_copy(t_own, blocks[s], s).wait()

    @pl.loop(0, parts)
    def _(step):
        slot = lax.rem(step, 2)
        w_copy(0, slot).wait()
        for s in range(1, parts):
            @pl.when(step + 1 == s)
            def _():
                w_copy(s, s % 2).start()

        @pl.when(step == parts - 1)
        def _():
            ladder_copy.start()

        j0 = lax.rem(own[0] - step + parts, parts) * per_part
        for tile in range(per_part // wide):
            acc = jnp.dot(
                t_all[...], w_buf[slot, :, tile * WIDE:(tile + 1) * WIDE], preferred_element_type=jnp.float32)
            for i in range(occupied):
                for k in range(wide):
                    n = j0 + (i * occupied + tile * wide + k)
                    for h in range(GROUP // 8):
                        row = i * GROUP + h * 8
                        pairs[pl.ds(h * 8 * pitch + n, 8, stride=pitch), :] = (
                            acc[row:row + 8, k * b_local:(k + 1) * b_local])

    ladder_copy.wait()
    steps = GROUP // STEP_A

    def out_copy(step, slot):
        rows = pl.ds(q * GROUP + step * STEP_A, STEP_A)
        return pltpu.make_async_copy(out_buf.at[slot], out_ref.at[rows], out_sem.at[slot])

    @pl.loop(0, steps)
    def _(step):
        slot = lax.rem(step, 2)

        @pl.when(step >= 2)
        def _():
            out_copy(step - 2, slot).wait()

        for g in range(STEP_A // wide):
            blocks = []
            for k in range(wide):
                row = pl.multiple_of((step * STEP_A + g * wide + k) * pitch, 8)
                blocks.append(pairs[pl.ds(row, count), :].astype(jnp.bfloat16))
            both = jnp.concatenate(blocks, axis=1)
            for m in range(count // 256):
                rows = slice(m * 256, (m + 1) * 256)
                mixed = jnp.dot(ladder[rows, :], both, preferred_element_type=jnp.float32)
                total = (mixed + both[rows, :].astype(jnp.float32)).astype(jnp.bfloat16)
                out_buf[slot, g * wide:(g + 1) * wide, :, rows] = total.T.reshape(wide, b_local, 256)
        out_copy(step, slot).start()

    for step in range(max(steps - 2, 0), steps):
        out_copy(step, step % 2).wait()


def chunk_update(own, pieces, panel_w, ladder, out, after, q, a_local, b_local, occupied):
    arrays, starts = zip(*pieces)
    rows = GROUP * occupied
    count = occupied * occupied
    k_all, width = panel_w[0].shape
    parts = 1 + panel_w[1].shape[1] // width
    args = [*arrays, *panel_w, ladder, *after]
    aliases = {}
    if out is not None:
        aliases = {len(args) + 1: 0}
        args.append(out)
    flops = 2 * rows * k_all * occupied * b_local + 2 * GROUP * b_local * count * count
    size = parts * k_all * width + count * count + rows * k_all + GROUP * b_local * count
    return pl.pallas_call(
        functools.partial(chunk_kernel, starts=starts, parts=parts, occupied=occupied, b_local=b_local, q=q),
        out_shape=jax.ShapeDtypeStruct((a_local, b_local, count), jnp.bfloat16),
        in_specs=[pl.BlockSpec(memory_space=pltpu.SMEM)] + [ANY] * len(args),
        out_specs=ANY,
        scratch_shapes=[
            pltpu.VMEM((rows, k_all), jnp.bfloat16),
            pltpu.VMEM((2, k_all, width), jnp.bfloat16),
            pltpu.VMEM((count, count), jnp.bfloat16),
            pltpu.VMEM((GROUP * (count + PAD), b_local), jnp.float32),
            pltpu.VMEM((2, STEP_A, b_local, count), jnp.bfloat16),
            pltpu.SemaphoreType.DMA((parts,)),
            pltpu.SemaphoreType.DMA((2,)),
            pltpu.SemaphoreType.DMA,
            pltpu.SemaphoreType.DMA((2,)),
        ],
        input_output_aliases=aliases,
        compiler_params=pltpu.CompilerParams(vmem_limit_bytes=60 * 1024 * 1024),
        cost_estimate=pl.CostEstimate(flops=flops, bytes_accessed=2 * size, transcendentals=0),
    )(own.reshape(1), *args)


def plain_update(own, pieces, panel_w, ladder, b_local, occupied):
    parts = (len(pieces) + 1) // 2
    back = jnp.argsort(lax.rem(own - jnp.arange(parts) + parts, parts))
    rows, depth = pieces[0].shape
    right, left = pieces[1:parts], pieces[parts:]
    by_shift = [pieces[0]] + [jnp.where(own >= s, right[s - 1], left[parts - s - 1]) for s in range(1, parts)]
    panel_t = jnp.transpose(jnp.stack(by_shift, 0)[back], (1, 0, 2)).reshape(rows, -1)
    cycle = jnp.dot(panel_t, jnp.concatenate(panel_w, axis=1), preferred_element_type=jnp.float32)
    cycle = cycle.astype(jnp.bfloat16).reshape(occupied, -1, parts, occupied // parts, b_local)[:, :, back]
    cycle = cycle.reshape(occupied, -1, occupied, b_local)
    a_count = cycle.shape[1]
    pairs = jnp.transpose(cycle, (1, 3, 0, 2)).reshape(a_count * b_local, occupied * occupied)
    mixed = lax.dot_general(pairs, ladder, (((1,), (1,)), ((), ())), preferred_element_type=jnp.float32)
    total = (mixed + pairs.astype(jnp.float32)).astype(jnp.bfloat16)
    return total.reshape(a_count, b_local, occupied * occupied)


def local(rows, cols, amplitudes, couplings, ladder):
    depth = amplitudes.shape[1]
    i_local = amplitudes.shape[0] // V
    j_local = couplings.shape[1] // V
    occupied = i_local * rows
    a_local, b_local = V // rows, V // cols
    own = lax.axis_index("col")

    chunks = a_local // GROUP
    blocks = amplitudes.reshape(i_local, rows, chunks, GROUP, depth)
    blocks, *arrived = cut(own, blocks, couplings, cols, j_local, b_local)
    for s in range(1, cols):
        arrived[s] = lax.ppermute(arrived[s], "col", [(c, (c + s) % cols) for c in range(cols)])
    blocks = lax.all_to_all(blocks, "row", split_axis=0, concat_axis=0, tiled=True)

    rest, _ = lax.optimization_barrier((arrived[1:], blocks))
    panel_w = [
        lax.all_gather(part, "row", axis=0, tiled=True) for part in (arrived[0], jnp.concatenate(rest, axis=1))
    ]

    per_part = occupied // cols
    plain = (b_local % 128 or WIDE % b_local or depth % 128 or cols < 4
             or per_part * b_local % WIDE or chunks < 4 or chunks % 2)

    def flat(sides):
        right, left = sides
        return [right[0], *right[1:], *left[1:]]

    def update(q, out, after):
        blocks = [piece if isinstance(piece, tuple) else (piece, 0) for piece in flat(pieces[q])]
        return chunk_update(own, blocks, panel_w, ladder, out, after, q, a_local, b_local, occupied)

    def hop(sides, s, direct=False):
        right, left = sides
        first = 0 if direct else s - 1
        step = s if direct else 1
        source = 0 if direct else -1
        right.append(lax.ppermute(right[source], "col", [(c, c + step) for c in range(first, cols - step)]))
        left.append(lax.ppermute(left[source], "col", [(c + step, c) for c in range(cols - step - first)]))

    pieces = []
    for q in range(chunks):
        held = blocks[:, q].reshape(occupied * GROUP, depth)
        pieces.append(([held], [held]))

    if plain:
        for sides in pieces:
            for s in range(1, cols):
                hop(sides, s)
        return jnp.concatenate(
            [plain_update(own, flat(sides), panel_w, ladder, b_local, occupied) for sides in pieces], axis=0)

    def after(done, sides):
        right, left = sides
        done, right[0], left[0] = lax.optimization_barrier((done, right[0], left[0]))
        return done

    *early, x, y = pieces
    for q in range(0, len(early), 2):
        if q:
            for before, sides in zip(early[q - 2:q], early[q:q + 2]):
                before[0][-2], before[1][-2] = after((before[0][-2], before[1][-2]), sides)
        for s in range(1, cols):
            for sides in early[q:q + 2]:
                hop(sides, s)
    before = early[-2]
    before[0][-2], before[1][-2] = after((before[0][-2], before[1][-2]), x)
    for s in range(1, cols - 1):
        hop(x, s)
    far = (jnp.concatenate([x[0][0], y[0][0]]),) * 2
    far = ([far[0]], [far[1]])
    size = x[0][0].shape[0]
    out = update(0, None, (x[0][1], x[1][1]))
    moving = (early[-1][0], early[-1][1], x[0], x[1])
    out, *ends = after((out, *[side[-1] for side in moving]), far)
    for side, end in zip(moving, ends):
        side[-1] = end
    out = after(out, y)
    hop(y, 1)
    hop(far, cols - 1, direct=True)
    for n in (0, 1):
        x[n].append((far[n][1], 0))
    out = update(1, out, ())
    out, y[0][-1], y[1][-1] = lax.optimization_barrier((out, y[0][-1], y[1][-1]))
    for s in range(2, cols - 1):
        hop(y, s)
    for n in (0, 1):
        y[n].append((far[n][1], size))
    for q in range(2, chunks):
        out = update(q, out, ())
    return out


def solution(mesh):
    in_specs = (P("row", "col"), P("row", "col"), P())
    out_specs = P("row", "col", None)
    body = functools.partial(local, mesh.shape["row"], mesh.shape["col"])
    return jax.shard_map(body, mesh=mesh, in_specs=in_specs, out_specs=out_specs, check_vma=False)
```

```python
import functools

import jax
import jax.numpy as jnp
from jax import lax
from jax.experimental import pallas as pl
from jax.experimental.pallas import tpu as pltpu
from jax.sharding import PartitionSpec as P

V = 512
GROUP = 16
STEP_A = 4
PAD = 8
WIDE = 512
ANY = pl.BlockSpec(memory_space=pl.ANY)


def cut_kernel(own, t_ref, w_ref, t_out, *refs, j_local, b_local):
    w_outs, t_sem, w_sem = refs[:-2], refs[-2], refs[-1]
    cols = len(w_outs)
    for s in range(cols):
        to = lax.rem(own[0] + s, cols)
        for j in range(j_local):
            start = pl.multiple_of((j * cols + to) * b_local, b_local)
            pltpu.make_async_copy(
                w_ref.at[:, pl.ds(start, b_local)], w_outs[s].at[:, j * b_local:(j + 1) * b_local], w_sem.at[s]
            ).start()
    for i in range(t_ref.shape[0]):
        for r in range(t_ref.shape[1]):
            pltpu.make_async_copy(t_ref.at[i, r], t_out.at[r, :, i], t_sem).start()
    for s in range(cols):
        pltpu.make_async_copy(w_outs[s], w_outs[s], w_sem.at[s]).wait()
    pltpu.make_async_copy(t_out, t_out, t_sem).wait()


def cut(own, blocks, couplings, cols, j_local, b_local):
    i_local, rows, chunks, group, t_depth = blocks.shape
    depth = couplings.shape[0]
    if b_local % 128 or t_depth % 128:
        split = couplings.reshape(depth, j_local, cols, b_local)
        parts = [
            lax.dynamic_index_in_dim(split, lax.rem(own + s, cols), 2, keepdims=False).reshape(depth, -1)
            for s in range(cols)
        ]
        return [blocks.transpose(1, 2, 0, 3, 4), *parts]
    return pl.pallas_call(
        functools.partial(cut_kernel, j_local=j_local, b_local=b_local),
        out_shape=[jax.ShapeDtypeStruct((rows, chunks, i_local, group, t_depth), blocks.dtype)]
        + [jax.ShapeDtypeStruct((depth, j_local * b_local), couplings.dtype)] * cols,
        in_specs=[pl.BlockSpec(memory_space=pltpu.SMEM), ANY, ANY],
        out_specs=[pl.BlockSpec(memory_space=pltpu.VMEM)] * (1 + cols),
        scratch_shapes=[pltpu.SemaphoreType.DMA, pltpu.SemaphoreType.DMA((cols,))],
        compiler_params=pltpu.CompilerParams(vmem_limit_bytes=60 * 1024 * 1024),
        cost_estimate=pl.CostEstimate(flops=0, bytes_accessed=4 * (blocks.size + couplings.size), transcendentals=0),
    )(own.reshape(1), blocks, couplings)


def chunk_kernel(own, *refs, starts, parts, occupied, b_local, q):
    t_refs = [ref.at[pl.ds(start, GROUP * occupied)] for ref, start in zip(refs, starts)]
    t_own, t_right, t_left = t_refs[0], t_refs[1:parts], t_refs[parts:]
    w_own, w_rest, ladder_hbm = refs[2 * parts - 1:2 * parts + 2]
    out_ref, t_all, w_buf, ladder, pairs, out_buf, t_sem, w_sem, l_sem, out_sem = refs[-10:]
    depth = t_own.shape[1]
    width = w_own.shape[1]
    count = occupied * occupied
    pitch = count + PAD
    per_part = occupied // parts
    wide = WIDE // b_local

    def t_copy(src, block, s):
        cols = pl.ds(pl.multiple_of(block * depth, depth), depth)
        return pltpu.make_async_copy(src, t_all.at[:, cols], t_sem.at[s])

    def w_copy(s, slot):
        src = w_rest.at[:, (s - 1) * width:s * width] if s else w_own
        return pltpu.make_async_copy(src, w_buf.at[slot], w_sem.at[slot])

    blocks = [lax.rem(own[0] - s + parts, parts) for s in range(parts)]
    t_copy(t_own, blocks[0], 0).start()
    for s in range(1, parts):
        @pl.when(own[0] >= s)
        def _():
            t_copy(t_right[s - 1], blocks[s], s).start()

        @pl.when(own[0] < s)
        def _():
            t_copy(t_left[parts - s - 1], blocks[s], s).start()
    w_copy(0, 0).start()
    ladder_copy = pltpu.make_async_copy(ladder_hbm, ladder, l_sem)
    for s in range(parts):
        t_copy(t_own, blocks[s], s).wait()

    @pl.loop(0, parts)
    def _(step):
        slot = lax.rem(step, 2)
        w_copy(0, slot).wait()
        for s in range(1, parts):
            @pl.when(step + 1 == s)
            def _():
                w_copy(s, s % 2).start()

        @pl.when(step == parts - 1)
        def _():
            ladder_copy.start()

        j0 = lax.rem(own[0] - step + parts, parts) * per_part
        for tile in range(per_part // wide):
            acc = jnp.dot(
                t_all[...], w_buf[slot, :, tile * WIDE:(tile + 1) * WIDE], preferred_element_type=jnp.float32)
            for i in range(occupied):
                for k in range(wide):
                    n = j0 + (i * occupied + tile * wide + k)
                    for h in range(GROUP // 8):
                        row = i * GROUP + h * 8
                        pairs[pl.ds(h * 8 * pitch + n, 8, stride=pitch), :] = (
                            acc[row:row + 8, k * b_local:(k + 1) * b_local])

    ladder_copy.wait()
    steps = GROUP // STEP_A

    def out_copy(step, slot):
        rows = pl.ds(q * GROUP + step * STEP_A, STEP_A)
        return pltpu.make_async_copy(out_buf.at[slot], out_ref.at[rows], out_sem.at[slot])

    @pl.loop(0, steps)
    def _(step):
        slot = lax.rem(step, 2)

        @pl.when(step >= 2)
        def _():
            out_copy(step - 2, slot).wait()

        for g in range(STEP_A // wide):
            blocks = []
            for k in range(wide):
                row = pl.multiple_of((step * STEP_A + g * wide + k) * pitch, 8)
                blocks.append(pairs[pl.ds(row, count), :].astype(jnp.bfloat16))
            both = jnp.concatenate(blocks, axis=1)
            for m in range(count // 256):
                rows = slice(m * 256, (m + 1) * 256)
                mixed = jnp.dot(ladder[rows, :], both, preferred_element_type=jnp.float32)
                total = (mixed + both[rows, :].astype(jnp.float32)).astype(jnp.bfloat16)
                out_buf[slot, g * wide:(g + 1) * wide, :, rows] = total.T.reshape(wide, b_local, 256)
        out_copy(step, slot).start()

    for step in range(max(steps - 2, 0), steps):
        out_copy(step, step % 2).wait()


def chunk_update(own, pieces, panel_w, ladder, out, after, q, a_local, b_local, occupied):
    arrays, starts = zip(*pieces)
    rows = GROUP * occupied
    count = occupied * occupied
    k_all, width = panel_w[0].shape
    parts = 1 + panel_w[1].shape[1] // width
    args = [*arrays, *panel_w, ladder, *after]
    aliases = {}
    if out is not None:
        aliases = {len(args) + 1: 0}
        args.append(out)
    flops = 2 * rows * k_all * occupied * b_local + 2 * GROUP * b_local * count * count
    size = parts * k_all * width + count * count + rows * k_all + GROUP * b_local * count
    return pl.pallas_call(
        functools.partial(chunk_kernel, starts=starts, parts=parts, occupied=occupied, b_local=b_local, q=q),
        out_shape=jax.ShapeDtypeStruct((a_local, b_local, count), jnp.bfloat16),
        in_specs=[pl.BlockSpec(memory_space=pltpu.SMEM)] + [ANY] * len(args),
        out_specs=ANY,
        scratch_shapes=[
            pltpu.VMEM((rows, k_all), jnp.bfloat16),
            pltpu.VMEM((2, k_all, width), jnp.bfloat16),
            pltpu.VMEM((count, count), jnp.bfloat16),
            pltpu.VMEM((GROUP * (count + PAD), b_local), jnp.float32),
            pltpu.VMEM((2, STEP_A, b_local, count), jnp.bfloat16),
            pltpu.SemaphoreType.DMA((parts,)),
            pltpu.SemaphoreType.DMA((2,)),
            pltpu.SemaphoreType.DMA,
            pltpu.SemaphoreType.DMA((2,)),
        ],
        input_output_aliases=aliases,
        compiler_params=pltpu.CompilerParams(vmem_limit_bytes=60 * 1024 * 1024),
        cost_estimate=pl.CostEstimate(flops=flops, bytes_accessed=2 * size, transcendentals=0),
    )(own.reshape(1), *args)


def plain_update(own, pieces, panel_w, ladder, b_local, occupied):
    parts = (len(pieces) + 1) // 2
    back = jnp.argsort(lax.rem(own - jnp.arange(parts) + parts, parts))
    rows, depth = pieces[0].shape
    right, left = pieces[1:parts], pieces[parts:]
    by_shift = [pieces[0]] + [jnp.where(own >= s, right[s - 1], left[parts - s - 1]) for s in range(1, parts)]
    panel_t = jnp.transpose(jnp.stack(by_shift, 0)[back], (1, 0, 2)).reshape(rows, -1)
    cycle = jnp.dot(panel_t, jnp.concatenate(panel_w, axis=1), preferred_element_type=jnp.float32)
    cycle = cycle.astype(jnp.bfloat16).reshape(occupied, -1, parts, occupied // parts, b_local)[:, :, back]
    cycle = cycle.reshape(occupied, -1, occupied, b_local)
    a_count = cycle.shape[1]
    pairs = jnp.transpose(cycle, (1, 3, 0, 2)).reshape(a_count * b_local, occupied * occupied)
    mixed = lax.dot_general(pairs, ladder, (((1,), (1,)), ((), ())), preferred_element_type=jnp.float32)
    total = (mixed + pairs.astype(jnp.float32)).astype(jnp.bfloat16)
    return total.reshape(a_count, b_local, occupied * occupied)


def local(rows, cols, amplitudes, couplings, ladder):
    depth = amplitudes.shape[1]
    i_local = amplitudes.shape[0] // V
    j_local = couplings.shape[1] // V
    occupied = i_local * rows
    a_local, b_local = V // rows, V // cols
    own = lax.axis_index("col")

    chunks = a_local // GROUP
    blocks = amplitudes.reshape(i_local, rows, chunks, GROUP, depth)
    blocks, *arrived = cut(own, blocks, couplings, cols, j_local, b_local)
    for s in range(1, cols):
        arrived[s] = lax.ppermute(arrived[s], "col", [(c, (c + s) % cols) for c in range(cols)])
    blocks = lax.all_to_all(blocks, "row", split_axis=0, concat_axis=0, tiled=True)

    rest, _ = lax.optimization_barrier((arrived[1:], blocks))
    panel_w = [
        lax.all_gather(part, "row", axis=0, tiled=True) for part in (arrived[0], jnp.concatenate(rest, axis=1))
    ]

    per_part = occupied // cols
    plain = (b_local % 128 or WIDE % b_local or depth % 128 or cols < 4
             or per_part * b_local % WIDE or chunks < 4 or chunks % 2)

    def flat(sides):
        right, left = sides
        return [right[0], *right[1:], *left[1:]]

    def update(q, out, after):
        blocks = [(piece, 0) for piece in flat(pieces[q])]
        return chunk_update(own, blocks, panel_w, ladder, out, after, q, a_local, b_local, occupied)

    def hop(sides, s, direct=False):
        right, left = sides
        first = 0 if direct else s - 1
        step = s if direct else 1
        source = 0 if direct else -1
        right.append(lax.ppermute(right[source], "col", [(c, c + step) for c in range(first, cols - step)]))
        left.append(lax.ppermute(left[source], "col", [(c + step, c) for c in range(cols - step - first)]))

    pieces = []
    for q in range(chunks):
        held = blocks[:, q].reshape(occupied * GROUP, depth)
        pieces.append(([held], [held]))

    if plain:
        for sides in pieces:
            for s in range(1, cols):
                hop(sides, s)
        return jnp.concatenate(
            [plain_update(own, flat(sides), panel_w, ladder, b_local, occupied) for sides in pieces], axis=0)

    def after(done, sides):
        right, left = sides
        done, right[0], left[0] = lax.optimization_barrier((done, right[0], left[0]))
        return done

    *early, x, y = pieces
    for q in range(0, len(early), 2):
        if q:
            for before, sides in zip(early[q - 2:q], early[q:q + 2]):
                before[0][-2], before[1][-2] = after((before[0][-2], before[1][-2]), sides)
        for s in range(1, cols):
            for sides in early[q:q + 2]:
                hop(sides, s)
    before = early[-2]
    before[0][-2], before[1][-2] = after((before[0][-2], before[1][-2]), x)
    for s in range(1, cols - 1):
        hop(x, s)
    out = update(0, None, (x[0][1], x[1][1]))
    moving = (early[-1][0], early[-1][1], x[0], x[1])
    out, *ends = after((out, *[side[-1] for side in moving]), x)
    for side, end in zip(moving, ends):
        side[-1] = end
    hop(x, cols - 1, direct=True)
    out = after(out, y)
    hop(y, 1)
    out = update(1, out, ())
    out, y[0][-1], y[1][-1], y[0][0], y[1][0] = lax.optimization_barrier(
        (out, y[0][-1], y[1][-1], y[0][0], y[1][0]))
    for s in range(2, cols - 1):
        hop(y, s)
    hop(y, cols - 1, direct=True)
    for q in range(2, chunks):
        out = update(q, out, ())
    return out


def solution(mesh):
    in_specs = (P("row", "col"), P("row", "col"), P())
    out_specs = P("row", "col", None)
    body = functools.partial(local, mesh.shape["row"], mesh.shape["col"])
    return jax.shard_map(body, mesh=mesh, in_specs=in_specs, out_specs=out_specs, check_vma=False)
```

```python
import functools

import jax
import jax.numpy as jnp
from jax import lax
from jax.experimental import pallas as pl
from jax.experimental.pallas import tpu as pltpu
from jax.sharding import PartitionSpec as P

V = 512
GROUP = 16
STEP_A = 4
PAD = 8
WIDE = 512
ANY = pl.BlockSpec(memory_space=pl.ANY)


def cut_kernel(own, t_ref, w_ref, t_out, *refs, j_local, b_local):
    w_outs, t_sem, w_sem = refs[:-2], refs[-2], refs[-1]
    cols = len(w_outs)
    for s in range(cols):
        to = lax.rem(own[0] + s, cols)
        for j in range(j_local):
            start = pl.multiple_of((j * cols + to) * b_local, b_local)
            pltpu.make_async_copy(
                w_ref.at[:, pl.ds(start, b_local)], w_outs[s].at[:, j * b_local:(j + 1) * b_local], w_sem.at[s]
            ).start()
    for i in range(t_ref.shape[0]):
        for r in range(t_ref.shape[1]):
            pltpu.make_async_copy(t_ref.at[i, r], t_out.at[r, :, i], t_sem).start()
    for s in range(cols):
        pltpu.make_async_copy(w_outs[s], w_outs[s], w_sem.at[s]).wait()
    pltpu.make_async_copy(t_out, t_out, t_sem).wait()


def cut(own, blocks, couplings, cols, j_local, b_local):
    i_local, rows, chunks, group, t_depth = blocks.shape
    depth = couplings.shape[0]
    if b_local % 128 or t_depth % 128:
        split = couplings.reshape(depth, j_local, cols, b_local)
        parts = [
            lax.dynamic_index_in_dim(split, lax.rem(own + s, cols), 2, keepdims=False).reshape(depth, -1)
            for s in range(cols)
        ]
        return [blocks.transpose(1, 2, 0, 3, 4), *parts]
    return pl.pallas_call(
        functools.partial(cut_kernel, j_local=j_local, b_local=b_local),
        out_shape=[jax.ShapeDtypeStruct((rows, chunks, i_local, group, t_depth), blocks.dtype)]
        + [jax.ShapeDtypeStruct((depth, j_local * b_local), couplings.dtype)] * cols,
        in_specs=[pl.BlockSpec(memory_space=pltpu.SMEM), ANY, ANY],
        out_specs=[pl.BlockSpec(memory_space=pltpu.VMEM)] * (1 + cols),
        scratch_shapes=[pltpu.SemaphoreType.DMA, pltpu.SemaphoreType.DMA((cols,))],
        compiler_params=pltpu.CompilerParams(vmem_limit_bytes=60 * 1024 * 1024),
        cost_estimate=pl.CostEstimate(flops=0, bytes_accessed=4 * (blocks.size + couplings.size), transcendentals=0),
    )(own.reshape(1), blocks, couplings)


def chunk_kernel(own, *refs, starts, parts, occupied, b_local, q):
    t_refs = [ref.at[pl.ds(start, GROUP * occupied)] for ref, start in zip(refs, starts)]
    t_own, t_right, t_left = t_refs[0], t_refs[1:parts], t_refs[parts:]
    w_own, w_rest, ladder_hbm = refs[2 * parts - 1:2 * parts + 2]
    out_ref, t_all, w_buf, ladder, pairs, out_buf, t_sem, w_sem, l_sem, out_sem = refs[-10:]
    depth = t_own.shape[1]
    width = w_own.shape[1]
    count = occupied * occupied
    pitch = count + PAD
    per_part = occupied // parts
    wide = WIDE // b_local

    def t_copy(src, block, s):
        cols = pl.ds(pl.multiple_of(block * depth, depth), depth)
        return pltpu.make_async_copy(src, t_all.at[:, cols], t_sem.at[s])

    def w_copy(s, slot):
        src = w_rest.at[:, (s - 1) * width:s * width] if s else w_own
        return pltpu.make_async_copy(src, w_buf.at[slot], w_sem.at[slot])

    blocks = [lax.rem(own[0] - s + parts, parts) for s in range(parts)]
    t_copy(t_own, blocks[0], 0).start()
    for s in range(1, parts):
        @pl.when(own[0] >= s)
        def _():
            t_copy(t_right[s - 1], blocks[s], s).start()

        @pl.when(own[0] < s)
        def _():
            t_copy(t_left[parts - s - 1], blocks[s], s).start()
    w_copy(0, 0).start()
    ladder_copy = pltpu.make_async_copy(ladder_hbm, ladder, l_sem)
    for s in range(parts):
        t_copy(t_own, blocks[s], s).wait()

    @pl.loop(0, parts)
    def _(step):
        slot = lax.rem(step, 2)
        w_copy(0, slot).wait()
        for s in range(1, parts):
            @pl.when(step + 1 == s)
            def _():
                w_copy(s, s % 2).start()

        @pl.when(step == parts - 1)
        def _():
            ladder_copy.start()

        j0 = lax.rem(own[0] - step + parts, parts) * per_part
        for tile in range(per_part // wide):
            acc = jnp.dot(
                t_all[...], w_buf[slot, :, tile * WIDE:(tile + 1) * WIDE], preferred_element_type=jnp.float32)
            for i in range(occupied):
                for k in range(wide):
                    n = j0 + (i * occupied + tile * wide + k)
                    for h in range(GROUP // 8):
                        row = i * GROUP + h * 8
                        pairs[pl.ds(h * 8 * pitch + n, 8, stride=pitch), :] = (
                            acc[row:row + 8, k * b_local:(k + 1) * b_local])

    ladder_copy.wait()
    steps = GROUP // STEP_A

    def out_copy(step, slot):
        rows = pl.ds(q * GROUP + step * STEP_A, STEP_A)
        return pltpu.make_async_copy(out_buf.at[slot], out_ref.at[rows], out_sem.at[slot])

    @pl.loop(0, steps)
    def _(step):
        slot = lax.rem(step, 2)

        @pl.when(step >= 2)
        def _():
            out_copy(step - 2, slot).wait()

        for g in range(STEP_A // wide):
            blocks = []
            for k in range(wide):
                row = pl.multiple_of((step * STEP_A + g * wide + k) * pitch, 8)
                blocks.append(pairs[pl.ds(row, count), :].astype(jnp.bfloat16))
            both = jnp.concatenate(blocks, axis=1)
            for m in range(count // 256):
                rows = slice(m * 256, (m + 1) * 256)
                mixed = jnp.dot(ladder[rows, :], both, preferred_element_type=jnp.float32)
                total = (mixed + both[rows, :].astype(jnp.float32)).astype(jnp.bfloat16)
                out_buf[slot, g * wide:(g + 1) * wide, :, rows] = total.T.reshape(wide, b_local, 256)
        out_copy(step, slot).start()

    for step in range(max(steps - 2, 0), steps):
        out_copy(step, step % 2).wait()


def chunk_update(own, pieces, panel_w, ladder, out, after, q, a_local, b_local, occupied):
    arrays, starts = zip(*pieces)
    rows = GROUP * occupied
    count = occupied * occupied
    k_all, width = panel_w[0].shape
    parts = 1 + panel_w[1].shape[1] // width
    args = [*arrays, *panel_w, ladder, *after]
    aliases = {}
    if out is not None:
        aliases = {len(args) + 1: 0}
        args.append(out)
    flops = 2 * rows * k_all * occupied * b_local + 2 * GROUP * b_local * count * count
    size = parts * k_all * width + count * count + rows * k_all + GROUP * b_local * count
    return pl.pallas_call(
        functools.partial(chunk_kernel, starts=starts, parts=parts, occupied=occupied, b_local=b_local, q=q),
        out_shape=jax.ShapeDtypeStruct((a_local, b_local, count), jnp.bfloat16),
        in_specs=[pl.BlockSpec(memory_space=pltpu.SMEM)] + [ANY] * len(args),
        out_specs=ANY,
        scratch_shapes=[
            pltpu.VMEM((rows, k_all), jnp.bfloat16),
            pltpu.VMEM((2, k_all, width), jnp.bfloat16),
            pltpu.VMEM((count, count), jnp.bfloat16),
            pltpu.VMEM((GROUP * (count + PAD), b_local), jnp.float32),
            pltpu.VMEM((2, STEP_A, b_local, count), jnp.bfloat16),
            pltpu.SemaphoreType.DMA((parts,)),
            pltpu.SemaphoreType.DMA((2,)),
            pltpu.SemaphoreType.DMA,
            pltpu.SemaphoreType.DMA((2,)),
        ],
        input_output_aliases=aliases,
        compiler_params=pltpu.CompilerParams(vmem_limit_bytes=60 * 1024 * 1024),
        cost_estimate=pl.CostEstimate(flops=flops, bytes_accessed=2 * size, transcendentals=0),
    )(own.reshape(1), *args)


def plain_update(own, pieces, panel_w, ladder, b_local, occupied):
    parts = (len(pieces) + 1) // 2
    back = jnp.argsort(lax.rem(own - jnp.arange(parts) + parts, parts))
    rows, depth = pieces[0].shape
    right, left = pieces[1:parts], pieces[parts:]
    by_shift = [pieces[0]] + [jnp.where(own >= s, right[s - 1], left[parts - s - 1]) for s in range(1, parts)]
    panel_t = jnp.transpose(jnp.stack(by_shift, 0)[back], (1, 0, 2)).reshape(rows, -1)
    cycle = jnp.dot(panel_t, jnp.concatenate(panel_w, axis=1), preferred_element_type=jnp.float32)
    cycle = cycle.astype(jnp.bfloat16).reshape(occupied, -1, parts, occupied // parts, b_local)[:, :, back]
    cycle = cycle.reshape(occupied, -1, occupied, b_local)
    a_count = cycle.shape[1]
    pairs = jnp.transpose(cycle, (1, 3, 0, 2)).reshape(a_count * b_local, occupied * occupied)
    mixed = lax.dot_general(pairs, ladder, (((1,), (1,)), ((), ())), preferred_element_type=jnp.float32)
    total = (mixed + pairs.astype(jnp.float32)).astype(jnp.bfloat16)
    return total.reshape(a_count, b_local, occupied * occupied)


def local(rows, cols, amplitudes, couplings, ladder):
    depth = amplitudes.shape[1]
    i_local = amplitudes.shape[0] // V
    j_local = couplings.shape[1] // V
    occupied = i_local * rows
    a_local, b_local = V // rows, V // cols
    own = lax.axis_index("col")

    chunks = a_local // GROUP
    blocks = amplitudes.reshape(i_local, rows, chunks, GROUP, depth)
    blocks, *arrived = cut(own, blocks, couplings, cols, j_local, b_local)
    for s in range(1, cols):
        arrived[s] = lax.ppermute(arrived[s], "col", [(c, (c + s) % cols) for c in range(cols)])
    blocks = lax.all_to_all(blocks, "row", split_axis=0, concat_axis=0, tiled=True)

    rest, _ = lax.optimization_barrier((arrived[1:], blocks))
    panel_w = [
        lax.all_gather(part, "row", axis=0, tiled=True) for part in (arrived[0], jnp.concatenate(rest, axis=1))
    ]

    per_part = occupied // cols
    plain = (b_local % 128 or WIDE % b_local or depth % 128 or cols < 4
             or per_part * b_local % WIDE or chunks < 4 or chunks % 2)

    def flat(sides):
        right, left = sides
        return [right[0], *right[1:], *left[1:]]

    def update(q, out, after):
        blocks = [(piece, 0) for piece in flat(pieces[q])]
        return chunk_update(own, blocks, panel_w, ladder, out, after, q, a_local, b_local, occupied)

    def hop(sides, s, direct=False):
        right, left = sides
        first = 0 if direct else s - 1
        step = s if direct else 1
        source = 0 if direct else -1
        right.append(lax.ppermute(right[source], "col", [(c, c + step) for c in range(first, cols - step)]))
        left.append(lax.ppermute(left[source], "col", [(c + step, c) for c in range(cols - step - first)]))

    pieces = []
    for q in range(chunks):
        held = blocks[:, q].reshape(occupied * GROUP, depth)
        pieces.append(([held], [held]))

    if plain:
        for sides in pieces:
            for s in range(1, cols):
                hop(sides, s)
        return jnp.concatenate(
            [plain_update(own, flat(sides), panel_w, ladder, b_local, occupied) for sides in pieces], axis=0)

    def after(done, sides):
        right, left = sides
        done, right[0], left[0] = lax.optimization_barrier((done, right[0], left[0]))
        return done

    *early, x, y = pieces
    for q in range(0, len(early), 2):
        if q:
            for before, sides in zip(early[q - 2:q], early[q:q + 2]):
                before[0][-2], before[1][-2] = after((before[0][-2], before[1][-2]), sides)
        for s in range(1, cols):
            for sides in early[q:q + 2]:
                hop(sides, s)
    before = early[-2]
    before[0][-2], before[1][-2] = after((before[0][-2], before[1][-2]), x)
    for s in range(1, cols - 1):
        hop(x, s)
    out = update(0, None, (x[0][1], x[1][1]))
    moving = (early[-1][0], early[-1][1], x[0], x[1])
    out, *ends = after((out, *[side[-1] for side in moving]), x)
    for side, end in zip(moving, ends):
        side[-1] = end
    hop(x, cols - 1)
    out = after(out, y)
    hop(y, 1)
    out = update(1, out, ())
    out, y[0][-1], y[1][-1], y[0][0], y[1][0] = lax.optimization_barrier(
        (out, y[0][-1], y[1][-1], y[0][0], y[1][0]))
    for s in range(2, cols - 1):
        hop(y, s)
    hop(y, cols - 1, direct=True)
    for q in range(2, chunks):
        out = update(q, out, ())
    return out


def solution(mesh):
    in_specs = (P("row", "col"), P("row", "col"), P())
    out_specs = P("row", "col", None)
    body = functools.partial(local, mesh.shape["row"], mesh.shape["col"])
    return jax.shard_map(body, mesh=mesh, in_specs=in_specs, out_specs=out_specs, check_vma=False)
```

```python
import functools

import jax
import jax.numpy as jnp
from jax import lax
from jax.experimental import pallas as pl
from jax.experimental.pallas import tpu as pltpu
from jax.sharding import PartitionSpec as P

V = 512
GROUP = 16
STEP_A = 4
PAD = 8
WIDE = 512
ANY = pl.BlockSpec(memory_space=pl.ANY)


def cut_kernel(own, t_ref, w_ref, t_out, *refs, j_local, b_local):
    w_outs, t_sem, w_sem = refs[:-2], refs[-2], refs[-1]
    cols = len(w_outs)
    for s in range(cols):
        to = lax.rem(own[0] + s, cols)
        for j in range(j_local):
            start = pl.multiple_of((j * cols + to) * b_local, b_local)
            pltpu.make_async_copy(
                w_ref.at[:, pl.ds(start, b_local)], w_outs[s].at[:, j * b_local:(j + 1) * b_local], w_sem.at[s]
            ).start()
    for i in range(t_ref.shape[0]):
        for r in range(t_ref.shape[1]):
            pltpu.make_async_copy(t_ref.at[i, r], t_out.at[r, :, i], t_sem).start()
    for s in range(cols):
        pltpu.make_async_copy(w_outs[s], w_outs[s], w_sem.at[s]).wait()
    pltpu.make_async_copy(t_out, t_out, t_sem).wait()


def cut(own, blocks, couplings, cols, j_local, b_local):
    i_local, rows, chunks, group, t_depth = blocks.shape
    depth = couplings.shape[0]
    if b_local % 128 or t_depth % 128:
        split = couplings.reshape(depth, j_local, cols, b_local)
        parts = [
            lax.dynamic_index_in_dim(split, lax.rem(own + s, cols), 2, keepdims=False).reshape(depth, -1)
            for s in range(cols)
        ]
        return [blocks.transpose(1, 2, 0, 3, 4), *parts]
    return pl.pallas_call(
        functools.partial(cut_kernel, j_local=j_local, b_local=b_local),
        out_shape=[jax.ShapeDtypeStruct((rows, chunks, i_local, group, t_depth), blocks.dtype)]
        + [jax.ShapeDtypeStruct((depth, j_local * b_local), couplings.dtype)] * cols,
        in_specs=[pl.BlockSpec(memory_space=pltpu.SMEM), ANY, ANY],
        out_specs=[pl.BlockSpec(memory_space=pltpu.VMEM)] * (1 + cols),
        scratch_shapes=[pltpu.SemaphoreType.DMA, pltpu.SemaphoreType.DMA((cols,))],
        compiler_params=pltpu.CompilerParams(vmem_limit_bytes=60 * 1024 * 1024),
        cost_estimate=pl.CostEstimate(flops=0, bytes_accessed=4 * (blocks.size + couplings.size), transcendentals=0),
    )(own.reshape(1), blocks, couplings)


def chunk_kernel(own, *refs, starts, parts, occupied, b_local, q):
    t_refs = [ref.at[pl.ds(start, GROUP * occupied)] for ref, start in zip(refs, starts)]
    t_own, t_right, t_left = t_refs[0], t_refs[1:parts], t_refs[parts:]
    w_own, w_rest, ladder_hbm = refs[2 * parts - 1:2 * parts + 2]
    out_ref, t_all, w_buf, ladder, pairs, out_buf, t_sem, w_sem, l_sem, out_sem = refs[-10:]
    depth = t_own.shape[1]
    width = w_own.shape[1]
    count = occupied * occupied
    pitch = count + PAD
    per_part = occupied // parts
    wide = WIDE // b_local

    def t_copy(src, block, s):
        cols = pl.ds(pl.multiple_of(block * depth, depth), depth)
        return pltpu.make_async_copy(src, t_all.at[:, cols], t_sem.at[s])

    def w_copy(s, slot):
        src = w_rest.at[:, (s - 1) * width:s * width] if s else w_own
        return pltpu.make_async_copy(src, w_buf.at[slot], w_sem.at[slot])

    blocks = [lax.rem(own[0] - s + parts, parts) for s in range(parts)]
    t_copy(t_own, blocks[0], 0).start()
    for s in range(1, parts):
        @pl.when(own[0] >= s)
        def _():
            t_copy(t_right[s - 1], blocks[s], s).start()

        @pl.when(own[0] < s)
        def _():
            t_copy(t_left[parts - s - 1], blocks[s], s).start()
    w_copy(0, 0).start()
    ladder_copy = pltpu.make_async_copy(ladder_hbm, ladder, l_sem)
    for s in range(parts):
        t_copy(t_own, blocks[s], s).wait()

    @pl.loop(0, parts)
    def _(step):
        slot = lax.rem(step, 2)
        w_copy(0, slot).wait()
        for s in range(1, parts):
            @pl.when(step + 1 == s)
            def _():
                w_copy(s, s % 2).start()

        @pl.when(step == parts - 1)
        def _():
            ladder_copy.start()

        j0 = lax.rem(own[0] - step + parts, parts) * per_part
        for tile in range(per_part // wide):
            acc = jnp.dot(
                t_all[...], w_buf[slot, :, tile * WIDE:(tile + 1) * WIDE], preferred_element_type=jnp.float32)
            for i in range(occupied):
                for k in range(wide):
                    n = j0 + (i * occupied + tile * wide + k)
                    for h in range(GROUP // 8):
                        row = i * GROUP + h * 8
                        pairs[pl.ds(h * 8 * pitch + n, 8, stride=pitch), :] = (
                            acc[row:row + 8, k * b_local:(k + 1) * b_local])

    ladder_copy.wait()
    steps = GROUP // STEP_A

    def out_copy(step, slot):
        rows = pl.ds(q * GROUP + step * STEP_A, STEP_A)
        return pltpu.make_async_copy(out_buf.at[slot], out_ref.at[rows], out_sem.at[slot])

    @pl.loop(0, steps)
    def _(step):
        slot = lax.rem(step, 2)

        @pl.when(step >= 2)
        def _():
            out_copy(step - 2, slot).wait()

        for g in range(STEP_A // wide):
            blocks = []
            for k in range(wide):
                row = pl.multiple_of((step * STEP_A + g * wide + k) * pitch, 8)
                blocks.append(pairs[pl.ds(row, count), :].astype(jnp.bfloat16))
            both = jnp.concatenate(blocks, axis=1)
            for m in range(count // 256):
                rows = slice(m * 256, (m + 1) * 256)
                mixed = jnp.dot(ladder[rows, :], both, preferred_element_type=jnp.float32)
                total = (mixed + both[rows, :].astype(jnp.float32)).astype(jnp.bfloat16)
                out_buf[slot, g * wide:(g + 1) * wide, :, rows] = total.T.reshape(wide, b_local, 256)
        out_copy(step, slot).start()

    for step in range(max(steps - 2, 0), steps):
        out_copy(step, step % 2).wait()


def chunk_update(own, pieces, panel_w, ladder, out, after, q, a_local, b_local, occupied):
    arrays, starts = zip(*pieces)
    rows = GROUP * occupied
    count = occupied * occupied
    k_all, width = panel_w[0].shape
    parts = 1 + panel_w[1].shape[1] // width
    args = [*arrays, *panel_w, ladder, *after]
    aliases = {}
    if out is not None:
        aliases = {len(args) + 1: 0}
        args.append(out)
    flops = 2 * rows * k_all * occupied * b_local + 2 * GROUP * b_local * count * count
    size = parts * k_all * width + count * count + rows * k_all + GROUP * b_local * count
    return pl.pallas_call(
        functools.partial(chunk_kernel, starts=starts, parts=parts, occupied=occupied, b_local=b_local, q=q),
        out_shape=jax.ShapeDtypeStruct((a_local, b_local, count), jnp.bfloat16),
        in_specs=[pl.BlockSpec(memory_space=pltpu.SMEM)] + [ANY] * len(args),
        out_specs=ANY,
        scratch_shapes=[
            pltpu.VMEM((rows, k_all), jnp.bfloat16),
            pltpu.VMEM((2, k_all, width), jnp.bfloat16),
            pltpu.VMEM((count, count), jnp.bfloat16),
            pltpu.VMEM((GROUP * (count + PAD), b_local), jnp.float32),
            pltpu.VMEM((2, STEP_A, b_local, count), jnp.bfloat16),
            pltpu.SemaphoreType.DMA((parts,)),
            pltpu.SemaphoreType.DMA((2,)),
            pltpu.SemaphoreType.DMA,
            pltpu.SemaphoreType.DMA((2,)),
        ],
        input_output_aliases=aliases,
        compiler_params=pltpu.CompilerParams(vmem_limit_bytes=60 * 1024 * 1024),
        cost_estimate=pl.CostEstimate(flops=flops, bytes_accessed=2 * size, transcendentals=0),
    )(own.reshape(1), *args)


def plain_update(own, pieces, panel_w, ladder, b_local, occupied):
    parts = (len(pieces) + 1) // 2
    back = jnp.argsort(lax.rem(own - jnp.arange(parts) + parts, parts))
    rows, depth = pieces[0].shape
    right, left = pieces[1:parts], pieces[parts:]
    by_shift = [pieces[0]] + [jnp.where(own >= s, right[s - 1], left[parts - s - 1]) for s in range(1, parts)]
    panel_t = jnp.transpose(jnp.stack(by_shift, 0)[back], (1, 0, 2)).reshape(rows, -1)
    cycle = jnp.dot(panel_t, jnp.concatenate(panel_w, axis=1), preferred_element_type=jnp.float32)
    cycle = cycle.astype(jnp.bfloat16).reshape(occupied, -1, parts, occupied // parts, b_local)[:, :, back]
    cycle = cycle.reshape(occupied, -1, occupied, b_local)
    a_count = cycle.shape[1]
    pairs = jnp.transpose(cycle, (1, 3, 0, 2)).reshape(a_count * b_local, occupied * occupied)
    mixed = lax.dot_general(pairs, ladder, (((1,), (1,)), ((), ())), preferred_element_type=jnp.float32)
    total = (mixed + pairs.astype(jnp.float32)).astype(jnp.bfloat16)
    return total.reshape(a_count, b_local, occupied * occupied)


def local(rows, cols, amplitudes, couplings, ladder):
    depth = amplitudes.shape[1]
    i_local = amplitudes.shape[0] // V
    j_local = couplings.shape[1] // V
    occupied = i_local * rows
    a_local, b_local = V // rows, V // cols
    own = lax.axis_index("col")

    chunks = a_local // GROUP
    blocks = amplitudes.reshape(i_local, rows, chunks, GROUP, depth)
    blocks, *arrived = cut(own, blocks, couplings, cols, j_local, b_local)
    for s in range(1, cols):
        arrived[s] = lax.ppermute(arrived[s], "col", [(c, (c + s) % cols) for c in range(cols)])
    blocks = lax.all_to_all(blocks, "row", split_axis=0, concat_axis=0, tiled=True)

    rest, _ = lax.optimization_barrier((arrived[1:], blocks))
    panel_w = [
        lax.all_gather(part, "row", axis=0, tiled=True) for part in (arrived[0], jnp.concatenate(rest, axis=1))
    ]

    per_part = occupied // cols
    plain = (b_local % 128 or WIDE % b_local or depth % 128 or cols < 4
             or per_part * b_local % WIDE or chunks < 4 or chunks % 2)

    def flat(sides):
        right, left = sides
        return [right[0], *right[1:], *left[1:]]

    def update(q, out, after):
        blocks = [(piece, 0) for piece in flat(pieces[q])]
        return chunk_update(own, blocks, panel_w, ladder, out, after, q, a_local, b_local, occupied)

    def hop(sides, s, direct=False):
        right, left = sides
        first = 0 if direct else s - 1
        step = s if direct else 1
        source = 0 if direct else -1
        right.append(lax.ppermute(right[source], "col", [(c, c + step) for c in range(first, cols - step)]))
        left.append(lax.ppermute(left[source], "col", [(c + step, c) for c in range(cols - step - first)]))

    pieces = []
    for q in range(chunks):
        held = blocks[:, q].reshape(occupied * GROUP, depth)
        pieces.append(([held], [held]))

    if plain:
        for sides in pieces:
            for s in range(1, cols):
                hop(sides, s)
        return jnp.concatenate(
            [plain_update(own, flat(sides), panel_w, ladder, b_local, occupied) for sides in pieces], axis=0)

    def after(done, sides):
        right, left = sides
        done, right[0], left[0] = lax.optimization_barrier((done, right[0], left[0]))
        return done

    *early, x, y = pieces
    for q in range(0, len(early), 2):
        if q:
            for before, sides in zip(early[q - 2:q], early[q:q + 2]):
                before[0][-2], before[1][-2] = after((before[0][-2], before[1][-2]), sides)
        for s in range(1, cols):
            for sides in early[q:q + 2]:
                hop(sides, s)
    before = early[-2]
    before[0][-2], before[1][-2] = after((before[0][-2], before[1][-2]), x)
    for s in range(1, cols - 1):
        hop(x, s)
    out = update(0, None, (x[0][1], x[1][1]))
    moving = (early[-1][0], early[-1][1], x[0], x[1])
    out, *ends = after((out, *[side[-1] for side in moving]), x)
    for side, end in zip(moving, ends):
        side[-1] = end
    hop(x, cols - 1)
    out = after(out, y)
    hop(y, 1)
    out = update(1, out, ())
    out, y[0][-1], y[1][-1], y[0][0], y[1][0] = lax.optimization_barrier(
        (out, y[0][-1], y[1][-1], y[0][0], y[1][0]))
    for s in range(2, cols - 1):
        hop(y, s)
    far = lax.ppermute(y[0][0], "col", [(0, cols - 1), (cols - 1, 0)])
    y[0].append(far)
    y[1].append(far)
    for q in range(2, chunks):
        out = update(q, out, ())
    return out


def solution(mesh):
    in_specs = (P("row", "col"), P("row", "col"), P())
    out_specs = P("row", "col", None)
    body = functools.partial(local, mesh.shape["row"], mesh.shape["col"])
    return jax.shard_map(body, mesh=mesh, in_specs=in_specs, out_specs=out_specs, check_vma=False)
```

```python
import functools

import jax
import jax.numpy as jnp
from jax import lax
from jax.experimental import pallas as pl
from jax.experimental.pallas import tpu as pltpu
from jax.sharding import PartitionSpec as P

V = 512
GROUP = 16
STEP_A = 4
PAD = 8
WIDE = 512
ANY = pl.BlockSpec(memory_space=pl.ANY)


def cut_kernel(own, t_ref, w_ref, t_out, *refs, j_local, b_local):
    w_outs, t_sem, w_sem = refs[:-2], refs[-2], refs[-1]
    cols = len(w_outs)
    for s in range(cols):
        to = lax.rem(own[0] + s, cols)
        for j in range(j_local):
            start = pl.multiple_of((j * cols + to) * b_local, b_local)
            pltpu.make_async_copy(
                w_ref.at[:, pl.ds(start, b_local)], w_outs[s].at[:, j * b_local:(j + 1) * b_local], w_sem.at[s]
            ).start()
    for i in range(t_ref.shape[0]):
        for r in range(t_ref.shape[1]):
            pltpu.make_async_copy(t_ref.at[i, r], t_out.at[r, :, i], t_sem).start()
    for s in range(cols):
        pltpu.make_async_copy(w_outs[s], w_outs[s], w_sem.at[s]).wait()
    pltpu.make_async_copy(t_out, t_out, t_sem).wait()


def cut(own, blocks, couplings, cols, j_local, b_local):
    i_local, rows, chunks, group, t_depth = blocks.shape
    depth = couplings.shape[0]
    if b_local % 128 or t_depth % 128:
        split = couplings.reshape(depth, j_local, cols, b_local)
        parts = [
            lax.dynamic_index_in_dim(split, lax.rem(own + s, cols), 2, keepdims=False).reshape(depth, -1)
            for s in range(cols)
        ]
        return [blocks.transpose(1, 2, 0, 3, 4), *parts]
    return pl.pallas_call(
        functools.partial(cut_kernel, j_local=j_local, b_local=b_local),
        out_shape=[jax.ShapeDtypeStruct((rows, chunks, i_local, group, t_depth), blocks.dtype)]
        + [jax.ShapeDtypeStruct((depth, j_local * b_local), couplings.dtype)] * cols,
        in_specs=[pl.BlockSpec(memory_space=pltpu.SMEM), ANY, ANY],
        out_specs=[pl.BlockSpec(memory_space=pltpu.VMEM)] * (1 + cols),
        scratch_shapes=[pltpu.SemaphoreType.DMA, pltpu.SemaphoreType.DMA((cols,))],
        compiler_params=pltpu.CompilerParams(vmem_limit_bytes=60 * 1024 * 1024),
        cost_estimate=pl.CostEstimate(flops=0, bytes_accessed=4 * (blocks.size + couplings.size), transcendentals=0),
    )(own.reshape(1), blocks, couplings)


def chunk_kernel(own, *refs, starts, parts, occupied, b_local, q):
    t_refs = [ref.at[pl.ds(start, GROUP * occupied)] for ref, start in zip(refs, starts)]
    t_own, t_right, t_left = t_refs[0], t_refs[1:parts], t_refs[parts:]
    w_own, w_rest, ladder_hbm = refs[2 * parts - 1:2 * parts + 2]
    out_ref, t_all, w_buf, ladder, pairs, out_buf, t_sem, w_sem, l_sem, out_sem = refs[-10:]
    depth = t_own.shape[1]
    width = w_own.shape[1]
    count = occupied * occupied
    pitch = count + PAD
    per_part = occupied // parts
    wide = WIDE // b_local

    def t_copy(src, block, s):
        cols = pl.ds(pl.multiple_of(block * depth, depth), depth)
        return pltpu.make_async_copy(src, t_all.at[:, cols], t_sem.at[s])

    tiles = per_part // wide

    def w_copy(s, slot, tile):
        cols = pl.ds(tile * WIDE, WIDE)
        src = w_rest.at[:, pl.ds((s - 1) * width + tile * WIDE, WIDE)] if s else w_own.at[:, cols]
        return pltpu.make_async_copy(src, w_buf.at[slot, :, cols], w_sem.at[slot, tile])

    blocks = [lax.rem(own[0] - s + parts, parts) for s in range(parts)]
    t_copy(t_own, blocks[0], 0).start()
    for s in range(1, parts):
        @pl.when(own[0] >= s)
        def _():
            t_copy(t_right[s - 1], blocks[s], s).start()

        @pl.when(own[0] < s)
        def _():
            t_copy(t_left[parts - s - 1], blocks[s], s).start()
    for tile in range(tiles):
        w_copy(0, 0, tile).start()
    ladder_copy = pltpu.make_async_copy(ladder_hbm, ladder, l_sem)
    for s in range(parts):
        t_copy(t_own, blocks[s], s).wait()

    @pl.loop(0, parts)
    def _(step):
        slot = lax.rem(step, 2)
        w_copy(0, slot, 0).wait()
        for s in range(1, parts):
            @pl.when(step + 1 == s)
            def _():
                for tile in range(tiles):
                    w_copy(s, s % 2, tile).start()

        @pl.when(step == parts - 1)
        def _():
            ladder_copy.start()

        j0 = lax.rem(own[0] - step + parts, parts) * per_part
        for tile in range(tiles):
            if tile:
                w_copy(0, slot, tile).wait()
            acc = jnp.dot(
                t_all[...], w_buf[slot, :, tile * WIDE:(tile + 1) * WIDE], preferred_element_type=jnp.float32)
            for i in range(occupied):
                for k in range(wide):
                    n = j0 + (i * occupied + tile * wide + k)
                    for h in range(GROUP // 8):
                        row = i * GROUP + h * 8
                        pairs[pl.ds(h * 8 * pitch + n, 8, stride=pitch), :] = (
                            acc[row:row + 8, k * b_local:(k + 1) * b_local])

    ladder_copy.wait()
    steps = GROUP // STEP_A

    def out_copy(step, slot):
        rows = pl.ds(q * GROUP + step * STEP_A, STEP_A)
        return pltpu.make_async_copy(out_buf.at[slot], out_ref.at[rows], out_sem.at[slot])

    @pl.loop(0, steps)
    def _(step):
        slot = lax.rem(step, 2)

        @pl.when(step >= 2)
        def _():
            out_copy(step - 2, slot).wait()

        for g in range(STEP_A // wide):
            blocks = []
            for k in range(wide):
                row = pl.multiple_of((step * STEP_A + g * wide + k) * pitch, 8)
                blocks.append(pairs[pl.ds(row, count), :].astype(jnp.bfloat16))
            both = jnp.concatenate(blocks, axis=1)
            for m in range(count // 256):
                rows = slice(m * 256, (m + 1) * 256)
                mixed = jnp.dot(ladder[rows, :], both, preferred_element_type=jnp.float32)
                total = (mixed + both[rows, :].astype(jnp.float32)).astype(jnp.bfloat16)
                out_buf[slot, g * wide:(g + 1) * wide, :, rows] = total.T.reshape(wide, b_local, 256)
        out_copy(step, slot).start()

    for step in range(max(steps - 2, 0), steps):
        out_copy(step, step % 2).wait()


def chunk_update(own, pieces, panel_w, ladder, out, after, q, a_local, b_local, occupied):
    arrays, starts = zip(*pieces)
    rows = GROUP * occupied
    count = occupied * occupied
    k_all, width = panel_w[0].shape
    parts = 1 + panel_w[1].shape[1] // width
    args = [*arrays, *panel_w, ladder, *after]
    aliases = {}
    if out is not None:
        aliases = {len(args) + 1: 0}
        args.append(out)
    flops = 2 * rows * k_all * occupied * b_local + 2 * GROUP * b_local * count * count
    size = parts * k_all * width + count * count + rows * k_all + GROUP * b_local * count
    return pl.pallas_call(
        functools.partial(chunk_kernel, starts=starts, parts=parts, occupied=occupied, b_local=b_local, q=q),
        out_shape=jax.ShapeDtypeStruct((a_local, b_local, count), jnp.bfloat16),
        in_specs=[pl.BlockSpec(memory_space=pltpu.SMEM)] + [ANY] * len(args),
        out_specs=ANY,
        scratch_shapes=[
            pltpu.VMEM((rows, k_all), jnp.bfloat16),
            pltpu.VMEM((2, k_all, width), jnp.bfloat16),
            pltpu.VMEM((count, count), jnp.bfloat16),
            pltpu.VMEM((GROUP * (count + PAD), b_local), jnp.float32),
            pltpu.VMEM((2, STEP_A, b_local, count), jnp.bfloat16),
            pltpu.SemaphoreType.DMA((parts,)),
            pltpu.SemaphoreType.DMA((2, width // WIDE)),
            pltpu.SemaphoreType.DMA,
            pltpu.SemaphoreType.DMA((2,)),
        ],
        input_output_aliases=aliases,
        compiler_params=pltpu.CompilerParams(vmem_limit_bytes=60 * 1024 * 1024),
        cost_estimate=pl.CostEstimate(flops=flops, bytes_accessed=2 * size, transcendentals=0),
    )(own.reshape(1), *args)


def plain_update(own, pieces, panel_w, ladder, b_local, occupied):
    parts = (len(pieces) + 1) // 2
    back = jnp.argsort(lax.rem(own - jnp.arange(parts) + parts, parts))
    rows, depth = pieces[0].shape
    right, left = pieces[1:parts], pieces[parts:]
    by_shift = [pieces[0]] + [jnp.where(own >= s, right[s - 1], left[parts - s - 1]) for s in range(1, parts)]
    panel_t = jnp.transpose(jnp.stack(by_shift, 0)[back], (1, 0, 2)).reshape(rows, -1)
    cycle = jnp.dot(panel_t, jnp.concatenate(panel_w, axis=1), preferred_element_type=jnp.float32)
    cycle = cycle.astype(jnp.bfloat16).reshape(occupied, -1, parts, occupied // parts, b_local)[:, :, back]
    cycle = cycle.reshape(occupied, -1, occupied, b_local)
    a_count = cycle.shape[1]
    pairs = jnp.transpose(cycle, (1, 3, 0, 2)).reshape(a_count * b_local, occupied * occupied)
    mixed = lax.dot_general(pairs, ladder, (((1,), (1,)), ((), ())), preferred_element_type=jnp.float32)
    total = (mixed + pairs.astype(jnp.float32)).astype(jnp.bfloat16)
    return total.reshape(a_count, b_local, occupied * occupied)


def local(rows, cols, amplitudes, couplings, ladder):
    depth = amplitudes.shape[1]
    i_local = amplitudes.shape[0] // V
    j_local = couplings.shape[1] // V
    occupied = i_local * rows
    a_local, b_local = V // rows, V // cols
    own = lax.axis_index("col")

    chunks = a_local // GROUP
    blocks = amplitudes.reshape(i_local, rows, chunks, GROUP, depth)
    blocks, *arrived = cut(own, blocks, couplings, cols, j_local, b_local)
    for s in range(1, cols):
        arrived[s] = lax.ppermute(arrived[s], "col", [(c, (c + s) % cols) for c in range(cols)])
    blocks = lax.all_to_all(blocks, "row", split_axis=0, concat_axis=0, tiled=True)

    held = [blocks[:, q].reshape(occupied * GROUP, depth) for q in range(chunks)]
    rest, _ = lax.optimization_barrier((arrived[1:], held))
    panel_w = [
        lax.all_gather(part, "row", axis=0, tiled=True) for part in (arrived[0], jnp.concatenate(rest, axis=1))
    ]

    per_part = occupied // cols
    plain = (b_local % 128 or WIDE % b_local or depth % 128 or cols < 4
             or per_part * b_local % WIDE or chunks < 4 or chunks % 2)

    def flat(sides):
        right, left = sides
        return [right[0], *right[1:], *left[1:]]

    def update(q, out, after):
        blocks = [(piece, 0) for piece in flat(pieces[q])]
        return chunk_update(own, blocks, panel_w, ladder, out, after, q, a_local, b_local, occupied)

    def hop(sides, s, direct=False):
        right, left = sides
        first = 0 if direct else s - 1
        step = s if direct else 1
        source = 0 if direct else -1
        right.append(lax.ppermute(right[source], "col", [(c, c + step) for c in range(first, cols - step)]))
        left.append(lax.ppermute(left[source], "col", [(c + step, c) for c in range(cols - step - first)]))

    pieces = [([block], [block]) for block in held]

    if plain:
        for sides in pieces:
            for s in range(1, cols):
                hop(sides, s)
        return jnp.concatenate(
            [plain_update(own, flat(sides), panel_w, ladder, b_local, occupied) for sides in pieces], axis=0)

    def after(done, sides):
        right, left = sides
        done, right[0], left[0] = lax.optimization_barrier((done, right[0], left[0]))
        return done

    *early, x, y = pieces
    for q in range(0, len(early), 2):
        if q:
            for before, sides in zip(early[q - 2:q], early[q:q + 2]):
                before[0][-2], before[1][-2] = after((before[0][-2], before[1][-2]), sides)
        for s in range(1, cols):
            for sides in early[q:q + 2]:
                hop(sides, s)
    before = early[-2]
    before[0][-2], before[1][-2] = after((before[0][-2], before[1][-2]), x)
    for s in range(1, cols - 1):
        hop(x, s)
    out = update(0, None, (x[0][1], x[1][1]))
    moving = (early[-1][0], early[-1][1], x[0], x[1])
    out, *ends = after((out, *[side[-1] for side in moving]), x)
    for side, end in zip(moving, ends):
        side[-1] = end
    hop(x, cols - 1)
    out = after(out, y)
    hop(y, 1)
    out = update(1, out, ())
    out, y[0][-1], y[1][-1], y[0][0], y[1][0] = lax.optimization_barrier(
        (out, y[0][-1], y[1][-1], y[0][0], y[1][0]))
    for s in range(2, cols - 1):
        hop(y, s)
    hop(y, cols - 1, direct=True)
    for q in range(2, chunks):
        out = update(q, out, ())
    return out


def solution(mesh):
    in_specs = (P("row", "col"), P("row", "col"), P())
    out_specs = P("row", "col", None)
    body = functools.partial(local, mesh.shape["row"], mesh.shape["col"])
    return jax.shard_map(body, mesh=mesh, in_specs=in_specs, out_specs=out_specs, check_vma=False)
```

```python
import functools

import jax
import jax.numpy as jnp
from jax import lax
from jax.experimental import pallas as pl
from jax.experimental.pallas import tpu as pltpu
from jax.sharding import PartitionSpec as P

V = 512
GROUP = 16
STEP_A = 4
PAD = 8
WIDE = 1024
TALL = 512
ANY = pl.BlockSpec(memory_space=pl.ANY)


def cut_kernel(own, t_ref, w_ref, t_out, *refs, j_local, b_local):
    w_outs, t_sem, w_sem = refs[:-2], refs[-2], refs[-1]
    cols = len(w_outs)
    for s in range(cols):
        to = lax.rem(own[0] + s, cols)
        for j in range(j_local):
            start = pl.multiple_of((j * cols + to) * b_local, b_local)
            pltpu.make_async_copy(
                w_ref.at[:, pl.ds(start, b_local)], w_outs[s].at[:, j * b_local:(j + 1) * b_local], w_sem.at[s]
            ).start()
    for i in range(t_ref.shape[0]):
        for r in range(t_ref.shape[1]):
            pltpu.make_async_copy(t_ref.at[i, r], t_out.at[r, :, i], t_sem).start()
    for s in range(cols):
        pltpu.make_async_copy(w_outs[s], w_outs[s], w_sem.at[s]).wait()
    pltpu.make_async_copy(t_out, t_out, t_sem).wait()


def cut(own, blocks, couplings, cols, j_local, b_local):
    i_local, rows, chunks, group, t_depth = blocks.shape
    depth = couplings.shape[0]
    if b_local % 128 or t_depth % 128:
        split = couplings.reshape(depth, j_local, cols, b_local)
        parts = [
            lax.dynamic_index_in_dim(split, lax.rem(own + s, cols), 2, keepdims=False).reshape(depth, -1)
            for s in range(cols)
        ]
        return [blocks.transpose(1, 2, 0, 3, 4), *parts]
    return pl.pallas_call(
        functools.partial(cut_kernel, j_local=j_local, b_local=b_local),
        out_shape=[jax.ShapeDtypeStruct((rows, chunks, i_local, group, t_depth), blocks.dtype)]
        + [jax.ShapeDtypeStruct((depth, j_local * b_local), couplings.dtype)] * cols,
        in_specs=[pl.BlockSpec(memory_space=pltpu.SMEM), ANY, ANY],
        out_specs=[pl.BlockSpec(memory_space=pltpu.VMEM)] * (1 + cols),
        scratch_shapes=[pltpu.SemaphoreType.DMA, pltpu.SemaphoreType.DMA((cols,))],
        compiler_params=pltpu.CompilerParams(vmem_limit_bytes=60 * 1024 * 1024),
        cost_estimate=pl.CostEstimate(flops=0, bytes_accessed=4 * (blocks.size + couplings.size), transcendentals=0),
    )(own.reshape(1), blocks, couplings)


def chunk_kernel(own, *refs, starts, parts, occupied, b_local, q):
    t_refs = [ref.at[pl.ds(start, GROUP * occupied)] for ref, start in zip(refs, starts)]
    t_own, t_right, t_left = t_refs[0], t_refs[1:parts], t_refs[parts:]
    w_own, w_rest, ladder_hbm = refs[2 * parts - 1:2 * parts + 2]
    out_ref, t_all, w_buf, ladder, pairs, out_buf, t_sem, w_sem, l_sem, out_sem = refs[-10:]
    depth = t_own.shape[1]
    width = w_own.shape[1]
    count = occupied * occupied
    pitch = count + PAD
    per_part = occupied // parts
    wide = WIDE // b_local

    def t_copy(src, block, s):
        cols = pl.ds(pl.multiple_of(block * depth, depth), depth)
        return pltpu.make_async_copy(src, t_all.at[:, cols], t_sem.at[s])

    def w_copy(s, slot):
        src = w_rest.at[:, (s - 1) * width:s * width] if s else w_own
        return pltpu.make_async_copy(src, w_buf.at[slot], w_sem.at[slot])

    blocks = [lax.rem(own[0] - s + parts, parts) for s in range(parts)]
    t_copy(t_own, blocks[0], 0).start()
    for s in range(1, parts):
        @pl.when(own[0] >= s)
        def _():
            t_copy(t_right[s - 1], blocks[s], s).start()

        @pl.when(own[0] < s)
        def _():
            t_copy(t_left[parts - s - 1], blocks[s], s).start()
    w_copy(0, 0).start()
    ladder_copy = pltpu.make_async_copy(ladder_hbm, ladder, l_sem)
    for s in range(parts):
        t_copy(t_own, blocks[s], s).wait()

    @pl.loop(0, parts)
    def _(step):
        slot = lax.rem(step, 2)
        w_copy(0, slot).wait()
        for s in range(1, parts):
            @pl.when(step + 1 == s)
            def _():
                w_copy(s, s % 2).start()

        @pl.when(step == parts - 1)
        def _():
            ladder_copy.start()

        j0 = lax.rem(own[0] - step + parts, parts) * per_part
        for tile in range(per_part // wide):
            acc = jnp.dot(
                t_all[...], w_buf[slot, :, tile * WIDE:(tile + 1) * WIDE], preferred_element_type=jnp.float32)
            for i in range(occupied):
                for k in range(wide):
                    n = j0 + (i * occupied + tile * wide + k)
                    for h in range(GROUP // 8):
                        row = i * GROUP + h * 8
                        pairs[pl.ds(h * 8 * pitch + n, 8, stride=pitch), :] = (
                            acc[row:row + 8, k * b_local:(k + 1) * b_local])

    ladder_copy.wait()
    steps = GROUP // STEP_A

    def out_copy(step, slot):
        rows = pl.ds(q * GROUP + step * STEP_A, STEP_A)
        return pltpu.make_async_copy(out_buf.at[slot], out_ref.at[rows], out_sem.at[slot])

    @pl.loop(0, steps)
    def _(step):
        slot = lax.rem(step, 2)

        @pl.when(step >= 2)
        def _():
            out_copy(step - 2, slot).wait()

        blocks = []
        for k in range(STEP_A):
            row = pl.multiple_of((step * STEP_A + k) * pitch, 8)
            blocks.append(pairs[pl.ds(row, count), :].astype(jnp.bfloat16))
        both = jnp.concatenate(blocks, axis=1)
        for m in range(count // TALL):
            rows = slice(m * TALL, (m + 1) * TALL)
            mixed = jnp.dot(ladder[rows, :], both, preferred_element_type=jnp.float32)
            total = (mixed + both[rows, :].astype(jnp.float32)).astype(jnp.bfloat16)
            out_buf[slot, :, :, rows] = total.T.reshape(STEP_A, b_local, TALL)
        out_copy(step, slot).start()

    for step in range(max(steps - 2, 0), steps):
        out_copy(step, step % 2).wait()


def chunk_update(own, pieces, panel_w, ladder, out, after, q, a_local, b_local, occupied):
    arrays, starts = zip(*pieces)
    rows = GROUP * occupied
    count = occupied * occupied
    k_all, width = panel_w[0].shape
    parts = 1 + panel_w[1].shape[1] // width
    args = [*arrays, *panel_w, ladder, *after]
    aliases = {}
    if out is not None:
        aliases = {len(args) + 1: 0}
        args.append(out)
    flops = 2 * rows * k_all * occupied * b_local + 2 * GROUP * b_local * count * count
    size = parts * k_all * width + count * count + rows * k_all + GROUP * b_local * count
    return pl.pallas_call(
        functools.partial(chunk_kernel, starts=starts, parts=parts, occupied=occupied, b_local=b_local, q=q),
        out_shape=jax.ShapeDtypeStruct((a_local, b_local, count), jnp.bfloat16),
        in_specs=[pl.BlockSpec(memory_space=pltpu.SMEM)] + [ANY] * len(args),
        out_specs=ANY,
        scratch_shapes=[
            pltpu.VMEM((rows, k_all), jnp.bfloat16),
            pltpu.VMEM((2, k_all, width), jnp.bfloat16),
            pltpu.VMEM((count, count), jnp.bfloat16),
            pltpu.VMEM((GROUP * (count + PAD), b_local), jnp.float32),
            pltpu.VMEM((2, STEP_A, b_local, count), jnp.bfloat16),
            pltpu.SemaphoreType.DMA((parts,)),
            pltpu.SemaphoreType.DMA((2,)),
            pltpu.SemaphoreType.DMA,
            pltpu.SemaphoreType.DMA((2,)),
        ],
        input_output_aliases=aliases,
        compiler_params=pltpu.CompilerParams(vmem_limit_bytes=60 * 1024 * 1024),
        cost_estimate=pl.CostEstimate(flops=flops, bytes_accessed=2 * size, transcendentals=0),
    )(own.reshape(1), *args)


def plain_update(own, pieces, panel_w, ladder, b_local, occupied):
    parts = (len(pieces) + 1) // 2
    back = jnp.argsort(lax.rem(own - jnp.arange(parts) + parts, parts))
    rows, depth = pieces[0].shape
    right, left = pieces[1:parts], pieces[parts:]
    by_shift = [pieces[0]] + [jnp.where(own >= s, right[s - 1], left[parts - s - 1]) for s in range(1, parts)]
    panel_t = jnp.transpose(jnp.stack(by_shift, 0)[back], (1, 0, 2)).reshape(rows, -1)
    cycle = jnp.dot(panel_t, jnp.concatenate(panel_w, axis=1), preferred_element_type=jnp.float32)
    cycle = cycle.astype(jnp.bfloat16).reshape(occupied, -1, parts, occupied // parts, b_local)[:, :, back]
    cycle = cycle.reshape(occupied, -1, occupied, b_local)
    a_count = cycle.shape[1]
    pairs = jnp.transpose(cycle, (1, 3, 0, 2)).reshape(a_count * b_local, occupied * occupied)
    mixed = lax.dot_general(pairs, ladder, (((1,), (1,)), ((), ())), preferred_element_type=jnp.float32)
    total = (mixed + pairs.astype(jnp.float32)).astype(jnp.bfloat16)
    return total.reshape(a_count, b_local, occupied * occupied)


def local(rows, cols, amplitudes, couplings, ladder):
    depth = amplitudes.shape[1]
    i_local = amplitudes.shape[0] // V
    j_local = couplings.shape[1] // V
    occupied = i_local * rows
    a_local, b_local = V // rows, V // cols
    own = lax.axis_index("col")

    chunks = a_local // GROUP
    blocks = amplitudes.reshape(i_local, rows, chunks, GROUP, depth)
    blocks, *arrived = cut(own, blocks, couplings, cols, j_local, b_local)
    for s in range(1, cols):
        arrived[s] = lax.ppermute(arrived[s], "col", [(c, (c + s) % cols) for c in range(cols)])
    blocks = lax.all_to_all(blocks, "row", split_axis=0, concat_axis=0, tiled=True)

    rest, _ = lax.optimization_barrier((arrived[1:], blocks))
    panel_w = [
        lax.all_gather(part, "row", axis=0, tiled=True) for part in (arrived[0], jnp.concatenate(rest, axis=1))
    ]

    per_part = occupied // cols
    plain = (b_local % 128 or WIDE % b_local or depth % 128 or cols < 4
             or per_part * b_local % WIDE or occupied * occupied % TALL or chunks < 4 or chunks % 2)

    def flat(sides):
        right, left = sides
        return [right[0], *right[1:], *left[1:]]

    def update(q, out, after):
        blocks = [(piece, 0) for piece in flat(pieces[q])]
        return chunk_update(own, blocks, panel_w, ladder, out, after, q, a_local, b_local, occupied)

    def hop(sides, s, direct=False):
        right, left = sides
        first = 0 if direct else s - 1
        step = s if direct else 1
        source = 0 if direct else -1
        right.append(lax.ppermute(right[source], "col", [(c, c + step) for c in range(first, cols - step)]))
        left.append(lax.ppermute(left[source], "col", [(c + step, c) for c in range(cols - step - first)]))

    pieces = []
    for q in range(chunks):
        held = blocks[:, q].reshape(occupied * GROUP, depth)
        pieces.append(([held], [held]))

    if plain:
        for sides in pieces:
            for s in range(1, cols):
                hop(sides, s)
        return jnp.concatenate(
            [plain_update(own, flat(sides), panel_w, ladder, b_local, occupied) for sides in pieces], axis=0)

    def after(done, sides):
        right, left = sides
        done, right[0], left[0] = lax.optimization_barrier((done, right[0], left[0]))
        return done

    *early, x, y = pieces
    for q in range(0, len(early), 2):
        if q:
            for before, sides in zip(early[q - 2:q], early[q:q + 2]):
                before[0][-2], before[1][-2] = after((before[0][-2], before[1][-2]), sides)
        for s in range(1, cols):
            for sides in early[q:q + 2]:
                hop(sides, s)
    before = early[-2]
    before[0][-2], before[1][-2] = after((before[0][-2], before[1][-2]), x)
    for s in range(1, cols - 1):
        hop(x, s)
    out = update(0, None, (x[0][1], x[1][1]))
    moving = (early[-1][0], early[-1][1], x[0], x[1])
    out, *ends = after((out, *[side[-1] for side in moving]), x)
    for side, end in zip(moving, ends):
        side[-1] = end
    hop(x, cols - 1)
    out = after(out, y)
    hop(y, 1)
    out = update(1, out, ())
    out, y[0][-1], y[1][-1], y[0][0], y[1][0] = lax.optimization_barrier(
        (out, y[0][-1], y[1][-1], y[0][0], y[1][0]))
    for s in range(2, cols - 1):
        hop(y, s)
    hop(y, cols - 1, direct=True)
    for q in range(2, chunks):
        out = update(q, out, ())
    return out


def solution(mesh):
    in_specs = (P("row", "col"), P("row", "col"), P())
    out_specs = P("row", "col", None)
    body = functools.partial(local, mesh.shape["row"], mesh.shape["col"])
    return jax.shard_map(body, mesh=mesh, in_specs=in_specs, out_specs=out_specs, check_vma=False)
```

```python
import functools

import jax
import jax.numpy as jnp
from jax import lax
from jax.experimental import pallas as pl
from jax.experimental.pallas import tpu as pltpu
from jax.sharding import PartitionSpec as P

V = 512
GROUP = 16
STEP_A = 4
PAD = 8
WIDE = 1024
TALL = 512
ANY = pl.BlockSpec(memory_space=pl.ANY)


def cut_kernel(own, t_ref, w_ref, t_out, *refs, j_local, b_local):
    w_outs, t_sem, w_sem = refs[:-2], refs[-2], refs[-1]
    cols = len(w_outs)
    for s in range(cols):
        to = lax.rem(own[0] + s, cols)
        for j in range(j_local):
            start = pl.multiple_of((j * cols + to) * b_local, b_local)
            pltpu.make_async_copy(
                w_ref.at[:, pl.ds(start, b_local)], w_outs[s].at[:, j * b_local:(j + 1) * b_local], w_sem.at[s]
            ).start()
    for i in range(t_ref.shape[0]):
        for r in range(t_ref.shape[1]):
            pltpu.make_async_copy(t_ref.at[i, r], t_out.at[r, :, i], t_sem).start()
    for s in range(cols):
        pltpu.make_async_copy(w_outs[s], w_outs[s], w_sem.at[s]).wait()
    pltpu.make_async_copy(t_out, t_out, t_sem).wait()


def cut(own, blocks, couplings, cols, j_local, b_local):
    i_local, rows, chunks, group, t_depth = blocks.shape
    depth = couplings.shape[0]
    if b_local % 128 or t_depth % 128:
        split = couplings.reshape(depth, j_local, cols, b_local)
        parts = [
            lax.dynamic_index_in_dim(split, lax.rem(own + s, cols), 2, keepdims=False).reshape(depth, -1)
            for s in range(cols)
        ]
        return [blocks.transpose(1, 2, 0, 3, 4), *parts]
    return pl.pallas_call(
        functools.partial(cut_kernel, j_local=j_local, b_local=b_local),
        out_shape=[jax.ShapeDtypeStruct((rows, chunks, i_local, group, t_depth), blocks.dtype)]
        + [jax.ShapeDtypeStruct((depth, j_local * b_local), couplings.dtype)] * cols,
        in_specs=[pl.BlockSpec(memory_space=pltpu.SMEM), ANY, ANY],
        out_specs=[pl.BlockSpec(memory_space=pltpu.VMEM)] * (1 + cols),
        scratch_shapes=[pltpu.SemaphoreType.DMA, pltpu.SemaphoreType.DMA((cols,))],
        compiler_params=pltpu.CompilerParams(vmem_limit_bytes=60 * 1024 * 1024),
        cost_estimate=pl.CostEstimate(flops=0, bytes_accessed=4 * (blocks.size + couplings.size), transcendentals=0),
    )(own.reshape(1), blocks, couplings)


def chunk_kernel(own, *refs, starts, parts, occupied, b_local, q):
    t_refs = [ref.at[pl.ds(start, GROUP * occupied)] for ref, start in zip(refs, starts)]
    t_own, t_right, t_left = t_refs[0], t_refs[1:parts], t_refs[parts:]
    w_own, w_rest, ladder_hbm = refs[2 * parts - 1:2 * parts + 2]
    out_ref, t_all, w_buf, ladder, pairs, out_buf, t_sem, w_sem, l_sem, out_sem = refs[-10:]
    depth = t_own.shape[1]
    width = w_own.shape[1]
    count = occupied * occupied
    pitch = count + PAD
    per_part = occupied // parts
    wide = WIDE // b_local

    def t_copy(src, block, s):
        cols = pl.ds(pl.multiple_of(block * depth, depth), depth)
        return pltpu.make_async_copy(src, t_all.at[:, cols], t_sem.at[s])

    def w_copy(s, slot):
        src = w_rest.at[s - 1] if s else w_own
        return pltpu.make_async_copy(src, w_buf.at[slot], w_sem.at[slot])

    blocks = [lax.rem(own[0] - s + parts, parts) for s in range(parts)]
    t_copy(t_own, blocks[0], 0).start()
    for s in range(1, parts):
        @pl.when(own[0] >= s)
        def _():
            t_copy(t_right[s - 1], blocks[s], s).start()

        @pl.when(own[0] < s)
        def _():
            t_copy(t_left[parts - s - 1], blocks[s], s).start()
    w_copy(0, 0).start()
    ladder_copy = pltpu.make_async_copy(ladder_hbm, ladder, l_sem)
    for s in range(parts):
        t_copy(t_own, blocks[s], s).wait()

    @pl.loop(0, parts)
    def _(step):
        slot = lax.rem(step, 2)
        w_copy(0, slot).wait()
        for s in range(1, parts):
            @pl.when(step + 1 == s)
            def _():
                w_copy(s, s % 2).start()

        @pl.when(step == parts - 1)
        def _():
            ladder_copy.start()

        j0 = lax.rem(own[0] - step + parts, parts) * per_part
        for tile in range(per_part // wide):
            acc = jnp.dot(
                t_all[...], w_buf[slot, :, tile * WIDE:(tile + 1) * WIDE], preferred_element_type=jnp.float32)
            for i in range(occupied):
                for k in range(wide):
                    n = j0 + (i * occupied + tile * wide + k)
                    for h in range(GROUP // 8):
                        row = i * GROUP + h * 8
                        pairs[pl.ds(h * 8 * pitch + n, 8, stride=pitch), :] = (
                            acc[row:row + 8, k * b_local:(k + 1) * b_local])

    ladder_copy.wait()
    steps = GROUP // STEP_A

    def out_copy(step, slot):
        rows = pl.ds(q * GROUP + step * STEP_A, STEP_A)
        return pltpu.make_async_copy(out_buf.at[slot], out_ref.at[rows], out_sem.at[slot])

    @pl.loop(0, steps)
    def _(step):
        slot = lax.rem(step, 2)

        @pl.when(step >= 2)
        def _():
            out_copy(step - 2, slot).wait()

        blocks = []
        for k in range(STEP_A):
            row = pl.multiple_of((step * STEP_A + k) * pitch, 8)
            blocks.append(pairs[pl.ds(row, count), :].astype(jnp.bfloat16))
        both = jnp.concatenate(blocks, axis=1)
        for m in range(count // TALL):
            rows = slice(m * TALL, (m + 1) * TALL)
            mixed = jnp.dot(ladder[rows, :], both, preferred_element_type=jnp.float32)
            total = (mixed + both[rows, :].astype(jnp.float32)).astype(jnp.bfloat16)
            out_buf[slot, :, :, rows] = total.T.reshape(STEP_A, b_local, TALL)
        out_copy(step, slot).start()

    for step in range(max(steps - 2, 0), steps):
        out_copy(step, step % 2).wait()


def chunk_update(own, pieces, panel_w, ladder, out, after, q, a_local, b_local, occupied):
    arrays, starts = zip(*pieces)
    rows = GROUP * occupied
    count = occupied * occupied
    k_all, width = panel_w[0].shape
    parts = 1 + panel_w[1].shape[0]
    args = [*arrays, *panel_w, ladder, *after]
    aliases = {}
    if out is not None:
        aliases = {len(args) + 1: 0}
        args.append(out)
    flops = 2 * rows * k_all * occupied * b_local + 2 * GROUP * b_local * count * count
    size = parts * k_all * width + count * count + rows * k_all + GROUP * b_local * count
    return pl.pallas_call(
        functools.partial(chunk_kernel, starts=starts, parts=parts, occupied=occupied, b_local=b_local, q=q),
        out_shape=jax.ShapeDtypeStruct((a_local, b_local, count), jnp.bfloat16),
        in_specs=[pl.BlockSpec(memory_space=pltpu.SMEM)] + [ANY] * len(args),
        out_specs=ANY,
        scratch_shapes=[
            pltpu.VMEM((rows, k_all), jnp.bfloat16),
            pltpu.VMEM((2, k_all, width), jnp.bfloat16),
            pltpu.VMEM((count, count), jnp.bfloat16),
            pltpu.VMEM((GROUP * (count + PAD), b_local), jnp.float32),
            pltpu.VMEM((2, STEP_A, b_local, count), jnp.bfloat16),
            pltpu.SemaphoreType.DMA((parts,)),
            pltpu.SemaphoreType.DMA((2,)),
            pltpu.SemaphoreType.DMA,
            pltpu.SemaphoreType.DMA((2,)),
        ],
        input_output_aliases=aliases,
        compiler_params=pltpu.CompilerParams(vmem_limit_bytes=60 * 1024 * 1024),
        cost_estimate=pl.CostEstimate(flops=flops, bytes_accessed=2 * size, transcendentals=0),
    )(own.reshape(1), *args)


def plain_update(own, pieces, panel_w, ladder, b_local, occupied):
    parts = (len(pieces) + 1) // 2
    back = jnp.argsort(lax.rem(own - jnp.arange(parts) + parts, parts))
    rows, depth = pieces[0].shape
    right, left = pieces[1:parts], pieces[parts:]
    by_shift = [pieces[0]] + [jnp.where(own >= s, right[s - 1], left[parts - s - 1]) for s in range(1, parts)]
    panel_t = jnp.transpose(jnp.stack(by_shift, 0)[back], (1, 0, 2)).reshape(rows, -1)
    cycle = jnp.dot(panel_t, jnp.concatenate([panel_w[0], *panel_w[1]], axis=1), preferred_element_type=jnp.float32)
    cycle = cycle.astype(jnp.bfloat16).reshape(occupied, -1, parts, occupied // parts, b_local)[:, :, back]
    cycle = cycle.reshape(occupied, -1, occupied, b_local)
    a_count = cycle.shape[1]
    pairs = jnp.transpose(cycle, (1, 3, 0, 2)).reshape(a_count * b_local, occupied * occupied)
    mixed = lax.dot_general(pairs, ladder, (((1,), (1,)), ((), ())), preferred_element_type=jnp.float32)
    total = (mixed + pairs.astype(jnp.float32)).astype(jnp.bfloat16)
    return total.reshape(a_count, b_local, occupied * occupied)


def local(rows, cols, amplitudes, couplings, ladder):
    depth = amplitudes.shape[1]
    i_local = amplitudes.shape[0] // V
    j_local = couplings.shape[1] // V
    occupied = i_local * rows
    a_local, b_local = V // rows, V // cols
    own = lax.axis_index("col")

    chunks = a_local // GROUP
    blocks = amplitudes.reshape(i_local, rows, chunks, GROUP, depth)
    blocks, *arrived = cut(own, blocks, couplings, cols, j_local, b_local)
    for s in range(1, cols):
        arrived[s] = lax.ppermute(arrived[s], "col", [(c, (c + s) % cols) for c in range(cols)])
    blocks = lax.all_to_all(blocks, "row", split_axis=0, concat_axis=0, tiled=True)

    rest, _ = lax.optimization_barrier((arrived[1:], blocks))
    panel_w = [
        lax.all_gather(arrived[0], "row", axis=0, tiled=True),
        lax.all_gather(jnp.stack(rest), "row", axis=1, tiled=True),
    ]

    per_part = occupied // cols
    plain = (b_local % 128 or WIDE % b_local or depth % 128 or cols < 4
             or per_part * b_local % WIDE or occupied * occupied % TALL or chunks < 4 or chunks % 2)

    def flat(sides):
        right, left = sides
        return [right[0], *right[1:], *left[1:]]

    def update(q, out, after):
        blocks = [(piece, 0) for piece in flat(pieces[q])]
        return chunk_update(own, blocks, panel_w, ladder, out, after, q, a_local, b_local, occupied)

    def hop(sides, s, direct=False):
        right, left = sides
        first = 0 if direct else s - 1
        step = s if direct else 1
        source = 0 if direct else -1
        right.append(lax.ppermute(right[source], "col", [(c, c + step) for c in range(first, cols - step)]))
        left.append(lax.ppermute(left[source], "col", [(c + step, c) for c in range(cols - step - first)]))

    pieces = []
    for q in range(chunks):
        held = blocks[:, q].reshape(occupied * GROUP, depth)
        pieces.append(([held], [held]))

    if plain:
        for sides in pieces:
            for s in range(1, cols):
                hop(sides, s)
        return jnp.concatenate(
            [plain_update(own, flat(sides), panel_w, ladder, b_local, occupied) for sides in pieces], axis=0)

    def after(done, sides):
        right, left = sides
        done, right[0], left[0] = lax.optimization_barrier((done, right[0], left[0]))
        return done

    *early, x, y = pieces
    for q in range(0, len(early), 2):
        if q:
            for before, sides in zip(early[q - 2:q], early[q:q + 2]):
                before[0][-2], before[1][-2] = after((before[0][-2], before[1][-2]), sides)
        for s in range(1, cols):
            for sides in early[q:q + 2]:
                hop(sides, s)
    before = early[-2]
    before[0][-2], before[1][-2] = after((before[0][-2], before[1][-2]), x)
    for s in range(1, cols - 1):
        hop(x, s)
    out = update(0, None, (x[0][1], x[1][1]))
    moving = (early[-1][0], early[-1][1], x[0], x[1])
    out, *ends = after((out, *[side[-1] for side in moving]), x)
    for side, end in zip(moving, ends):
        side[-1] = end
    hop(x, cols - 1)
    out = after(out, y)
    hop(y, 1)
    out = update(1, out, ())
    out, y[0][-1], y[1][-1], y[0][0], y[1][0] = lax.optimization_barrier(
        (out, y[0][-1], y[1][-1], y[0][0], y[1][0]))
    for s in range(2, cols - 1):
        hop(y, s)
    hop(y, cols - 1, direct=True)
    for q in range(2, chunks):
        out = update(q, out, ())
    return out


def solution(mesh):
    in_specs = (P("row", "col"), P("row", "col"), P())
    out_specs = P("row", "col", None)
    body = functools.partial(local, mesh.shape["row"], mesh.shape["col"])
    return jax.shard_map(body, mesh=mesh, in_specs=in_specs, out_specs=out_specs, check_vma=False)
```
